128 devices in a mesh: fsdp: 32 (over x, z, core), tensor: 4 (over y).
Axes of the slice: x: 4, y: 4, z: 4, core: 2. Of those that a mesh axis runs over, the one named last changes fastest.
Arguments:
- tokens: bfloat16 [2, 2048, 2048], P(None, 'fsdp'), may hold values from -6 to 6
- segment: int32 [2, 2048], replicated, may hold values from 0 to 2, as said below
- routes: int32 [2, 2048, 6], P(None, 'fsdp'), may hold values from 0 to 7, all different within a row
- cotangent: bfloat16 [2, 2048, 2048], P(None, 'fsdp'), may hold values from -6 to 6
- gain_attn: bfloat16 [2048], P('fsdp'), may hold values from 0.5 to 1.5
- w_query: bfloat16 [2048, 3072], P('fsdp', 'tensor'), may hold values from -0.125 to 0.125
- w_compress: bfloat16 [2048, 576], P('fsdp'), may hold values from -0.125 to 0.125
- gain_latent: bfloat16 [512], P('fsdp'), may hold values from 0.5 to 1.5
- w_expand: bfloat16 [512, 4096], P('fsdp', 'tensor'), may hold values from -0.25 to 0.25
- w_output: bfloat16 [2048, 2048], P('fsdp', 'tensor'), may hold values from -2 to 2
- gain_ffn: bfloat16 [2048], P('fsdp'), may hold values from 0.5 to 1.5
- w_router: bfloat16 [2048, 8], P('fsdp'), may hold values from -0.0625 to 0.0625
- w_expert_in: bfloat16 [2048, 8, 2, 1408], P('fsdp', None, None, 'tensor'), may hold values from -0.125 to 0.125
- w_expert_out: bfloat16 [2048, 8, 1408], P('fsdp', None, 'tensor'), may hold values from -0.625 to 0.625
- w_shared_in: bfloat16 [2048, 2, 2816], P('fsdp', None, 'tensor'), may hold values from -0.125 to 0.125
- w_shared_out: bfloat16 [2048, 2816], P('fsdp', 'tensor'), may hold values from -0.15625 to 0.15625
Outputs:
- mixed: bfloat16 [2, 2048, 2048], P(None, 'fsdp')
- grad_tokens: bfloat16 [2, 2048, 2048], P(None, 'fsdp')
- grad_gain_attn: float32 [2048], P('fsdp')
- grad_w_query: float32 [2048, 3072], P('fsdp', 'tensor')
- grad_w_compress: float32 [2048, 576], P('fsdp')
- grad_gain_latent: float32 [512], P('fsdp')
- grad_w_expand: float32 [512, 4096], P('fsdp', 'tensor')
- grad_w_output: float32 [2048, 2048], P('fsdp', 'tensor')
- grad_gain_ffn: float32 [2048], P('fsdp')
- grad_w_router: float32 [2048, 8], P('fsdp')
- grad_w_expert_in: float32 [2048, 8, 2, 1408], P('fsdp', None, None, 'tensor')
- grad_w_expert_out: float32 [2048, 8, 1408], P('fsdp', None, 'tensor')
- grad_w_shared_in: float32 [2048, 2, 2816], P('fsdp', None, 'tensor')
- grad_w_shared_out: float32 [2048, 2816], P('fsdp', 'tensor')
The draws below stay inside these ranges and needn't reach their ends.
Inputs may be any that keep to these rules, and one draw needn't show every extreme that they name: `segment`: along each micro-batch the document numbers never fall; document 1 begins within the first 64 tokens and ends within the last 64. `routes`: each token names 6 different experts.
All inputs are finite; a program needn't handle non-finite values.
Results may differ from the reference program's by a relative error of at most 0.03.
Values may be sent and summed in bfloat16 or wider, within the bound.
No kernel may reach another device: no remote copies, remote signals or barrier semaphores. Data moves between devices by JAX's collectives and lax.ppermute only.
A program may use at most 256 MiB of HBM per device.

```python
import jax
import jax.numpy as jnp
from jax import lax

D = 2048
HEADS = 16
NOPE = 128
ROPE = 64
VHEAD = 128
RANK = 512
FFE = 1408
FFS = 2816
EXPERTS = 8
TOPK = 6
MICRO = 2
TOK_DEV = 64
TOKENS = 2048


def draw_segment(key, part):
    key = jax.random.fold_in(key, 11)
    first_key, last_key = jax.random.split(key)
    head = jax.random.randint(first_key, (MICRO, 1), 1, TOK_DEV)
    tail = jax.random.randint(last_key, (MICRO, 1), TOKENS - TOK_DEV + 1, TOKENS)
    position = jnp.arange(TOKENS, dtype=jnp.int32)[None, :]
    return (position >= head).astype(jnp.int32) + (position >= tail).astype(jnp.int32)


def level_of(key, extent, cuts, low, largest):
    factor_of, own = 1.0, jax.random.fold_in(key, 6)
    for axis_at, shards_of in cuts:
        draws = jnp.exp(jax.random.uniform(jax.random.fold_in(own, axis_at), (shards_of,), jnp.float32, low / len(cuts), largest / len(cuts)))
        factor_of = factor_of * jnp.repeat(draws, extent[axis_at] // shards_of).reshape([-1 if axis == axis_at else 1 for axis in range(len(extent))])
    return factor_of


def distinct(rng, rows, count, top, lift):
    ranking = jax.random.permutation(jax.random.fold_in(rng, 1), count)
    boost = ranking
    for power in range(3):
        boost = boost * boost // count
    boost = boost * lift // count
    lots = jax.random.randint(jax.random.fold_in(rng, 2), (rows, count), 0, 4096) + boost
    holders = jax.random.permutation(jax.random.fold_in(rng, 3), rows)[jnp.arange(count) % rows]
    lots = jnp.where(jnp.arange(rows)[:, None] == holders[None, :], 1 << 14, lots)
    score = lots * count + jnp.arange(count)
    return lax.top_k(score.astype(jnp.int32), top)[1].astype(jnp.int32)


def normal_values(stream_key, dims, spread, most, cuts=(), held_as=jnp.bfloat16):
    entries = jax.random.normal(stream_key, dims, jnp.float32) * spread
    if len(cuts) > 0:
        entries = level_of(stream_key, dims, cuts, -0.22, 0.18) * entries
    return jnp.clip(entries, min=-most, max=most).astype(held_as)


def setup_inputs(seed: int = 0) -> dict:
    arg_keys = jax.random.split(jax.random.key(seed), 17)
    return {
        "tokens": normal_values(arg_keys[0], (MICRO, TOKENS, D), 1.0, 6.0, ((1, 32),)),
        "segment": draw_segment(jax.random.fold_in(arg_keys[16], 71), 0),
        "routes": distinct(arg_keys[2], MICRO * TOKENS, EXPERTS, TOPK, 6144).reshape((MICRO, TOKENS, TOPK)),
        "cotangent": normal_values(arg_keys[3], (MICRO, TOKENS, D), 1.0, 6.0, ((1, 32),)),
        "gain_attn": jnp.clip(1.0 + 0.1 * jax.random.normal(arg_keys[4], (D,), jnp.float32), 0.5, 1.5).astype(jnp.bfloat16),
        "w_query": normal_values(arg_keys[5], (D, HEADS * (NOPE + ROPE)), D ** -0.5, 0.125, ((0, 32), (1, 4))),
        "w_compress": normal_values(arg_keys[6], (D, RANK + ROPE), D ** -0.5, 0.125, ((0, 32),)),
        "gain_latent": jnp.clip(1.0 + 0.1 * jax.random.normal(arg_keys[7], (RANK,), jnp.float32), 0.5, 1.5).astype(jnp.bfloat16),
        "w_expand": normal_values(arg_keys[8], (RANK, HEADS * (NOPE + VHEAD)), RANK ** -0.5, 0.25, ((0, 32), (1, 4))),
        "w_output": normal_values(arg_keys[9], (D, HEADS * VHEAD), (max(HEADS * VHEAD // 256, 1)) ** -0.5, 2.0, ((0, 32), (1, 4))),
        "gain_ffn": jnp.clip(1.0 + 0.1 * jax.random.normal(arg_keys[10], (D,), jnp.float32), 0.5, 1.5).astype(jnp.bfloat16),
        "w_router": normal_values(arg_keys[11], (D, EXPERTS), (4 * D) ** -0.5, 0.0625, ((0, 32),)),
        "w_expert_in": normal_values(arg_keys[12], (D, EXPERTS, 2, FFE), D ** -0.5, 0.125, ((0, 32), (3, 4))),
        "w_expert_out": normal_values(arg_keys[13], (D, EXPERTS, FFE), (FFE // 16) ** -0.5, 0.625, ((0, 32), (2, 4))),
        "w_shared_in": normal_values(arg_keys[14], (D, 2, FFS), D ** -0.5, 0.125, ((0, 32), (2, 4))),
        "w_shared_out": normal_values(arg_keys[15], (D, FFS), (FFS // 2) ** -0.5, 0.15625, ((0, 32), (1, 4))),
    }


epsilon = 1e-06
highest = lax.Precision.HIGHEST

@jax.custom_vjp
def low(v):
    return lax.optimization_barrier(v.astype(jnp.bfloat16)).astype(jnp.float32)

@jax.custom_vjp
def low_back(v):
    return v

def low_keep(v):
    return (low(v), None)

def low_pass(kept, grad):
    return (grad,)

def back_keep(v):
    return (v, None)

def back_low(kept, grad):
    return (low(grad),)
low.defvjp(low_keep, low_pass)
low_back.defvjp(back_keep, back_low)

def rms_scale(values, gain):
    return values * lax.rsqrt(lax.optimization_barrier(jnp.mean(values * values, axis=-1, keepdims=True)) + epsilon) * gain

def rotate(values, position):
    half = values.shape[-1] // 2
    freq = jnp.exp(jnp.arange(half, dtype=jnp.float32) * (-jnp.log(10000.0) / half))
    angle = position.astype(jnp.float32)[:, None] * freq[None, :]
    cosine = jnp.cos(angle)
    sine = jnp.sin(angle)
    if values.ndim == 3:
        cosine = cosine[:, None, :]
        sine = sine[:, None, :]
    first = values[..., :half]
    second = values[..., half:]
    return jnp.concatenate([first * cosine - second * sine, second * cosine + first * sine], axis=-1)

def layer(inputs, gain_attn, w_query, w_compress, gain_latent, w_expand, w_output, gain_ffn, w_router, w_expert_in, w_expert_out, w_shared_in, w_shared_out, segment_row, route_row):
    count = inputs.shape[0]
    position = jnp.arange(count, dtype=jnp.int32)
    scale = (NOPE + ROPE) ** (-0.5)
    normed = low(rms_scale(inputs, gain_attn))
    q_raw = low_back(jnp.dot(normed, w_query, precision=highest)).reshape(count, HEADS, NOPE + ROPE)
    query = low(jnp.concatenate([q_raw[..., :NOPE], rotate(q_raw[..., NOPE:], position)], axis=-1))
    compressed = low_back(jnp.dot(normed, w_compress, precision=highest))
    latent = low(rms_scale(compressed[:, :RANK], gain_latent))
    key_rot = low(rotate(compressed[:, RANK:], position))
    expanded = low(low_back(jnp.dot(latent, w_expand, precision=highest))).reshape(count, HEADS, NOPE + VHEAD)
    allowed = (position[:, None] >= position[None, :]) & (segment_row[:, None] == segment_row[None, :])

    def one_head(operands):
        q_head, kv_head = operands
        score = jnp.dot(q_head[:, :NOPE], kv_head[:, :NOPE].T, precision=highest) + jnp.dot(q_head[:, NOPE:], key_rot.T, precision=highest)
        score = low_back(score * scale)
        score = jnp.where(allowed, score, -1e+30)
        probs = low(jax.nn.softmax(score, axis=-1))
        return jnp.dot(probs, kv_head[:, NOPE:], precision=highest)
    heads_out = lax.map(jax.checkpoint(one_head), (jnp.transpose(query, (1, 0, 2)), jnp.transpose(expanded, (1, 0, 2))))
    attended = low(low_back(jnp.transpose(heads_out, (1, 0, 2)).reshape(count, HEADS * VHEAD)))
    branch = low_back(jnp.dot(attended, w_output.T, precision=highest))
    middle = inputs + branch
    normed_ffn = low(rms_scale(middle, gain_ffn))
    logits = low_back(jnp.dot(normed_ffn, w_router, precision=highest))
    router = jax.nn.softmax(logits, axis=-1)
    chosen = lax.optimization_barrier(jnp.sum((route_row[:, :, None] == jnp.arange(EXPERTS, dtype=jnp.int32)[None, None, :]).astype(jnp.float32), axis=1))
    gate = router * chosen
    gate_up = low_back(jnp.einsum('td,degf->tegf', normed_ffn, w_expert_in, precision=highest))
    weighted = low(gate[:, :, None] * jax.nn.silu(gate_up[:, :, 0]) * gate_up[:, :, 1])
    routed = jnp.einsum('tef,def->td', weighted, w_expert_out, precision=highest)
    shared_in = low_back(jnp.einsum('td,dgf->tgf', normed_ffn, w_shared_in, precision=highest))
    shared_act = low(jax.nn.silu(shared_in[:, 0]) * shared_in[:, 1])
    shared = jnp.dot(shared_act, w_shared_out.T, precision=highest)
    return middle + routed + shared

def reference(tokens, segment, routes, cotangent, gain_attn, w_query, w_compress, gain_latent, w_expand, w_output, gain_ffn, w_router, w_expert_in, w_expert_out, w_shared_in, w_shared_out):
    weights = tuple((item.astype(jnp.float32) for item in (gain_attn, w_query, w_compress, gain_latent, w_expand, w_output, gain_ffn, w_router, w_expert_in, w_expert_out, w_shared_in, w_shared_out)))

    def step(totals, batch):
        inputs, segment_row, route_row, grad_out = batch

        def forward(values, *params):
            return layer(values, *params, segment_row, route_row)
        result, pullback = jax.vjp(forward, inputs.astype(jnp.float32), *weights)
        grads = pullback(grad_out.astype(jnp.float32))
        new_totals = tuple((total + term for total, term in zip(totals, grads[1:])))
        return (new_totals, (result.astype(jnp.bfloat16), grads[0].astype(jnp.bfloat16)))
    zeros = tuple((jnp.zeros(item.shape, jnp.float32) for item in weights))
    totals, outputs = lax.scan(step, zeros, (tokens, segment, routes, cotangent))
    return (outputs[0], outputs[1], totals[0], totals[1], totals[2], totals[3], totals[4], totals[5], totals[6], totals[7], totals[8], totals[9], totals[10], totals[11])
```

```python
import jax
import jax.numpy as jnp
from jax import lax
from jax.experimental import pallas as pl
from jax.experimental.pallas import tpu as pltpu
from jax.sharding import Mesh
from jax.sharding import PartitionSpec as P

NOPE = 128
ROPE = 64
VHEAD = 128
RANK = 512
EXPERTS = 8

epsilon = 1e-06
bf16 = jnp.bfloat16
f32 = jnp.float32


def rotate_parts(values, position, inverse):
    half = values.shape[-1] // 2
    freq = jnp.exp(jnp.arange(half, dtype=f32) * (-jnp.log(10000.0) / half))
    angle = position.astype(f32)[:, None] * freq[None, :]
    cosine = jnp.cos(angle)
    sine = jnp.sin(angle)
    if inverse:
        sine = -sine
    if values.ndim == 3:
        cosine = cosine[:, None, :]
        sine = sine[:, None, :]
    first = values[..., :half]
    second = values[..., half:]
    return jnp.concatenate(
        [first * cosine - second * sine, second * cosine + first * sine], axis=-1
    )


def norm_forward(values, gain):
    factor = lax.rsqrt(jnp.mean(values * values, axis=-1, keepdims=True) + epsilon)
    return (values * factor * gain, factor)


def norm_backward(values, factor, gain, grad):
    scaled = grad * gain
    d_values = factor * scaled - values * (factor * factor * factor) * jnp.mean(
        values * scaled, axis=-1, keepdims=True
    )
    d_gain = jnp.sum(grad * values * factor, axis=0)
    return (d_values, d_gain)


def shift(value, axis, step):
    count = lax.axis_size(axis)
    return lax.ppermute(value, axis, [(i, (i + step) % count) for i in range(count)])


def pick(value, place, at):
    return lax.dynamic_index_in_dim(value, place, at, keepdims=False)


def gather_near(value, axis):
    return [value] + [shift(value, axis, s) for s in range(1, lax.axis_size(axis))]


def gather_at(value, axis):
    count = lax.axis_size(axis)
    me = lax.axis_index(axis)
    whole = jnp.zeros((count,) + value.shape, value.dtype)
    for s in range(count):
        part = value if s == 0 else shift(value, axis, s)
        whole = lax.dynamic_update_index_in_dim(whole, part, lax.rem(me - s + count, count), 0)
    return whole


def sum_near(parts, axis):
    total = parts[0].astype(f32)
    for s in range(1, len(parts)):
        total = total + shift(parts[s], axis, -s).astype(f32)
    return total


def sum_ahead(parts, axis):
    total = parts[0].astype(f32)
    for s in range(1, len(parts)):
        total = total + shift(parts[s], axis, s).astype(f32)
    return total


def sum_at(value, axis, at):
    count = lax.axis_size(axis)
    me = lax.axis_index(axis)
    return sum_ahead([pick(value, lax.rem(me + s, count), at) for s in range(count)], axis)


def exchange_at(value, axis):
    count = lax.axis_size(axis)
    me = lax.axis_index(axis)
    whole = jnp.zeros_like(value)
    for s in range(count):
        part = pick(value, lax.rem(me + s, count), 0)
        part = part if s == 0 else shift(part, axis, s)
        whole = lax.dynamic_update_index_in_dim(whole, part, lax.rem(me - s + count, count), 0)
    return whole


def to_far(value):
    rows = value.shape[0]
    return value.reshape(rows, 4, 4, 128).transpose(0, 2, 1, 3).reshape(rows, 2048)


def dot_nn(a, b):
    return jnp.dot(a, b, preferred_element_type=f32)


def dot_nt(a, b):
    return lax.dot_general(a, b, (((1,), (1,)), ((), ())), preferred_element_type=f32)


def dot_tn(a, b):
    return lax.dot_general(a, b, (((0,), (0,)), ((), ())), preferred_element_type=f32)


def whole(*shape):
    return pl.BlockSpec(shape, lambda h: (0,) * len(shape))


SCALARS = pl.BlockSpec(memory_space=pltpu.SMEM)
SCALE = (NOPE + ROPE) ** (-0.5)
MIB = 1024 * 1024


def attend_kernel(
    place, q, a0, a1, a2, a3, b0, b1, b2, b3, expand, out_w, where_q, where_k,
    prob, kv, attended, lat, r0, r1, r2, r3, key_rot, total,
):
    head = pl.program_id(0)

    @pl.when(head == 0)
    def _():
        for sx in range(4):
            lat[sx * 512 : sx * 512 + 512, 256:576] = (b0, b1, b2, b3)[sx][...]
            for sz in range(4):
                row = (sx * 4 + sz) * 128
                lat[row : row + 128, 0:256] = (a0, a1, a2, a3)[sz][sx * 128 : sx * 128 + 128, :]
        key_rot[...] = jnp.concatenate(
            [lat[:, RANK:576], jnp.zeros((2048, 64), bf16)], axis=1
        )
        total[...] = jnp.zeros_like(total)

    expand_h = expand[...].reshape(RANK, 256)
    kv_h = dot_nn(lat[:, :RANK], expand_h).astype(bf16)
    kv[...] = kv_h
    score = (dot_nt(q[:, :128], kv_h[:, :128]) + dot_nt(q[:, 128:], key_rot[...])) * SCALE
    allowed = (where_q[:, 0:1] >= where_k[0:1, :]) & (where_q[:, 1:2] == where_k[1:2, :])
    score = jnp.where(allowed, score, -1e30)
    power = jnp.exp(score - jnp.max(score, axis=1, keepdims=True))
    prob_h = power / jnp.sum(power, axis=1, keepdims=True)
    prob[0] = prob_h
    attended_h = dot_nn(prob_h.astype(bf16), kv_h[:, 128:]).astype(bf16)
    attended[...] = attended_h
    total[...] += dot_nt(attended_h, out_w[...])

    @pl.when(head == 3)
    def _():
        for s, out in enumerate((r0, r1, r2, r3)):
            row = pl.multiple_of(lax.rem(place[3] + s, 4) * 32, 32)
            out[...] = total[pl.ds(row, 32), :].astype(bf16)


def attend(place, q, parts_a, parts_b, attn_all, where_q, where_k):
    by_head = attn_all.reshape(32, 4, 16, 1536)
    return pl.pallas_call(
        attend_kernel,
        grid=(4,),
        in_specs=[SCALARS, pl.BlockSpec((128, 256), lambda h: (0, h))]
        + [whole(512, 256)] * 4
        + [whole(512, 320)] * 4
        + [
            pl.BlockSpec((32, 1, 16, 256), lambda h: (0, h, 0, 5)),
            pl.BlockSpec((2048, 128), lambda h: (0, 6 + h)),
            whole(128, 2),
            whole(2, 2048),
        ],
        out_specs=[
            pl.BlockSpec((1, 128, 2048), lambda h: (h, 0, 0)),
            pl.BlockSpec((2048, 256), lambda h: (0, h)),
            pl.BlockSpec((128, 128), lambda h: (0, h)),
            whole(2048, 576),
        ]
        + [whole(32, 2048)] * 4,
        out_shape=[
            jax.ShapeDtypeStruct((4, 128, 2048), f32),
            jax.ShapeDtypeStruct((2048, 1024), bf16),
            jax.ShapeDtypeStruct((128, 512), bf16),
            jax.ShapeDtypeStruct((2048, 576), bf16),
        ]
        + [jax.ShapeDtypeStruct((32, 2048), bf16)] * 4,
        scratch_shapes=[pltpu.VMEM((2048, 128), bf16), pltpu.VMEM((128, 2048), f32)],
        compiler_params=pltpu.CompilerParams(vmem_limit_bytes=48 * MIB),
        cost_estimate=pl.CostEstimate(
            flops=5 * 10**9, bytes_accessed=22 * 10**6, transcendentals=2**20
        ),
        name="attend",
    )(place, q, *parts_a, *parts_b, by_head, attn_all, where_q, where_k)


def attend_back_kernel(
    place, d0, d1, d2, d3, out_w, q, kv, prob, lat, expand, nope_w, rot_w, cosine, sine,
    d_q, d_rot, d_exp, d_branch, a0, a1, a2, a3, b0, b1, b2, b3, r0, r1, r2, r3,
    key_rot, lat_sum, rot_sum, rot_q, total,
):
    head = pl.program_id(0)

    @pl.when(head == 0)
    def _():
        for s, part in enumerate((d0, d1, d2, d3)):
            row = pl.multiple_of(lax.rem(place[3] - s + 4, 4) * 32, 32)
            d_branch[pl.ds(row, 32), :] = part[...]
        key_rot[...] = jnp.concatenate(
            [lat[:, RANK:576], jnp.zeros((2048, 64), bf16)], axis=1
        )
        lat_sum[...] = jnp.zeros_like(lat_sum)
        rot_sum[...] = jnp.zeros_like(rot_sum)
        total[...] = jnp.zeros_like(total)

    d_att = dot_nn(d_branch[...], out_w[...]).astype(bf16)
    prob_h = prob[0]
    d_prob = dot_nt(d_att, kv[:, 128:])
    row_sum = jnp.sum(prob_h * d_prob, axis=1, keepdims=True)
    d_score = (prob_h * (d_prob - row_sum)).astype(bf16)
    d_nope = (dot_nn(d_score, kv[:, :128]) * SCALE).astype(bf16)
    d_q[...] = d_nope
    rot_q[head] = dot_nn(d_score, key_rot[...]) * SCALE
    d_key = dot_tn(d_score, q[...]) * SCALE
    d_val = dot_tn(prob_h.astype(bf16), d_att)
    d_exp_h = jnp.concatenate([d_key[:, :128], d_val], axis=1).astype(bf16)
    d_exp[...] = d_exp_h
    rot_sum[...] += d_key[:, 128:]
    lat_sum[...] += dot_nt(d_exp_h, expand[...].reshape(RANK, 256))
    total[...] += dot_nt(d_nope, nope_w[...])

    @pl.when(head == 3)
    def _():
        rot = jnp.concatenate([rot_q[h][:, :64] for h in range(4)], axis=1)
        lane = lax.broadcasted_iota(jnp.int32, rot.shape, 1)
        partner = jnp.where(
            lane % 64 < 32, pltpu.roll(rot, 224, 1), pltpu.roll(rot, 32, 1)
        )
        rot = (rot * cosine[...] + partner * sine[...]).astype(bf16)
        d_rot[...] = rot
        summed = total[...] + dot_nt(rot, rot_w[...])
        total[...] = summed
        for s, out in enumerate((r0, r1, r2, r3)):
            row = pl.multiple_of(lax.rem(place[3] + s, 4) * 32, 32)
            out[...] = total[pl.ds(row, 32), :].astype(bf16)
        for sx in range(4):
            (a0, a1, a2, a3)[sx][...] = lat_sum[sx * 512 : sx * 512 + 512, :256].astype(bf16)
            for sz in range(4):
                row = (sx * 4 + sz) * 128
                out = (b0, b1, b2, b3)[sz]
                out[sx, :, :256] = lat_sum[row : row + 128, 256:].astype(bf16)
                out[sx, :, 256:] = rot_sum[row : row + 128, :64].astype(bf16)


def attend_back(place, parts, q, kv, prob, lat, attn_all, cosine, sine):
    by_head = attn_all.reshape(32, 4, 16, 1536)
    return pl.pallas_call(
        attend_back_kernel,
        grid=(4,),
        in_specs=[SCALARS]
        + [whole(32, 2048)] * 4
        + [
            pl.BlockSpec((2048, 128), lambda h: (0, 6 + h)),
            pl.BlockSpec((128, 256), lambda h: (0, h)),
            pl.BlockSpec((2048, 256), lambda h: (0, h)),
            pl.BlockSpec((1, 128, 2048), lambda h: (h, 0, 0)),
            whole(2048, 576),
            pl.BlockSpec((32, 1, 16, 256), lambda h: (0, h, 0, 5)),
            pl.BlockSpec((2048, 128), lambda h: (0, h)),
            pl.BlockSpec((2048, 256), lambda h: (0, 2)),
            whole(128, 256),
            whole(128, 256),
        ],
        out_specs=[
            pl.BlockSpec((128, 128), lambda h: (0, h)),
            whole(128, 256),
            pl.BlockSpec((2048, 256), lambda h: (0, h)),
            whole(128, 2048),
        ]
        + [whole(512, 256)] * 4
        + [whole(4, 128, 320)] * 4
        + [whole(32, 2048)] * 4,
        out_shape=[
            jax.ShapeDtypeStruct((128, 512), bf16),
            jax.ShapeDtypeStruct((128, 256), bf16),
            jax.ShapeDtypeStruct((2048, 1024), bf16),
            jax.ShapeDtypeStruct((128, 2048), bf16),
        ]
        + [jax.ShapeDtypeStruct((512, 256), bf16)] * 4
        + [jax.ShapeDtypeStruct((4, 128, 320), bf16)] * 4
        + [jax.ShapeDtypeStruct((32, 2048), bf16)] * 4,
        scratch_shapes=[
            pltpu.VMEM((2048, 128), bf16),
            pltpu.VMEM((2048, 512), f32),
            pltpu.VMEM((2048, 128), f32),
            pltpu.VMEM((4, 128, 128), f32),
            pltpu.VMEM((128, 2048), f32),
        ],
        compiler_params=pltpu.CompilerParams(vmem_limit_bytes=56 * MIB),
        cost_estimate=pl.CostEstimate(
            flops=8 * 10**9, bytes_accessed=30 * 10**6, transcendentals=0
        ),
        name="attend_back",
    )(place, *parts, attn_all, q, kv, prob, lat, by_head, attn_all, attn_all, cosine, sine)


def expert_kernel(
    place, far, spread, w0, w1, w2, w3, d_far, d_hidden, hidden, out, weight, sems
):
    @pl.when(pl.program_id(0) == 0)
    def _():
        copies = []
        for s, part in enumerate((w0, w1, w2, w3)):
            row = pl.multiple_of(lax.rem(place[1] - s + 4, 4) * 512, 512)
            copies.append(pltpu.make_async_copy(part, weight.at[pl.ds(row, 512)], sems.at[s]))
        for copy in copies:
            copy.start()
        for copy in copies:
            copy.wait()

    expert = 2 * place[0] + place[2]
    raw = dot_nn(far[...], weight[:, :896])
    d_weighted = dot_nn(spread[:, :2048], weight[:, 896:])
    rows = raw.shape[0]
    logits = raw[:, 880:888]
    power = jnp.exp(logits - jnp.max(logits, axis=1, keepdims=True))
    router = power / jnp.sum(power, axis=1, keepdims=True)
    is_mine = lax.broadcasted_iota(jnp.int32, (rows, 8), 1) == expert
    chosen = spread[:, 2048:2176][:, :8].astype(f32)
    gate = jnp.sum(jnp.where(is_mine, router * chosen, 0.0), axis=1, keepdims=True)
    routed = lax.broadcasted_iota(jnp.int32, (rows, 440), 1) < 352
    gate = jnp.where(routed, gate, 1.0)
    low, upper = raw[:, :440], raw[:, 440:880]
    sigma = 1.0 / (1.0 + jnp.exp(-low))
    silu = low * sigma
    slope = sigma + silu * (1.0 - sigma)
    act = silu * upper
    weighted = (gate * act).astype(bf16)
    d_gate = jnp.sum(jnp.where(routed, d_weighted * act, 0.0), axis=1, keepdims=True)
    d_act = d_weighted * gate
    d_up = jnp.concatenate(
        [d_act * upper * slope, d_act * silu, jnp.zeros((rows, 16), f32)], axis=1
    ).astype(bf16)
    d_hidden[...] = d_up
    hidden[...] = jnp.concatenate([weighted, jnp.zeros((rows, 72), bf16)], axis=1)
    d_far[:, :2048] = dot_nt(d_up, weight[:, :896]).astype(bf16)
    lane = lax.broadcasted_iota(jnp.int32, (rows, 128), 1)
    d_far[:, 2048:] = jnp.where(lane == expert, d_gate, 0.0).astype(bf16)
    out[...] = dot_nt(weighted, weight[:, 896:]).astype(bf16)


def run_expert(place, far, spread, pieces):
    rows = 256
    by_rows = lambda columns: pl.BlockSpec((rows, columns), lambda i: (i, 0))
    return pl.pallas_call(
        expert_kernel,
        grid=(512 // rows,),
        in_specs=[SCALARS, by_rows(2048), by_rows(2176)] + [pl.BlockSpec(memory_space=pl.ANY)] * 4,
        out_specs=[by_rows(2176), by_rows(896), by_rows(512), by_rows(2048)],
        out_shape=[
            jax.ShapeDtypeStruct((512, 2176), bf16),
            jax.ShapeDtypeStruct((512, 896), bf16),
            jax.ShapeDtypeStruct((512, 512), bf16),
            jax.ShapeDtypeStruct((512, 2048), bf16),
        ],
        scratch_shapes=[pltpu.VMEM((2048, 1336), bf16), pltpu.SemaphoreType.DMA((4,))],
        compiler_params=pltpu.CompilerParams(vmem_limit_bytes=48 * MIB),
        cost_estimate=pl.CostEstimate(
            flops=6 * 10**9, bytes_accessed=18 * 10**6, transcendentals=2**18
        ),
        name="expert",
    )(place, far, spread, *pieces)


def expert_grad_kernel(x0, x1, y0, y1, d0, d1, h0, h1, out):
    out[:, :896] = (dot_tn(x0[...], d0[...]) + dot_tn(x1[...], d1[...])).astype(bf16)
    down = dot_tn(y0[...], h0[...]) + dot_tn(y1[...], h1[...])
    out[:, 896:] = down[:, :440].astype(bf16)


def expert_grad(fars, spreads, d_hiddens, hiddens):
    block = 512
    columns = pl.BlockSpec((512, block), lambda i: (0, i))
    return pl.pallas_call(
        expert_grad_kernel,
        grid=(2048 // block,),
        in_specs=[columns] * 4 + [whole(512, 896)] * 2 + [whole(512, 512)] * 2,
        out_specs=pl.BlockSpec((block, 1336), lambda i: (i, 0)),
        out_shape=jax.ShapeDtypeStruct((2048, 1336), bf16),
        compiler_params=pltpu.CompilerParams(vmem_limit_bytes=48 * MIB),
        cost_estimate=pl.CostEstimate(
            flops=6 * 10**9, bytes_accessed=18 * 10**6, transcendentals=0
        ),
        name="expert_grad",
    )(*fars, *spreads, *d_hiddens, *hiddens)


def attn_grad_kernel(normed, d_q, d_rot, d_branch, attended, out):
    out[:, :512] = dot_tn(normed[...], d_q[...]).astype(bf16)
    out[:, 512:768] = dot_tn(normed[...], d_rot[...]).astype(bf16)
    out[:, 768:] = dot_tn(d_branch[...], attended[...]).astype(bf16)


def attn_grad(normed, d_q, d_rot, d_branch, attended):
    block = 512
    columns = pl.BlockSpec((128, block), lambda i: (0, i))
    return pl.pallas_call(
        attn_grad_kernel,
        grid=(2048 // block,),
        in_specs=[columns, whole(128, 512), whole(128, 256), columns, whole(128, 512)],
        out_specs=pl.BlockSpec((block, 1280), lambda i: (i, 0)),
        out_shape=jax.ShapeDtypeStruct((2048, 1280), bf16),
        compiler_params=pltpu.CompilerParams(vmem_limit_bytes=48 * MIB),
        cost_estimate=pl.CostEstimate(
            flops=7 * 10**8, bytes_accessed=7 * 10**6, transcendentals=0
        ),
        name="attn_grad",
    )(normed, d_q, d_rot, d_branch, attended)


def on_device(
    tokens,
    segment,
    routes,
    cotangent,
    gain_attn,
    w_query,
    w_compress,
    gain_latent,
    w_expand,
    w_output,
    gain_ffn,
    w_router,
    w_expert_in,
    w_expert_out,
    w_shared_in,
    w_shared_out,
):
    xi, zi, ci, yi = (lax.axis_index(a) for a in ("x", "z", "c", "y"))
    place = jnp.stack([xi, zi, ci, yi]).astype(jnp.int32)
    is_first = ci == 0
    heads = 4
    dim = 2048

    def enter(value):
        mine, other = pick(value, ci, 0), shift(pick(value, 1 - ci, 0), "c", 1)
        return jnp.concatenate(
            [jnp.where(is_first, mine, other), jnp.where(is_first, other, mine)], axis=0
        )

    def leave(value):
        halves = value.reshape((2, 64) + value.shape[1:])
        mine, other = pick(halves, ci, 0), shift(pick(halves, 1 - ci, 0), "c", 1)
        return jnp.stack([jnp.where(is_first, mine, other), jnp.where(is_first, other, mine)])

    small = jnp.concatenate(
        [
            w_compress,
            gain_attn[:, None],
            gain_ffn[:, None],
            w_router,
            jnp.pad(gain_latent, (0, 48))[:, None],
            jnp.zeros((64, 53), bf16),
        ],
        axis=1,
    )
    small_all = lax.all_gather(small, ("x", "z", "c"), axis=0, tiled=True)
    compress_w = small_all[:, :576]
    gain_first = small_all[:, 576].astype(f32)
    gain_second = small_all[:, 577].astype(f32)
    router_w = small_all[:, 578:586]
    latent_gain = small_all[:, 586].reshape(32, 64)[:, :16].reshape(RANK).astype(f32)

    by_head = w_query.reshape(64, heads, NOPE + ROPE)
    attn_all = lax.all_gather(
        jnp.concatenate(
            [
                by_head[:, :, :NOPE].reshape(64, 512),
                by_head[:, :, NOPE:].reshape(64, 256),
                w_output,
                w_expand.reshape(16, heads, 256).transpose(1, 0, 2).reshape(64, 256),
            ],
            axis=1,
        ),
        ("x", "z", "c"),
        axis=0,
        tiled=True,
    )

    packed_w = jnp.concatenate(
        [
            w_expert_in[:, :, 0],
            w_shared_in[:, 0].reshape(64, 8, 88),
            w_expert_in[:, :, 1],
            w_shared_in[:, 1].reshape(64, 8, 88),
            jnp.broadcast_to(w_router[:, None, :], (64, 8, 8)),
            jnp.zeros((64, 8, 8), bf16),
            w_expert_out,
            w_shared_out.reshape(64, 8, 88),
        ],
        axis=-1,
    )
    packed_w = packed_w.transpose(1, 0, 2).reshape(4, 2, 64, 1336)
    mine_w, other_w = pick(packed_w, ci, 1), shift(pick(packed_w, 1 - ci, 1), "c", 1)
    pair_w = jnp.concatenate(
        [jnp.where(is_first, mine_w, other_w), jnp.where(is_first, other_w, mine_w)], axis=1
    )
    pieces = gather_near(exchange_at(pair_w, "x").reshape(512, 1336), "z")

    inputs = enter(tokens).astype(f32)
    chosen = jnp.sum(
        (routes[..., None] == jnp.arange(EXPERTS, dtype=jnp.int32)).astype(f32), axis=2
    )
    spread = jnp.concatenate(
        [
            to_far(cotangent.reshape(128, dim)),
            chosen.reshape(128, 8).astype(bf16),
            jnp.zeros((128, 120), bf16),
        ],
        axis=1,
    )
    spread = enter(spread.reshape(2, 64, 2176))

    def own(value):
        return lax.dynamic_slice_in_dim(value, yi * 32, 32, 0)

    spread_own = own(spread)
    d_out_own = to_far(spread_own[:, :2048])
    chosen_own = spread_own[:, 2048:2056].astype(f32)
    inputs_own = own(inputs)
    spread = jnp.concatenate(
        [lax.dynamic_slice_in_dim(spread, lax.rem(yi - s + 4, 4) * 32, 32, 0) for s in range(4)]
    )
    spread = jnp.concatenate(gather_near(spread, "x"), axis=0)
    spread_other = shift(spread, "c", 1)

    position = (xi * 4 + zi) * 128 + jnp.arange(128, dtype=jnp.int32)
    segment_row = pick(segment, ci, 0)
    blocks = jnp.stack(
        [lax.rem(xi - sx + 4, 4) * 4 + lax.rem(zi - sz + 4, 4) for sx in range(4) for sz in range(4)]
    )
    segment_near = segment_row.reshape(16, 128)[blocks].reshape(2048)
    key_place = (blocks[:, None] * 128 + jnp.arange(128, dtype=jnp.int32)[None, :]).reshape(2048)
    where_k = jnp.stack([key_place, segment_near])
    where_q = jnp.stack(
        [position, lax.dynamic_slice_in_dim(segment_row, (xi * 4 + zi) * 128, 128)], axis=1
    )
    normed_full, factor_one = norm_forward(inputs, gain_first)
    normed = normed_full.astype(bf16)
    compressed = dot_nn(normed, compress_w)
    latent_full, factor_latent = norm_forward(compressed[:, :RANK], latent_gain)
    packed = jnp.concatenate(
        [latent_full, rotate_parts(compressed[:, RANK:], position, False)], axis=1
    ).astype(bf16)
    parts_a = gather_near(jnp.concatenate(gather_near(packed[:, :256], "x"), axis=0), "z")
    parts_b = gather_near(jnp.concatenate(gather_near(packed[:, 256:], "z"), axis=0), "x")

    q_raw = dot_nn(normed, attn_all[:, :768])
    rot = rotate_parts(q_raw[:, 512:].reshape(128, heads, ROPE), position, False)
    query = (
        jnp.concatenate(
            [q_raw[:, :512].reshape(128, heads, NOPE), rot, jnp.zeros((128, heads, 64), f32)],
            axis=-1,
        )
        .astype(bf16)
        .reshape(128, heads * 256)
    )
    prob, kv, attended, latent_all, *branch = attend(
        place, query, parts_a, parts_b, attn_all, where_q, where_k
    )
    middle = inputs_own + sum_ahead(branch, "y")

    normed_ffn_full, factor_two = norm_forward(middle, gain_second)
    normed_ffn = normed_ffn_full.astype(bf16)
    far = to_far(normed_ffn)
    far_a = jnp.stack(gather_near(jnp.concatenate(gather_near(far[:, :1024], "x")), "y"))
    far_b = jnp.stack(gather_near(jnp.concatenate(gather_near(far[:, 1024:], "y")), "x"))
    far_a = far_a.reshape(4, 4, 32, 1024).transpose(1, 0, 2, 3).reshape(512, 1024)
    far = jnp.concatenate([far_a, far_b.reshape(512, 1024)], axis=1)
    far_other = shift(far, "c", 1)
    d_far, d_hidden, hidden, out_far = run_expert(place, far, spread, pieces)
    d_far2, d_hidden2, hidden2, out_far2 = run_expert(place, far_other, spread_other, pieces)

    d_far = (d_far.astype(f32) + shift(d_far2, "c", 1).astype(f32)).astype(bf16)
    d_far = d_far.reshape(4, 4, 32, 2176)
    part_a = sum_near([d_far[s, :, :, :1024] for s in range(4)], "x").astype(bf16)
    part_b = sum_near([d_far[:, s, :, 1024:] for s in range(4)], "y").astype(bf16)
    d_own = jnp.concatenate(
        [
            sum_near([part_a[s] for s in range(4)], "y"),
            sum_near([part_b[s] for s in range(4)], "x"),
        ],
        axis=1,
    )

    out_far = (out_far.astype(f32) + shift(out_far2, "c", 1).astype(f32)).astype(bf16)
    out_far = out_far.reshape(4, 128, dim)
    out_far = sum_near([out_far[s] for s in range(4)], "x").astype(bf16).reshape(4, 32, dim)
    out_far = sum_near([out_far[s] for s in range(4)], "y")
    mixed = (middle + to_far(out_far)).astype(bf16)
    mixed = leave(gather_at(mixed, "y").reshape(128, dim))

    grad_ffn = expert_grad(
        (far, far_other), (spread, spread_other), (d_hidden, d_hidden2), (hidden, hidden2)
    )
    grad_ffn = lax.psum_scatter(grad_ffn, "z", scatter_dimension=0, tiled=True)
    grad_ffn = exchange_at(grad_ffn.reshape(4, 128, 1336), "x").reshape(4, 2, 64, 1336)
    mine_g, other_g = pick(grad_ffn, ci, 1), shift(pick(grad_ffn, 1 - ci, 1), "c", 1)
    grad_ffn = jnp.stack(
        [jnp.where(is_first, mine_g, other_g), jnp.where(is_first, other_g, mine_g)], axis=1
    )
    grad_ffn = grad_ffn.reshape(8, 64, 1336).transpose(1, 0, 2).astype(f32)
    g_expert_in = jnp.stack([grad_ffn[..., :352], grad_ffn[..., 440:792]], axis=2)
    g_shared_in = jnp.stack(
        [grad_ffn[..., 352:440].reshape(64, 704), grad_ffn[..., 792:880].reshape(64, 704)], axis=1
    )
    g_expert_out = grad_ffn[..., 896:1248]
    g_shared_out = grad_ffn[..., 1248:].reshape(64, 704)

    router = jax.nn.softmax(dot_nn(normed_ffn, router_w), axis=-1)
    d_chosen = d_own[:, 2048:2056] * chosen_own
    d_logits = (router * (d_chosen - jnp.sum(router * d_chosen, axis=-1, keepdims=True))).astype(bf16)
    d_normed_ffn = to_far(d_own[:, :2048]) + dot_nt(d_logits, router_w)
    d_middle_norm, d_gain_two = norm_backward(middle, factor_two, gain_second, d_normed_ffn)
    d_middle = d_out_own.astype(f32) + d_middle_norm
    g_router = dot_tn(normed_ffn, d_logits)

    half = ROPE // 2
    freq = jnp.exp(jnp.arange(half, dtype=f32) * (-jnp.log(10000.0) / half))
    angle = position.astype(f32)[:, None] * freq[None, :]
    cosine = jnp.tile(jnp.cos(angle), (1, 8))
    sine = jnp.tile(jnp.concatenate([jnp.sin(angle), -jnp.sin(angle)], axis=1), (1, 4))
    d_q, d_rot, d_expanded, d_branch, *rest = attend_back(
        place, gather_near(d_middle.astype(bf16), "y"), query, kv, prob, latent_all, attn_all,
        cosine, sine,
    )
    terms_a = sum_near(rest[0:4], "x").astype(bf16).reshape(4, 128, 256)
    terms_b = sum_near(rest[4:8], "z").astype(bf16)
    terms = jnp.concatenate(
        [
            sum_near([terms_a[s] for s in range(4)], "z"),
            sum_near([terms_b[s] for s in range(4)], "x"),
        ],
        axis=1,
    ).astype(bf16)
    terms = sum_at(terms.reshape(4, 32, 576), "y", 0)
    d_query_own = sum_ahead(rest[8:12], "y")

    d_comp_latent, d_latent_gain = norm_backward(
        own(compressed)[:, :RANK], own(factor_latent), latent_gain, terms[:, :RANK]
    )
    d_compressed = jnp.concatenate(
        [d_comp_latent, rotate_parts(terms[:, RANK:], own(position), True)], axis=1
    ).astype(bf16)
    d_normed = d_query_own + dot_nt(d_compressed, compress_w)
    d_inputs, d_gain_one = norm_backward(inputs_own, own(factor_one), gain_first, d_normed)
    grad_rows = (d_middle + d_inputs).astype(bf16)
    grad_rows = leave(gather_at(grad_rows, "y").reshape(128, dim))

    def fsdp_sum(value, first, second):
        value = value.reshape(4, 4, 2, 64, -1)
        value = sum_ahead([pick(value, ci, 2), pick(value, 1 - ci, 2)], "c").astype(bf16)
        value = sum_at(value, first, 0 if first == "x" else 1).astype(bf16)
        return sum_at(value, second, 0)

    g_attn = attn_grad(normed, d_q, d_rot, d_branch, attended)
    g_query = fsdp_sum(g_attn[:, :768], "x", "z")
    g_query = jnp.concatenate(
        [g_query[:, :512].reshape(64, heads, NOPE), g_query[:, 512:].reshape(64, heads, ROPE)],
        axis=-1,
    ).reshape(64, 768)
    g_expand = dot_tn(latent_all[:, :RANK], d_expanded)
    g_expand = (
        g_expand.astype(bf16)
        .reshape(32, 16, heads, 256)
        .transpose(0, 2, 1, 3)
        .reshape(2048, 256)
    )
    g_other = fsdp_sum(jnp.concatenate([g_attn[:, 768:], g_expand], axis=1), "z", "x")
    g_output = g_other[:, :512]
    g_expand = (
        g_other[:, 512:].reshape(heads, 16, 256).transpose(1, 0, 2).reshape(16, heads * 256)
    )

    d_compressed_all = gather_at(d_compressed, "y").reshape(128, 576)
    d_compressed_mine = jnp.concatenate(
        [
            lax.dynamic_slice_in_dim(d_compressed_all[:, :RANK], yi * 128, 128, 1),
            d_compressed_all[:, RANK:],
        ],
        axis=1,
    )
    g_compress = dot_tn(normed, d_compressed_mine)
    g_small = jnp.concatenate(
        [
            g_compress,
            d_gain_one[:, None],
            d_gain_two[:, None],
            g_router,
            jnp.pad(d_latent_gain.reshape(32, 16), ((0, 0), (0, 48))).reshape(dim, 1),
            jnp.zeros((dim, 53), f32),
        ],
        axis=1,
    ).astype(bf16)
    g_small = gather_at(fsdp_sum(g_small, "x", "z").astype(bf16), "y").astype(f32)
    g_compress = jnp.concatenate(
        [g_small[i, :, :128] for i in range(4)] + [g_small[0, :, 128:192]], axis=1
    )
    g_small = jnp.sum(g_small[:, :, 192:], axis=0)

    return (
        mixed,
        grad_rows,
        g_small[:, 0],
        g_query,
        g_compress,
        g_small[:16, 10],
        g_expand,
        g_output,
        g_small[:, 1],
        g_small[:, 2:10],
        g_expert_in,
        g_expert_out,
        g_shared_in,
        g_shared_out,
    )


def solution(mesh):
    fine = Mesh(mesh.devices.reshape(4, 4, 2, 4), ("x", "z", "c", "y"))
    rows = ("x", "z", "c")
    return jax.shard_map(
        on_device,
        mesh=fine,
        in_specs=(
            P(None, rows, None),
            P(),
            P(None, rows, None),
            P(None, rows, None),
            P(rows),
            P(rows, "y"),
            P(rows, None),
            P(rows),
            P(rows, "y"),
            P(rows, "y"),
            P(rows),
            P(rows, None),
            P(rows, None, None, "y"),
            P(rows, None, "y"),
            P(rows, None, "y"),
            P(rows, "y"),
        ),
        out_specs=(
            P(None, rows, None),
            P(None, rows, None),
            P(rows),
            P(rows, "y"),
            P(rows, None),
            P(rows),
            P(rows, "y"),
            P(rows, "y"),
            P(rows),
            P(rows, None),
            P(rows, None, None, "y"),
            P(rows, None, "y"),
            P(rows, None, "y"),
            P(rows, "y"),
        ),
        check_vma=False,
    )
```

```python
import jax
import jax.numpy as jnp
from jax import lax
from jax.experimental import pallas as pl
from jax.experimental.pallas import tpu as pltpu
from jax.sharding import Mesh
from jax.sharding import PartitionSpec as P

NOPE = 128
ROPE = 64
VHEAD = 128
RANK = 512
EXPERTS = 8

epsilon = 1e-06
bf16 = jnp.bfloat16
f32 = jnp.float32


def rotate_parts(values, position, inverse):
    half = values.shape[-1] // 2
    freq = jnp.exp(jnp.arange(half, dtype=f32) * (-jnp.log(10000.0) / half))
    angle = position.astype(f32)[:, None] * freq[None, :]
    cosine = jnp.cos(angle)
    sine = jnp.sin(angle)
    if inverse:
        sine = -sine
    if values.ndim == 3:
        cosine = cosine[:, None, :]
        sine = sine[:, None, :]
    first = values[..., :half]
    second = values[..., half:]
    return jnp.concatenate(
        [first * cosine - second * sine, second * cosine + first * sine], axis=-1
    )


def norm_forward(values, gain):
    factor = lax.rsqrt(jnp.mean(values * values, axis=-1, keepdims=True) + epsilon)
    return (values * factor * gain, factor)


def norm_backward(values, factor, gain, grad):
    scaled = grad * gain
    d_values = factor * scaled - values * (factor * factor * factor) * jnp.mean(
        values * scaled, axis=-1, keepdims=True
    )
    d_gain = jnp.sum(grad * values * factor, axis=0)
    return (d_values, d_gain)


def shift(value, axis, step):
    count = lax.axis_size(axis)
    return lax.ppermute(value, axis, [(i, (i + step) % count) for i in range(count)])


def pick(value, place, at):
    return lax.dynamic_index_in_dim(value, place, at, keepdims=False)


def gather_near(value, axis):
    return [value] + [shift(value, axis, s) for s in range(1, lax.axis_size(axis))]


def gather_at(value, axis):
    count = lax.axis_size(axis)
    me = lax.axis_index(axis)
    whole = jnp.zeros((count,) + value.shape, value.dtype)
    for s in range(count):
        part = value if s == 0 else shift(value, axis, s)
        whole = lax.dynamic_update_index_in_dim(whole, part, lax.rem(me - s + count, count), 0)
    return whole


def sum_near(parts, axis):
    total = parts[0].astype(f32)
    for s in range(1, len(parts)):
        total = total + shift(parts[s], axis, -s).astype(f32)
    return total


def sum_ahead(parts, axis):
    total = parts[0].astype(f32)
    for s in range(1, len(parts)):
        total = total + shift(parts[s], axis, s).astype(f32)
    return total


def sum_at(value, axis, at):
    count = lax.axis_size(axis)
    me = lax.axis_index(axis)
    return sum_ahead([pick(value, lax.rem(me + s, count), at) for s in range(count)], axis)


def exchange_at(value, axis):
    count = lax.axis_size(axis)
    me = lax.axis_index(axis)
    whole = jnp.zeros_like(value)
    for s in range(count):
        part = pick(value, lax.rem(me + s, count), 0)
        part = part if s == 0 else shift(part, axis, s)
        whole = lax.dynamic_update_index_in_dim(whole, part, lax.rem(me - s + count, count), 0)
    return whole


def to_far(value):
    rows = value.shape[0]
    return value.reshape(rows, 4, 4, 128).transpose(0, 2, 1, 3).reshape(rows, 2048)


def dot_nn(a, b):
    return jnp.dot(a, b, preferred_element_type=f32)


def dot_nt(a, b):
    return lax.dot_general(a, b, (((1,), (1,)), ((), ())), preferred_element_type=f32)


def dot_tn(a, b):
    return lax.dot_general(a, b, (((0,), (0,)), ((), ())), preferred_element_type=f32)


def whole(*shape):
    return pl.BlockSpec(shape, lambda h: (0,) * len(shape))


SCALARS = pl.BlockSpec(memory_space=pltpu.SMEM)
SCALE = (NOPE + ROPE) ** (-0.5)
MIB = 1024 * 1024


def front_kernel(
    place, tok, mine, other, cosine, sine, normed, packed, compressed, weight, gains
):
    for sx in range(4):
        for sz in range(4):
            block = lax.rem(place[0] - sx + 4, 4) * 4 + lax.rem(place[1] - sz + 4, 4)
            for part, core in ((mine, place[2]), (other, 1 - place[2])):
                row = pl.multiple_of(block * 128 + core * 64, 64)
                src = (sz * 4 + sx) * 64
                weight[pl.ds(row, 64), :] = part[src : src + 64, :]
    turned = weight[:, 512:640].astype(f32).T
    gains[0:2, :] = turned[64:66, :]
    latent_gain = jnp.concatenate(
        [turned[74:75, 64 * i : 64 * i + 16] for i in range(32)], axis=1
    )
    gains[2:3, :RANK] = latent_gain
    values = tok[...].astype(f32)
    factor = lax.rsqrt(jnp.mean(values * values, axis=1, keepdims=True) + epsilon)
    low = (values * factor * turned[64:65, :]).astype(bf16)
    normed[...] = low
    raw = dot_nn(low, weight[:, :576])
    compressed[...] = raw
    main = raw[:, :RANK]
    factor = lax.rsqrt(jnp.mean(main * main, axis=1, keepdims=True) + epsilon)
    latent = (main * factor * latent_gain).astype(bf16)
    first, second = raw[:, RANK : RANK + 32], raw[:, RANK + 32 :]
    cos, sin = cosine[:, :32], sine[:, :32]
    rot = jnp.concatenate([first * cos - second * sin, second * cos + first * sin], axis=1)
    packed[:, :RANK] = latent
    packed[:, RANK:] = jnp.concatenate([rot, jnp.zeros((128, 64), f32)], axis=1).astype(bf16)


def front(place, tok, mine, other, cosine, sine):
    return pl.pallas_call(
        front_kernel,
        in_specs=[SCALARS] + [pl.BlockSpec(memory_space=pltpu.VMEM)] * 5,
        out_specs=[pl.BlockSpec(memory_space=pltpu.VMEM)] * 5,
        out_shape=[
            jax.ShapeDtypeStruct((128, 2048), bf16),
            jax.ShapeDtypeStruct((128, 640), bf16),
            jax.ShapeDtypeStruct((128, 576), f32),
            jax.ShapeDtypeStruct((2048, 640), bf16),
            jax.ShapeDtypeStruct((8, 2048), f32),
        ],
        compiler_params=pltpu.CompilerParams(vmem_limit_bytes=32 * MIB),
        cost_estimate=pl.CostEstimate(
            flops=10**9, bytes_accessed=9 * 10**6, transcendentals=0
        ),
        name="front",
    )(place, tok, mine, other, cosine, sine)


def attend_kernel(
    place, normed, nope_w, rot_w, cosine, sine, l0, l1, l2, l3, expand, out_w,
    where_q, where_k, prob, kv, attended, lat, q, r0, r1, r2, r3, rot_q, total,
):
    head = pl.program_id(0)

    @pl.when(head == 0)
    def _():
        for sx in range(4):
            lat[sx * 512 : sx * 512 + 512, :] = (l0, l1, l2, l3)[sx][...]
        total[...] = jnp.zeros_like(total)
        rot = dot_nn(normed[...], rot_w[...])
        lane = lax.broadcasted_iota(jnp.int32, rot.shape, 1)
        partner = jnp.where(
            lane % 64 < 32, pltpu.roll(rot, 224, 1), pltpu.roll(rot, 32, 1)
        )
        rot = (rot * cosine[...] - partner * sine[...]).astype(bf16)
        for h in range(4):
            rot_q[h] = jnp.concatenate(
                [rot[:, 64 * h : 64 * h + 64], jnp.zeros((128, 64), bf16)], axis=1
            )

    nope = dot_nn(normed[...], nope_w[...]).astype(bf16)
    rot_h = rot_q[head]
    q[:, :128] = nope
    q[:, 128:] = rot_h
    expand_h = expand[...].reshape(RANK, 256)
    kv_h = dot_nn(lat[:, :RANK], expand_h).astype(bf16)
    kv[...] = kv_h
    score = (dot_nt(nope, kv_h[:, :128]) + dot_nt(rot_h, lat[:, RANK:])) * SCALE
    allowed = (where_q[:, 0:1] >= where_k[0:1, :]) & (where_q[:, 1:2] == where_k[1:2, :])
    score = jnp.where(allowed, score, -1e30)
    power = jnp.exp(score - jnp.max(score, axis=1, keepdims=True))
    prob_h = power / jnp.sum(power, axis=1, keepdims=True)
    prob[0] = prob_h
    attended_h = dot_nn(prob_h.astype(bf16), kv_h[:, 128:]).astype(bf16)
    attended[...] = attended_h
    total[...] += dot_nt(attended_h, out_w[...])

    @pl.when(head == 3)
    def _():
        for s, out in enumerate((r0, r1, r2, r3)):
            row = pl.multiple_of(lax.rem(place[3] + s, 4) * 32, 32)
            out[...] = total[pl.ds(row, 32), :].astype(bf16)


LOOSE = pl.BlockSpec(memory_space=pl.ANY)


def attend(place, normed, parts, attn_all, cosine, sine, where_q, where_k):
    by_head = attn_all.reshape(32, 4, 16, 1536)
    return pl.pallas_call(
        attend_kernel,
        grid=(4,),
        in_specs=[
            SCALARS,
            whole(128, 2048),
            pl.BlockSpec((2048, 128), lambda h: (0, h)),
            pl.BlockSpec((2048, 256), lambda h: (0, 2)),
            whole(128, 256),
            whole(128, 256),
        ]
        + [whole(512, 640)] * 4
        + [
            pl.BlockSpec((32, 1, 16, 256), lambda h: (0, h, 0, 5)),
            pl.BlockSpec((2048, 128), lambda h: (0, 6 + h)),
            whole(128, 2),
            whole(2, 2048),
        ],
        out_specs=[
            pl.BlockSpec((1, 128, 2048), lambda h: (h, 0, 0)),
            pl.BlockSpec((2048, 256), lambda h: (0, h)),
            pl.BlockSpec((128, 128), lambda h: (0, h)),
            whole(2048, 640),
            pl.BlockSpec((128, 256), lambda h: (0, h)),
        ]
        + [whole(32, 2048)] * 4,
        out_shape=[
            jax.ShapeDtypeStruct((4, 128, 2048), f32),
            jax.ShapeDtypeStruct((2048, 1024), bf16),
            jax.ShapeDtypeStruct((128, 512), bf16),
            jax.ShapeDtypeStruct((2048, 640), bf16),
            jax.ShapeDtypeStruct((128, 1024), bf16),
        ]
        + [jax.ShapeDtypeStruct((32, 2048), bf16)] * 4,
        scratch_shapes=[
            pltpu.VMEM((4, 128, 128), bf16),
            pltpu.VMEM((128, 2048), f32),
        ],
        compiler_params=pltpu.CompilerParams(vmem_limit_bytes=48 * MIB),
        cost_estimate=pl.CostEstimate(
            flops=5 * 10**9, bytes_accessed=26 * 10**6, transcendentals=2**20
        ),
        name="attend",
    )(
        place, normed, attn_all, attn_all, cosine, sine, *parts, by_head, attn_all,
        where_q, where_k,
    )


def far_block(b):
    return (b % 4) * 4 + b // 4


def middle_kernel(place, r0, r1, r2, r3, tok, gains, tie, middle, far):
    row = pl.multiple_of(place[3] * 32, 32)
    values = tok[pl.ds(row, 32), :].astype(f32)
    for part in (r0, r1, r2, r3):
        values = values + part[...].astype(f32)
    middle[...] = values
    factor = lax.rsqrt(jnp.mean(values * values, axis=1, keepdims=True) + epsilon)
    low = (values * factor * gains[1:2, :]).astype(bf16)
    for b in range(16):
        at = far_block(b)
        far[:, at * 128 : at * 128 + 128] = low[:, b * 128 : b * 128 + 128]


def run_middle(place, parts, tok, gains, tie):
    vmem = pl.BlockSpec(memory_space=pltpu.VMEM)
    return pl.pallas_call(
        middle_kernel,
        in_specs=[SCALARS] + [vmem] * 6 + [LOOSE],
        out_specs=[vmem] * 2,
        out_shape=[
            jax.ShapeDtypeStruct((32, 2048), f32),
            jax.ShapeDtypeStruct((32, 2048), bf16),
        ],
        cost_estimate=pl.CostEstimate(flops=10**6, bytes_accessed=2 * 10**6, transcendentals=0),
        name="middle",
    )(place, *parts, tok, gains, tie)


def middle_back_kernel(
    place, a0, a1, a2, a3, spread, middle, gains, weight, tie, d_mid, d_low, small
):
    row = pl.multiple_of(place[3] * 32, 32)
    total = a0[...].astype(f32)
    for part in (a1, a2, a3):
        total = total + part[...].astype(f32)
    near = lambda v: jnp.concatenate(
        [v[:, far_block(b) * 128 : far_block(b) * 128 + 128] for b in range(16)], axis=1
    )
    d_normed = near(total[:, :2048])
    d_gate = total[:, 2048:]
    mine = spread[pl.ds(row, 32), :]
    d_out = near(mine[:, :2048]).astype(f32)
    chosen = mine[:, 2048:].astype(f32)
    values = middle[...]
    gain = gains[1:2, :]
    factor = lax.rsqrt(jnp.mean(values * values, axis=1, keepdims=True) + epsilon)
    low = (values * factor * gain).astype(bf16)
    table = weight[:, 512:640]
    lane = lax.broadcasted_iota(jnp.int32, (32, 128), 1)
    is_expert = (lane >= 66) & (lane < 74)
    logits = jnp.where(is_expert, dot_nn(low, table), -1e30)
    power = jnp.exp(logits - jnp.max(logits, axis=1, keepdims=True))
    router = power / jnp.sum(power, axis=1, keepdims=True)
    d_chosen = d_gate * chosen
    d_logits = router * (d_chosen - jnp.sum(router * d_chosen, axis=1, keepdims=True))
    d_logits = d_logits.astype(bf16)
    d_normed = d_normed + dot_nt(d_logits, table)
    scaled = d_normed * gain
    d_norm = factor * scaled - values * (factor * factor * factor) * jnp.mean(
        values * scaled, axis=1, keepdims=True
    )
    d_values = d_out + d_norm
    d_mid[...] = d_values
    d_low[...] = d_values.astype(bf16)
    terms = (d_normed * values * factor).astype(bf16)
    small[...] = (
        dot_tn(low, d_logits) + dot_tn(terms, (lane == 65).astype(bf16))
    ).astype(bf16)


def middle_back(place, parts, spread, middle, gains, weight, tie):
    vmem = pl.BlockSpec(memory_space=pltpu.VMEM)
    return pl.pallas_call(
        middle_back_kernel,
        in_specs=[SCALARS] + [vmem] * 8 + [LOOSE],
        out_specs=[vmem] * 3,
        out_shape=[
            jax.ShapeDtypeStruct((32, 2048), f32),
            jax.ShapeDtypeStruct((32, 2048), bf16),
            jax.ShapeDtypeStruct((2048, 128), bf16),
        ],
        compiler_params=pltpu.CompilerParams(vmem_limit_bytes=32 * MIB),
        cost_estimate=pl.CostEstimate(
            flops=10**8, bytes_accessed=5 * 10**6, transcendentals=0
        ),
        name="middle_back",
    )(place, *parts, spread, middle, gains, weight, tie)


def latent_back_kernel(
    place, t0, t1, t2, t3, compressed, gains, cosine, sine, tie, d_comp, small
):
    row = pl.multiple_of(place[3] * 32, 32)
    terms = t0[...].astype(f32)
    for part in (t1, t2, t3):
        terms = terms + part[...].astype(f32)
    main = compressed[pl.ds(row, 32), :][:, :RANK]
    factor = lax.rsqrt(jnp.mean(main * main, axis=1, keepdims=True) + epsilon)
    grad_main = terms[:, :RANK]
    scaled = grad_main * gains[2:3, :RANK]
    d_main = factor * scaled - main * (factor * factor * factor) * jnp.mean(
        main * scaled, axis=1, keepdims=True
    )
    first, second = terms[:, RANK : RANK + 32], terms[:, RANK + 32 : RANK + 64]
    cos, sin = cosine[pl.ds(row, 32), :][:, :32], sine[pl.ds(row, 32), :][:, :32]
    rot = jnp.concatenate([first * cos + second * sin, second * cos - first * sin], axis=1)
    d_comp[:, :RANK] = d_main.astype(bf16)
    d_comp[:, RANK:] = jnp.concatenate([rot, jnp.zeros((32, 64), f32)], axis=1).astype(bf16)
    latent_terms = grad_main * main * factor
    gap = jnp.zeros((32, 48), f32)
    latent_terms = jnp.concatenate(
        [p for i in range(32) for p in (latent_terms[:, 16 * i : 16 * i + 16], gap)], axis=1
    )
    lane = lax.broadcasted_iota(jnp.int32, (32, 128), 1)
    small[...] = dot_tn(latent_terms.astype(bf16), (lane == 74).astype(bf16)).astype(bf16)


def latent_back(place, terms, compressed, gains, cosine, sine, tie):
    vmem = pl.BlockSpec(memory_space=pltpu.VMEM)
    return pl.pallas_call(
        latent_back_kernel,
        in_specs=[SCALARS] + [vmem] * 8 + [LOOSE],
        out_specs=[vmem] * 2,
        out_shape=[
            jax.ShapeDtypeStruct((32, 640), bf16),
            jax.ShapeDtypeStruct((2048, 128), bf16),
        ],
        compiler_params=pltpu.CompilerParams(vmem_limit_bytes=32 * MIB),
        cost_estimate=pl.CostEstimate(flops=10**7, bytes_accessed=10**6, transcendentals=0),
        name="latent_back",
    )(place, *terms, compressed, gains, cosine, sine, tie)


def token_back_kernel(place, d_comp, q0, q1, q2, q3, tok, gains, weight, d_mid, grad, small):
    row = pl.multiple_of(place[3] * 32, 32)
    d_normed = dot_nt(d_comp[...], weight[:, :640])
    for part in (q0, q1, q2, q3):
        d_normed = d_normed + part[...].astype(f32)
    values = tok[pl.ds(row, 32), :].astype(f32)
    factor = lax.rsqrt(jnp.mean(values * values, axis=1, keepdims=True) + epsilon)
    scaled = d_normed * gains[0:1, :]
    d_norm = factor * scaled - values * (factor * factor * factor) * jnp.mean(
        values * scaled, axis=1, keepdims=True
    )
    grad[...] = (d_mid[...] + d_norm).astype(bf16)
    lane = lax.broadcasted_iota(jnp.int32, (32, 128), 1)
    small[...] = dot_tn(
        (d_normed * values * factor).astype(bf16), (lane == 64).astype(bf16)
    ).astype(bf16)


def token_back(place, d_comp, d_queries, tok, gains, weight, d_mid):
    vmem = pl.BlockSpec(memory_space=pltpu.VMEM)
    return pl.pallas_call(
        token_back_kernel,
        in_specs=[SCALARS] + [vmem] * 9,
        out_specs=[vmem] * 2,
        out_shape=[
            jax.ShapeDtypeStruct((32, 2048), bf16),
            jax.ShapeDtypeStruct((2048, 128), bf16),
        ],
        compiler_params=pltpu.CompilerParams(vmem_limit_bytes=32 * MIB),
        cost_estimate=pl.CostEstimate(
            flops=10**8, bytes_accessed=4 * 10**6, transcendentals=0
        ),
        name="token_back",
    )(place, d_comp, *d_queries, tok, gains, weight, d_mid)


def compress_grad_kernel(place, c0, c1, c2, c3, normed, s0, s1, s2, *rest):
    mine, other, d_all = rest[-3:]
    for s, part in enumerate((c0, c1, c2, c3)):
        row = pl.multiple_of(lax.rem(place[3] - s + 4, 4) * 32, 32)
        d_all[pl.ds(row, 32), :] = part[...]
    column = pl.multiple_of(place[3] * 128, 128)
    own = d_all[:, pl.ds(column, 128)]
    rot = d_all[:, RANK:]
    main = dot_tn(normed[...], own).astype(bf16)
    rest = dot_tn(normed[...], rot)
    for part in (s0, s1, s2):
        rest = rest + part[...].astype(f32)
    rest = rest.astype(bf16)
    is_first = place[2] == 0
    for b in range(16):
        for columns, value in ((slice(0, 128), main), (slice(128, 256), rest)):
            low, high = value[b * 128 : b * 128 + 64], value[b * 128 + 64 : b * 128 + 128]
            mine[b * 64 : b * 64 + 64, columns] = jnp.where(is_first, low, high)
            other[b * 64 : b * 64 + 64, columns] = jnp.where(is_first, high, low)


def compress_grad(place, parts, normed, smalls, tie):
    vmem = pl.BlockSpec(memory_space=pltpu.VMEM)
    return pl.pallas_call(
        compress_grad_kernel,
        in_specs=[SCALARS] + [vmem] * 8 + [LOOSE] * len(tie),
        out_specs=[vmem] * 2,
        out_shape=[jax.ShapeDtypeStruct((1024, 256), bf16)] * 2,
        scratch_shapes=[pltpu.VMEM((128, 640), bf16)],
        compiler_params=pltpu.CompilerParams(vmem_limit_bytes=32 * MIB),
        cost_estimate=pl.CostEstimate(
            flops=2 * 10**8, bytes_accessed=3 * 10**6, transcendentals=0
        ),
        name="compress_grad",
    )(place, *parts, normed, *smalls, *tie)


def attend_back_kernel(
    place, d0, d1, d2, d3, out_w, q, kv, prob, lat, expand, nope_w, rot_w, cosine, sine, tie,
    d_q, d_rot, d_exp, d_branch, k0, k1, k2, k3, r0, r1, r2, r3,
    lat_sum, rot_sum, rot_q, total,
):
    head = pl.program_id(0)

    @pl.when(head == 0)
    def _():
        for s, part in enumerate((d0, d1, d2, d3)):
            row = pl.multiple_of(lax.rem(place[3] - s + 4, 4) * 32, 32)
            d_branch[pl.ds(row, 32), :] = part[...]
        lat_sum[...] = jnp.zeros_like(lat_sum)
        rot_sum[...] = jnp.zeros_like(rot_sum)
        total[...] = jnp.zeros_like(total)

    d_att = dot_nn(d_branch[...], out_w[...]).astype(bf16)
    prob_h = prob[0]
    d_prob = dot_nt(d_att, kv[:, 128:])
    row_sum = jnp.sum(prob_h * d_prob, axis=1, keepdims=True)
    d_score = (prob_h * (d_prob - row_sum)).astype(bf16)
    d_nope = (dot_nn(d_score, kv[:, :128]) * SCALE).astype(bf16)
    d_q[...] = d_nope
    rot_q[head] = dot_nn(d_score, lat[:, RANK:]) * SCALE
    d_key = dot_tn(d_score, q[...]) * SCALE
    d_val = dot_tn(prob_h.astype(bf16), d_att)
    d_exp_h = jnp.concatenate([d_key[:, :128], d_val], axis=1).astype(bf16)
    d_exp[...] = d_exp_h
    rot_sum[...] += d_key[:, 128:]
    lat_sum[...] += dot_nt(d_exp_h, expand[...].reshape(RANK, 256))
    total[...] += dot_nt(d_nope, nope_w[...])

    @pl.when(head == 3)
    def _():
        rot = jnp.concatenate([rot_q[h][:, :64] for h in range(4)], axis=1)
        lane = lax.broadcasted_iota(jnp.int32, rot.shape, 1)
        partner = jnp.where(
            lane % 64 < 32, pltpu.roll(rot, 224, 1), pltpu.roll(rot, 32, 1)
        )
        rot = (rot * cosine[...] + partner * sine[...]).astype(bf16)
        d_rot[...] = rot
        summed = total[...] + dot_nt(rot, rot_w[...])
        total[...] = summed
        for s, out in enumerate((r0, r1, r2, r3)):
            row = pl.multiple_of(lax.rem(place[3] + s, 4) * 32, 32)
            out[...] = total[pl.ds(row, 32), :].astype(bf16)
        for sx in range(4):
            rows = slice(sx * 512, sx * 512 + 512)
            out = (k0, k1, k2, k3)[sx]
            out[:, :RANK] = lat_sum[rows, :].astype(bf16)
            out[:, RANK:] = rot_sum[rows, :].astype(bf16)


def attend_back(place, parts, q, kv, prob, lat, attn_all, cosine, sine, tie):
    by_head = attn_all.reshape(32, 4, 16, 1536)
    return pl.pallas_call(
        attend_back_kernel,
        grid=(4,),
        in_specs=[SCALARS]
        + [whole(32, 2048)] * 4
        + [
            pl.BlockSpec((2048, 128), lambda h: (0, 6 + h)),
            pl.BlockSpec((128, 256), lambda h: (0, h)),
            pl.BlockSpec((2048, 256), lambda h: (0, h)),
            pl.BlockSpec((1, 128, 2048), lambda h: (h, 0, 0)),
            whole(2048, 640),
            pl.BlockSpec((32, 1, 16, 256), lambda h: (0, h, 0, 5)),
            pl.BlockSpec((2048, 128), lambda h: (0, h)),
            pl.BlockSpec((2048, 256), lambda h: (0, 2)),
            whole(128, 256),
            whole(128, 256),
            LOOSE,
        ],
        out_specs=[
            pl.BlockSpec((128, 128), lambda h: (0, h)),
            whole(128, 256),
            pl.BlockSpec((2048, 256), lambda h: (0, h)),
            whole(128, 2048),
        ]
        + [whole(512, 640)] * 4
        + [whole(32, 2048)] * 4,
        out_shape=[
            jax.ShapeDtypeStruct((128, 512), bf16),
            jax.ShapeDtypeStruct((128, 256), bf16),
            jax.ShapeDtypeStruct((2048, 1024), bf16),
            jax.ShapeDtypeStruct((128, 2048), bf16),
        ]
        + [jax.ShapeDtypeStruct((512, 640), bf16)] * 4
        + [jax.ShapeDtypeStruct((32, 2048), bf16)] * 4,
        scratch_shapes=[
            pltpu.VMEM((2048, 512), f32),
            pltpu.VMEM((2048, 128), f32),
            pltpu.VMEM((4, 128, 128), f32),
            pltpu.VMEM((128, 2048), f32),
        ],
        compiler_params=pltpu.CompilerParams(vmem_limit_bytes=56 * MIB),
        cost_estimate=pl.CostEstimate(
            flops=8 * 10**9, bytes_accessed=30 * 10**6, transcendentals=0
        ),
        name="attend_back",
    )(
        place, *parts, attn_all, q, kv, prob, lat, by_head, attn_all, attn_all, cosine, sine, tie
    )


def expert_kernel(place, far, spread, whole_w, d_far, d_hidden, hidden, out, weight, sem):
    @pl.when(pl.program_id(0) == 0)
    def _():
        copy = pltpu.make_async_copy(whole_w, weight, sem)
        copy.start()
        copy.wait()

    expert = 2 * place[0] + place[2]
    raw = dot_nn(far[...], weight[:, :896])
    d_weighted = dot_nn(spread[:, :2048], weight[:, 896:])
    rows = raw.shape[0]
    logits = raw[:, 880:888]
    power = jnp.exp(logits - jnp.max(logits, axis=1, keepdims=True))
    router = power / jnp.sum(power, axis=1, keepdims=True)
    is_mine = lax.broadcasted_iota(jnp.int32, (rows, 8), 1) == expert
    chosen = spread[:, 2048:2176][:, 66:74].astype(f32)
    gate = jnp.sum(jnp.where(is_mine, router * chosen, 0.0), axis=1, keepdims=True)
    routed = lax.broadcasted_iota(jnp.int32, (rows, 440), 1) < 352
    gate = jnp.where(routed, gate, 1.0)
    low, upper = raw[:, :440], raw[:, 440:880]
    sigma = 1.0 / (1.0 + jnp.exp(-low))
    silu = low * sigma
    slope = sigma + silu * (1.0 - sigma)
    act = silu * upper
    weighted = (gate * act).astype(bf16)
    d_gate = jnp.sum(jnp.where(routed, d_weighted * act, 0.0), axis=1, keepdims=True)
    d_act = d_weighted * gate
    d_up = jnp.concatenate(
        [d_act * upper * slope, d_act * silu, jnp.zeros((rows, 16), f32)], axis=1
    ).astype(bf16)
    d_hidden[...] = d_up
    hidden[...] = jnp.concatenate([weighted, jnp.zeros((rows, 72), bf16)], axis=1)
    d_far[:, :2048] = dot_nt(d_up, weight[:, :896]).astype(bf16)
    lane = lax.broadcasted_iota(jnp.int32, (rows, 128), 1)
    d_far[:, 2048:] = jnp.where(lane == expert + 66, d_gate, 0.0).astype(bf16)
    out[...] = dot_nt(weighted, weight[:, 896:]).astype(bf16)


def run_expert(place, far, spread, weight):
    rows = 256
    by_rows = lambda columns: pl.BlockSpec((rows, columns), lambda i: (i, 0))
    return pl.pallas_call(
        expert_kernel,
        grid=(512 // rows,),
        in_specs=[SCALARS, by_rows(2048), by_rows(2176), LOOSE],
        out_specs=[by_rows(2176), by_rows(896), by_rows(512), by_rows(2048)],
        out_shape=[
            jax.ShapeDtypeStruct((512, 2176), bf16),
            jax.ShapeDtypeStruct((512, 896), bf16),
            jax.ShapeDtypeStruct((512, 512), bf16),
            jax.ShapeDtypeStruct((512, 2048), bf16),
        ],
        scratch_shapes=[pltpu.VMEM((2048, 1336), bf16), pltpu.SemaphoreType.DMA],
        compiler_params=pltpu.CompilerParams(vmem_limit_bytes=48 * MIB),
        cost_estimate=pl.CostEstimate(
            flops=6 * 10**9, bytes_accessed=18 * 10**6, transcendentals=2**18
        ),
        name="expert",
    )(place, far, spread, weight)


def expert_grad_kernel(x0, x1, y0, y1, d0, d1, h0, h1, t1, t2, t3, out):
    out[:, :896] = (dot_tn(x0[...], d0[...]) + dot_tn(x1[...], d1[...])).astype(bf16)
    down = dot_tn(y0[...], h0[...]) + dot_tn(y1[...], h1[...])
    out[:, 896:] = down[:, :440].astype(bf16)


def expert_grad(fars, spreads, d_hiddens, hiddens, tie):
    block = 512
    columns = pl.BlockSpec((512, block), lambda i: (0, i))
    return pl.pallas_call(
        expert_grad_kernel,
        grid=(2048 // block,),
        in_specs=[columns] * 4 + [whole(512, 896)] * 2 + [whole(512, 512)] * 2 + [LOOSE] * 3,
        out_specs=pl.BlockSpec((block, 1336), lambda i: (i, 0)),
        out_shape=jax.ShapeDtypeStruct((2048, 1336), bf16),
        compiler_params=pltpu.CompilerParams(vmem_limit_bytes=48 * MIB),
        cost_estimate=pl.CostEstimate(
            flops=6 * 10**9, bytes_accessed=18 * 10**6, transcendentals=0
        ),
        name="expert_grad",
    )(*fars, *spreads, *d_hiddens, *hiddens, *tie)


def attn_grad_kernel(normed, d_q, d_rot, d_branch, attended, lat, d_exp, *rest):
    out, g_exp = rest[-2:]
    step = pl.program_id(0)

    @pl.when(step == 0)
    def _():
        g_exp[...] = dot_tn(lat[:, :RANK], d_exp[...]).astype(bf16)

    out[:, :512] = dot_tn(normed[...], d_q[...]).astype(bf16)
    out[:, 512:768] = dot_tn(normed[...], d_rot[...]).astype(bf16)
    out[:, 768:1280] = dot_tn(d_branch[...], attended[...]).astype(bf16)
    for d in range(8):
        for h in range(4):
            row = pl.multiple_of((step * 8 + d) * 16, 16)
            to = d * 64 + h * 16
            out[to : to + 16, 1280:] = g_exp[pl.ds(row, 16), h * 256 : h * 256 + 256]


def attn_grad(normed, d_q, d_rot, d_branch, attended, lat, d_exp, tie):
    columns = pl.BlockSpec((128, 512), lambda i: (0, i))
    return pl.pallas_call(
        attn_grad_kernel,
        grid=(4,),
        in_specs=[
            columns,
            whole(128, 512),
            whole(128, 256),
            columns,
            whole(128, 512),
            whole(2048, 640),
            whole(2048, 1024),
        ]
        + [LOOSE] * len(tie),
        out_specs=pl.BlockSpec((512, 1536), lambda i: (i, 0)),
        out_shape=jax.ShapeDtypeStruct((2048, 1536), bf16),
        scratch_shapes=[pltpu.VMEM((512, 1024), bf16)],
        compiler_params=pltpu.CompilerParams(vmem_limit_bytes=48 * MIB),
        cost_estimate=pl.CostEstimate(
            flops=4 * 10**9, bytes_accessed=15 * 10**6, transcendentals=0
        ),
        name="attn_grad",
    )(normed, d_q, d_rot, d_branch, attended, lat, d_exp, *tie)


def pair_kernel(place, mine, other, tie, p0, p1, p2, p3):
    is_first = place[2] == 0
    for s, out in enumerate((p0, p1, p2, p3)):
        to = lax.rem(place[0] + s, 4)
        a, b = mine[to], other[to]
        out[:64, :] = jnp.where(is_first, a, b)
        out[64:, :] = jnp.where(is_first, b, a)


def pair(place, mine, other, tie):
    vmem = pl.BlockSpec(memory_space=pltpu.VMEM)
    return pl.pallas_call(
        pair_kernel,
        in_specs=[SCALARS, vmem, vmem, LOOSE],
        out_specs=[vmem] * 4,
        out_shape=[jax.ShapeDtypeStruct((128, 1336), bf16)] * 4,
        cost_estimate=pl.CostEstimate(flops=10**6, bytes_accessed=3 * 10**6, transcendentals=0),
        name="pair",
    )(place, mine, other, tie)


def turn_kernel(place, value, tie, out):
    for s in range(4):
        row = pl.multiple_of(lax.rem(place[3] - s + 4, 4) * 32, 32)
        out[s * 32 : s * 32 + 32, :] = value[pl.ds(row, 32), :]


def turn(place, value, tie):
    vmem = pl.BlockSpec(memory_space=pltpu.VMEM)
    return pl.pallas_call(
        turn_kernel,
        in_specs=[SCALARS, vmem, LOOSE],
        out_specs=vmem,
        out_shape=jax.ShapeDtypeStruct(value.shape, bf16),
        cost_estimate=pl.CostEstimate(flops=10**6, bytes_accessed=10**6, transcendentals=0),
        name="turn",
    )(place, value, tie)


def out_parts_kernel(mine, other, middle, t1, t2, t3, p0, p1, p2, p3):
    for s, out in enumerate((p0, p1, p2, p3)):
        rows = slice(s * 128, s * 128 + 128)
        total = mine[rows, :].astype(f32) + other[rows, :].astype(f32)
        out[...] = total.astype(bf16)
        if s == 0:
            for b in range(16):
                at = far_block(b) * 128
                out[:32, at : at + 128] = (
                    total[:32, at : at + 128] + middle[:, b * 128 : b * 128 + 128]
                ).astype(bf16)


def out_parts(mine, other, middle, tie):
    vmem = pl.BlockSpec(memory_space=pltpu.VMEM)
    return pl.pallas_call(
        out_parts_kernel,
        in_specs=[vmem] * 3 + [LOOSE] * 3,
        out_specs=[vmem] * 4,
        out_shape=[jax.ShapeDtypeStruct((128, 2048), bf16)] * 4,
        compiler_params=pltpu.CompilerParams(vmem_limit_bytes=32 * MIB),
        cost_estimate=pl.CostEstimate(flops=10**6, bytes_accessed=6 * 10**6, transcendentals=0),
        name="out_parts",
    )(mine, other, middle, *tie)


def out_rows_kernel(place, p0, p1, p2, p3, out):
    for s in range(4):
        rows = slice(s * 32, s * 32 + 32)
        row = pl.multiple_of(lax.rem(place[3] - s + 4, 4) * 32, 32)
        total = p0[rows, :].astype(f32)
        for part in (p1, p2, p3):
            total = total + part[rows, :].astype(f32)
        for b in range(16):
            at = far_block(b) * 128
            out[pl.ds(row, 32), b * 128 : b * 128 + 128] = total[:, at : at + 128].astype(bf16)


def out_rows(place, parts):
    vmem = pl.BlockSpec(memory_space=pltpu.VMEM)
    return pl.pallas_call(
        out_rows_kernel,
        in_specs=[SCALARS] + [vmem] * 4,
        out_specs=vmem,
        out_shape=jax.ShapeDtypeStruct((128, 2048), bf16),
        cost_estimate=pl.CostEstimate(flops=10**6, bytes_accessed=3 * 10**6, transcendentals=0),
        name="out_rows",
    )(place, *parts)


def cut_kernel(place, value, tie, p0, p1, p2, p3):
    for s, out in enumerate((p0, p1, p2, p3)):
        row = pl.multiple_of(lax.rem(place[0] + s, 4) * 128, 128)
        out[...] = value[pl.ds(row, 128), :]


def cut(place, value, tie):
    vmem = pl.BlockSpec(memory_space=pltpu.VMEM)
    return pl.pallas_call(
        cut_kernel,
        in_specs=[SCALARS, vmem, LOOSE],
        out_specs=[vmem] * 4,
        out_shape=[jax.ShapeDtypeStruct((128, 1336), bf16)] * 4,
        cost_estimate=pl.CostEstimate(flops=10**6, bytes_accessed=3 * 10**6, transcendentals=0),
        name="cut",
    )(place, value, tie)


def by_core_kernel(place, p0, p1, p2, p3, mine, other):
    is_first = place[2] == 0
    for s, part in enumerate((p0, p1, p2, p3)):
        at = lax.rem(place[0] - s + 4, 4)
        low, high = part[:64, :], part[64:, :]
        mine[at] = jnp.where(is_first, low, high)
        other[at] = jnp.where(is_first, high, low)


def by_core(place, parts):
    vmem = pl.BlockSpec(memory_space=pltpu.VMEM)
    return pl.pallas_call(
        by_core_kernel,
        in_specs=[SCALARS] + [vmem] * 4,
        out_specs=[vmem] * 2,
        out_shape=[jax.ShapeDtypeStruct((4, 64, 1336), bf16)] * 2,
        cost_estimate=pl.CostEstimate(flops=10**6, bytes_accessed=3 * 10**6, transcendentals=0),
        name="by_core",
    )(place, *parts)


def unpack_kernel(place, mine, other, expert_in, expert_out, shared_in, shared_out):
    is_first = place[2] == 0
    ins, outs, downs = [], [], []
    for x in range(4):
        for core in range(2):
            a, b = (mine[x], other[x]) if core == 0 else (other[x], mine[x])
            value = jnp.where(is_first, a, b).astype(f32)
            expert = 2 * x + core
            expert_in[:, expert, 0, :] = value[:, :352]
            expert_in[:, expert, 1, :] = value[:, 440:792]
            expert_out[:, expert, :] = value[:, 896:1248]
            ins.append(value[:, 352:440])
            outs.append(value[:, 792:880])
            downs.append(value[:, 1248:])
    shared_in[:, 0, :] = jnp.concatenate(ins, axis=1)
    shared_in[:, 1, :] = jnp.concatenate(outs, axis=1)
    shared_out[...] = jnp.concatenate(downs, axis=1)


def unpack(place, mine, other):
    vmem = pl.BlockSpec(memory_space=pltpu.VMEM)
    return pl.pallas_call(
        unpack_kernel,
        in_specs=[SCALARS, vmem, vmem],
        out_specs=[vmem] * 4,
        out_shape=[
            jax.ShapeDtypeStruct((64, 8, 2, 352), f32),
            jax.ShapeDtypeStruct((64, 8, 352), f32),
            jax.ShapeDtypeStruct((64, 2, 704), f32),
            jax.ShapeDtypeStruct((64, 704), f32),
        ],
        compiler_params=pltpu.CompilerParams(vmem_limit_bytes=32 * MIB),
        cost_estimate=pl.CostEstimate(flops=10**6, bytes_accessed=6 * 10**6, transcendentals=0),
        name="unpack",
    )(place, mine, other)


def finish_kernel(total, *rest):
    query, output, expand = rest[-3:]
    value = total[...].astype(f32)
    query[...] = jnp.concatenate(
        [
            p
            for h in range(4)
            for p in (
                value[:, h * 128 : h * 128 + 128],
                value[:, 512 + h * 64 : 576 + h * 64],
            )
        ],
        axis=1,
    )
    output[...] = value[:, 768:1280]
    for h in range(4):
        expand[:, h * 256 : h * 256 + 256] = value[h * 16 : h * 16 + 16, 1280:]


def finish(total, tie):
    vmem = pl.BlockSpec(memory_space=pltpu.VMEM)
    return pl.pallas_call(
        finish_kernel,
        in_specs=[vmem] + [LOOSE] * len(tie),
        out_specs=[vmem] * 3,
        out_shape=[
            jax.ShapeDtypeStruct((64, 768), f32),
            jax.ShapeDtypeStruct((64, 512), f32),
            jax.ShapeDtypeStruct((16, 1024), f32),
        ],
        cost_estimate=pl.CostEstimate(flops=10**6, bytes_accessed=10**6, transcendentals=0),
        name="finish",
    )(total, *tie)


def on_device(
    tokens,
    segment,
    routes,
    cotangent,
    gain_attn,
    w_query,
    w_compress,
    gain_latent,
    w_expand,
    w_output,
    gain_ffn,
    w_router,
    w_expert_in,
    w_expert_out,
    w_shared_in,
    w_shared_out,
):
    xi, zi, ci, yi = (lax.axis_index(a) for a in ("x", "z", "c", "y"))
    place = jnp.stack([xi, zi, ci, yi]).astype(jnp.int32)
    is_first = ci == 0
    heads = 4
    dim = 2048

    def enter(value):
        mine, other = pick(value, ci, 0), shift(pick(value, 1 - ci, 0), "c", 1)
        return jnp.concatenate(
            [jnp.where(is_first, mine, other), jnp.where(is_first, other, mine)], axis=0
        )

    def leave(value):
        halves = value.reshape((2, 64) + value.shape[1:])
        mine, other = pick(halves, ci, 0), shift(pick(halves, 1 - ci, 0), "c", 1)
        return jnp.stack([jnp.where(is_first, mine, other), jnp.where(is_first, other, mine)])

    small = jnp.concatenate(
        [
            w_compress,
            gain_attn[:, None],
            gain_ffn[:, None],
            w_router,
            jnp.pad(gain_latent, (0, 48))[:, None],
            jnp.zeros((64, 53), bf16),
        ],
        axis=1,
    )
    small_mine = jnp.concatenate(gather_near(jnp.concatenate(gather_near(small, "x")), "z"))
    small_other = shift(small_mine, "c", 1)

    by_head = w_query.reshape(64, heads, NOPE + ROPE)
    attn_all = lax.all_gather(
        jnp.concatenate(
            [
                by_head[:, :, :NOPE].reshape(64, 512),
                by_head[:, :, NOPE:].reshape(64, 256),
                w_output,
                w_expand.reshape(16, heads, 256).transpose(1, 0, 2).reshape(64, 256),
            ],
            axis=1,
        ),
        ("x", "z", "c"),
        axis=0,
        tiled=True,
    )

    packed_w = jnp.concatenate(
        [
            w_expert_in[:, :, 0],
            w_shared_in[:, 0].reshape(64, 8, 88),
            w_expert_in[:, :, 1],
            w_shared_in[:, 1].reshape(64, 8, 88),
            jnp.broadcast_to(w_router[:, None, :], (64, 8, 8)),
            jnp.zeros((64, 8, 8), bf16),
            w_expert_out,
            w_shared_out.reshape(64, 8, 88),
        ],
        axis=-1,
    )
    packed_w = packed_w.transpose(1, 0, 2).reshape(4, 2, 64, 1336)
    mine_w, other_w = pick(packed_w, ci, 1), shift(pick(packed_w, 1 - ci, 1), "c", 1)
    mine_w, other_w = mine_w.reshape(4, 64, 1336), other_w.reshape(4, 64, 1336)
    tok = enter(tokens)
    chosen = jnp.sum(
        (routes[..., None] == jnp.arange(EXPERTS, dtype=jnp.int32)).astype(f32), axis=2
    )
    spread = jnp.concatenate(
        [
            to_far(cotangent.reshape(128, dim)),
            jnp.zeros((128, 66), bf16),
            chosen.reshape(128, 8).astype(bf16),
            jnp.zeros((128, 54), bf16),
        ],
        axis=1,
    )
    spread_here = enter(spread.reshape(2, 64, 2176))

    position = (xi * 4 + zi) * 128 + jnp.arange(128, dtype=jnp.int32)
    segment_row = pick(segment, ci, 0)
    blocks = jnp.stack(
        [lax.rem(xi - sx + 4, 4) * 4 + lax.rem(zi - sz + 4, 4) for sx in range(4) for sz in range(4)]
    )
    segment_near = segment_row.reshape(16, 128)[blocks].reshape(2048)
    key_place = (blocks[:, None] * 128 + jnp.arange(128, dtype=jnp.int32)[None, :]).reshape(2048)
    where_k = jnp.stack([key_place, segment_near])
    where_q = jnp.stack(
        [position, lax.dynamic_slice_in_dim(segment_row, (xi * 4 + zi) * 128, 128)], axis=1
    )
    lane = jnp.arange(256)[None, :]
    freq = jnp.exp((lane % 32).astype(f32) * (-jnp.log(10000.0) / 32))
    angle = position.astype(f32)[:, None] * freq
    cosine = jnp.cos(angle)
    sine = jnp.where(lane % 64 < 32, 1.0, -1.0) * jnp.sin(angle)

    normed, packed, compressed, weight, gains = front(
        place, tok, small_mine, small_other, cosine, sine
    )
    pair_w = pair(place, mine_w, other_w, small)
    pair_w = [pair_w[0]] + [shift(pair_w[s], "x", s) for s in range(1, 4)]
    expert_w = jnp.zeros((4, 128, 1336), bf16)
    for s in range(4):
        expert_w = lax.dynamic_update_index_in_dim(
            expert_w, pair_w[s], lax.rem(xi - s + 4, 4), 0
        )
    ffn_all = lax.all_gather(expert_w.reshape(512, 1336), "z", axis=0, tiled=True)
    latents = gather_near(jnp.concatenate(gather_near(packed, "z"), axis=0), "x")
    spread = turn(place, spread_here, latents[1])
    spread = jnp.concatenate(gather_near(spread, "x"), axis=0)
    spread_other = shift(spread, "c", 1)
    prob, kv, attended, latent_all, query, *branch = attend(
        place, normed, latents, attn_all, cosine, sine, where_q, where_k
    )
    branch = [branch[0]] + [shift(branch[s], "y", s) for s in range(1, 4)]
    middle, far = run_middle(place, branch, tok, gains, spread)

    far = jnp.concatenate(gather_near(jnp.concatenate(gather_near(far, "y")), "x"))
    far_other = shift(far, "c", 1)
    d_far, d_hidden, hidden, out_far = run_expert(place, far, spread, ffn_all)
    d_far2, d_hidden2, hidden2, out_far2 = run_expert(place, far_other, spread_other, ffn_all)

    d_far = (d_far.astype(f32) + shift(d_far2, "c", 1).astype(f32)).astype(bf16)
    d_far = [d_far[s * 128 : s * 128 + 128] for s in range(4)]
    d_far = [d_far[0]] + [shift(d_far[s], "x", -s) for s in range(1, 4)]
    tie = d_far[1:]
    d_far = sum(p.astype(f32) for p in d_far).astype(bf16)
    d_far = [d_far[s * 32 : s * 32 + 32] for s in range(4)]
    d_far = [d_far[0]] + [shift(d_far[s], "y", -s) for s in range(1, 4)]
    out_far = out_parts(out_far, shift(out_far2, "c", 1), middle, tie)
    d_mid, d_low, small_a = middle_back(
        place, d_far, spread_here, middle, gains, weight, out_far[0]
    )
    out_far = [out_far[0]] + [shift(out_far[s], "x", -s) for s in range(1, 4)]
    mixed = out_rows(place, out_far)
    mixed = [mixed] + [shift(mixed, "y", s) for s in range(1, 4)]
    d_low = gather_near(d_low, "y")

    grad_ffn = expert_grad(
        (far, far_other), (spread, spread_other), (d_hidden, d_hidden2), (hidden, hidden2), tie
    )
    grad_ffn = lax.psum_scatter(grad_ffn, "z", scatter_dimension=0, tiled=True)
    d_q, d_rot, d_expanded, d_branch, *rest = attend_back(
        place, d_low, query, kv, prob, latent_all, attn_all, cosine, sine, mixed[0]
    )
    terms = [rest[0]] + [shift(rest[s], "x", -s) for s in range(1, 4)]
    tie = terms[1:] + mixed[1:]
    terms = sum(p.astype(f32) for p in terms).astype(bf16)
    terms = [terms[s * 128 : s * 128 + 128] for s in range(4)]
    terms = [terms[0]] + [shift(terms[s], "z", -s) for s in range(1, 4)]
    late = terms[1]
    terms = sum(p.astype(f32) for p in terms).astype(bf16).reshape(4, 32, 640)
    terms = [pick(terms, lax.rem(yi + s, 4), 0) for s in range(4)]
    terms = [terms[0]] + [shift(terms[s], "y", s) for s in range(1, 4)]
    d_queries = [rest[4]] + [shift(rest[4 + s], "y", s) for s in range(1, 4)]
    grad_ffn = cut(place, grad_ffn, late)
    grad_ffn = [grad_ffn[0]] + [shift(grad_ffn[s], "x", s) for s in range(1, 4)]
    mine_g, other_g = by_core(place, grad_ffn)
    other_g = shift(other_g, "c", 1)
    d_comp, small_b = latent_back(place, terms, compressed, gains, cosine, sine, mine_g)
    g_expert_in, g_expert_out, g_shared_in, g_shared_out = unpack(place, mine_g, other_g)

    grad_rows, small_c = token_back(place, d_comp, d_queries, tok, gains, weight, d_mid)
    grad_rows = leave(gather_at(grad_rows, "y").reshape(128, dim))
    mixed = [m.astype(f32) for m in mixed]
    mixed = leave(((mixed[0] + mixed[2]) + (mixed[1] + mixed[3])).astype(bf16))

    def fsdp_sum(mine, other, cuts):
        value = (mine.astype(f32) + shift(other, "c", 1).astype(f32)).astype(bf16)
        value = value.reshape(4, 4, 64, -1)
        done = []
        for start, stop, first, second in cuts:
            part = sum_at(value[..., start:stop], first, 0 if first == "x" else 1).astype(bf16)
            done.append(sum_at(part, second, 0))
        return done

    g_attn = attn_grad(normed, d_q, d_rot, d_branch, attended, latent_all, d_expanded, tie)
    g_attn = lax.psum_scatter(g_attn, ("x", "z", "c"), scatter_dimension=0, tiled=True)
    g_mine, g_other = compress_grad(
        place,
        gather_near(d_comp, "y"),
        normed,
        (small_a, small_b, small_c),
        (g_expert_in, g_expert_out, g_shared_in, g_shared_out),
    )
    (g_small,) = fsdp_sum(g_mine, g_other, ((0, 256, "x", "z"),))
    g_small = g_small.astype(bf16)
    g_parts = gather_near(g_small, "y")
    g_query, g_output, g_expand = finish(g_attn, g_parts[1:])
    g_small = jnp.zeros((4, 64, 256), bf16)
    for s in range(4):
        g_small = lax.dynamic_update_index_in_dim(g_small, g_parts[s], lax.rem(yi - s + 4, 4), 0)
    g_small = g_small.astype(f32)
    g_compress = jnp.concatenate(
        [g_small[i, :, :128] for i in range(4)] + [g_small[0, :, 128:192]], axis=1
    )
    g_small = jnp.sum(g_small[:, :, 192:], axis=0)

    return (
        mixed,
        grad_rows,
        g_small[:, 0],
        g_query,
        g_compress,
        g_small[:16, 10],
        g_expand,
        g_output,
        g_small[:, 1],
        g_small[:, 2:10],
        g_expert_in,
        g_expert_out,
        g_shared_in,
        g_shared_out,
    )


def solution(mesh):
    fine = Mesh(mesh.devices.reshape(4, 4, 2, 4), ("x", "z", "c", "y"))
    rows = ("x", "z", "c")
    return jax.shard_map(
        on_device,
        mesh=fine,
        in_specs=(
            P(None, rows, None),
            P(),
            P(None, rows, None),
            P(None, rows, None),
            P(rows),
            P(rows, "y"),
            P(rows, None),
            P(rows),
            P(rows, "y"),
            P(rows, "y"),
            P(rows),
            P(rows, None),
            P(rows, None, None, "y"),
            P(rows, None, "y"),
            P(rows, None, "y"),
            P(rows, "y"),
        ),
        out_specs=(
            P(None, rows, None),
            P(None, rows, None),
            P(rows),
            P(rows, "y"),
            P(rows, None),
            P(rows),
            P(rows, "y"),
            P(rows, "y"),
            P(rows),
            P(rows, None),
            P(rows, None, None, "y"),
            P(rows, None, "y"),
            P(rows, None, "y"),
            P(rows, "y"),
        ),
        check_vma=False,
    )
```

```python
import jax
import jax.numpy as jnp
from jax import lax
from jax.experimental import pallas as pl
from jax.experimental.pallas import tpu as pltpu
from jax.sharding import Mesh
from jax.sharding import PartitionSpec as P

NOPE = 128
ROPE = 64
VHEAD = 128
RANK = 512
EXPERTS = 8

epsilon = 1e-06
bf16 = jnp.bfloat16
f32 = jnp.float32


def rotate_parts(values, position, inverse):
    half = values.shape[-1] // 2
    freq = jnp.exp(jnp.arange(half, dtype=f32) * (-jnp.log(10000.0) / half))
    angle = position.astype(f32)[:, None] * freq[None, :]
    cosine = jnp.cos(angle)
    sine = jnp.sin(angle)
    if inverse:
        sine = -sine
    if values.ndim == 3:
        cosine = cosine[:, None, :]
        sine = sine[:, None, :]
    first = values[..., :half]
    second = values[..., half:]
    return jnp.concatenate(
        [first * cosine - second * sine, second * cosine + first * sine], axis=-1
    )


def norm_forward(values, gain):
    factor = lax.rsqrt(jnp.mean(values * values, axis=-1, keepdims=True) + epsilon)
    return (values * factor * gain, factor)


def norm_backward(values, factor, gain, grad):
    scaled = grad * gain
    d_values = factor * scaled - values * (factor * factor * factor) * jnp.mean(
        values * scaled, axis=-1, keepdims=True
    )
    d_gain = jnp.sum(grad * values * factor, axis=0)
    return (d_values, d_gain)


def shift(value, axis, step):
    count = lax.axis_size(axis)
    return lax.ppermute(value, axis, [(i, (i + step) % count) for i in range(count)])


def pick(value, place, at):
    return lax.dynamic_index_in_dim(value, place, at, keepdims=False)


def gather_near(value, axis):
    return [value] + [shift(value, axis, s) for s in range(1, lax.axis_size(axis))]


def place_at(parts, axis):
    count = lax.axis_size(axis)
    me = lax.axis_index(axis)
    whole = jnp.zeros((count,) + parts[0].shape, parts[0].dtype)
    for s in range(count):
        at = lax.rem(me - s + count, count)
        whole = lax.dynamic_update_index_in_dim(whole, parts[s], at, 0)
    return whole


def sum_ahead(parts, axis):
    total = parts[0].astype(f32)
    for s in range(1, len(parts)):
        total = total + shift(parts[s], axis, s).astype(f32)
    return total


def sum_at(value, axis, at):
    count = lax.axis_size(axis)
    me = lax.axis_index(axis)
    return sum_ahead([pick(value, lax.rem(me + s, count), at) for s in range(count)], axis)


def dot_nn(a, b):
    return jnp.dot(a, b, preferred_element_type=f32)


def dot_nt(a, b):
    return lax.dot_general(a, b, (((1,), (1,)), ((), ())), preferred_element_type=f32)


def dot_tn(a, b):
    return lax.dot_general(a, b, (((0,), (0,)), ((), ())), preferred_element_type=f32)


def whole(*shape):
    return pl.BlockSpec(shape, lambda *_: (0,) * len(shape))


def corner(value):
    lead = value.ndim - 2
    return pl.BlockSpec((1,) * lead + (16, 128), lambda *_: (0,) * value.ndim)


def without(kernel, count, first):
    def body(*refs):
        return kernel(*refs[:first], *refs[first + count :])

    return body


SCALARS = pl.BlockSpec(memory_space=pltpu.SMEM)
SCALE = (NOPE + ROPE) ** (-0.5)
MIB = 1024 * 1024


def like(*shape, dtype=bf16):
    return jax.ShapeDtypeStruct(shape, dtype)


def run(kernel, place, inputs, outs, after=(), scratch=(), size=40, flops=10**6):
    vmem = pl.BlockSpec(memory_space=pltpu.VMEM)
    lead = [] if place is None else [SCALARS]
    given = [] if place is None else [place]
    moved = sum(v.size * v.dtype.itemsize for v in list(inputs) + list(outs))
    return pl.pallas_call(
        without(kernel, len(after), len(lead) + len(inputs)),
        grid=(1,) if after else (),
        in_specs=lead + [vmem] * len(inputs) + [corner(v) for v in after],
        out_specs=[vmem] * len(outs),
        out_shape=list(outs),
        scratch_shapes=list(scratch),
        compiler_params=pltpu.CompilerParams(vmem_limit_bytes=size * MIB),
        cost_estimate=pl.CostEstimate(flops=flops, bytes_accessed=moved, transcendentals=0),
        name=kernel.__name__.removesuffix("_kernel"),
    )(*given, *inputs, *after)


def enter_kernel(place, tokens, cotangent, routes, tok0, tok1, spread0, spread1):
    for side, tok, spread in ((place[2], tok0, spread0), (1 - place[2], tok1, spread1)):
        tok[...] = tokens[side]
        spread[:, :2048] = cotangent[side]
        named = routes[side]
        lane = lax.broadcasted_iota(jnp.int32, (64, 128), 1) - 66
        chosen = named[:, 0:1] == lane
        for k in range(1, named.shape[1]):
            chosen = chosen | (named[:, k : k + 1] == lane)
        spread[:, 2048:] = chosen.astype(f32).astype(bf16)


def front_kernel(
    place, tok0, tok1, mine, other, cosine, sine,
    normed, packed, compressed, weight, gains, tok,
):
    is_first = place[2] == 0
    tok[:64, :] = jnp.where(is_first, tok0[...], tok1[...])
    tok[64:, :] = jnp.where(is_first, tok1[...], tok0[...])
    for sx in range(4):
        for sz in range(4):
            block = lax.rem(place[0] - sx + 4, 4) * 4 + lax.rem(place[1] - sz + 4, 4)
            for part, core in ((mine, place[2]), (other, 1 - place[2])):
                row = pl.multiple_of(block * 128 + core * 64, 64)
                src = (sx * 4 + sz) * 64
                weight[pl.ds(row, 64), :] = part[src : src + 64, :]
    turned = weight[:, 512:640].astype(f32).T
    gains[0:2, :] = turned[64:66, :]
    latent_gain = jnp.concatenate(
        [turned[74:75, 64 * i : 64 * i + 16] for i in range(32)], axis=1
    )
    gains[2:3, :RANK] = latent_gain
    values = tok[...].astype(f32)
    factor = lax.rsqrt(jnp.mean(values * values, axis=1, keepdims=True) + epsilon)
    low = (values * factor * turned[64:65, :]).astype(bf16)
    normed[...] = low
    raw = dot_nn(low, weight[:, :576])
    compressed[...] = raw
    main = raw[:, :RANK]
    factor = lax.rsqrt(jnp.mean(main * main, axis=1, keepdims=True) + epsilon)
    latent = (main * factor * latent_gain).astype(bf16)
    first, second = raw[:, RANK : RANK + 32], raw[:, RANK + 32 :]
    cos, sin = cosine[:, :32], sine[:, :32]
    rot = jnp.concatenate([first * cos - second * sin, second * cos + first * sin], axis=1)
    packed[:, :RANK] = latent
    packed[:, RANK:] = jnp.concatenate([rot, jnp.zeros((128, 64), f32)], axis=1).astype(bf16)


def attend_kernel(
    place, normed, nope_w, rot_w, cosine, sine, l0, l1, l2, l3, expand, out_w,
    where_q, where_k, prob, kv, attended, lat, q, r0, r1, r2, r3, rot_q, total,
):
    head = pl.program_id(0)

    @pl.when(head == 0)
    def _():
        for sx in range(4):
            lat[sx * 512 : sx * 512 + 512, :] = (l0, l1, l2, l3)[sx][...]
        total[...] = jnp.zeros_like(total)
        rot = dot_nn(normed[...], rot_w[...])
        lane = lax.broadcasted_iota(jnp.int32, rot.shape, 1)
        partner = jnp.where(
            lane % 64 < 32, pltpu.roll(rot, 224, 1), pltpu.roll(rot, 32, 1)
        )
        rot = (rot * cosine[...] - partner * sine[...]).astype(bf16)
        for h in range(4):
            rot_q[h] = jnp.concatenate(
                [rot[:, 64 * h : 64 * h + 64], jnp.zeros((128, 64), bf16)], axis=1
            )

    nope = dot_nn(normed[...], nope_w[...]).astype(bf16)
    rot_h = rot_q[head]
    q[:, :128] = nope
    q[:, 128:] = rot_h
    expand_h = expand[...].reshape(RANK, 256)
    kv_h = dot_nn(lat[:, :RANK], expand_h).astype(bf16)
    kv[...] = kv_h
    score = (dot_nt(nope, kv_h[:, :128]) + dot_nt(rot_h, lat[:, RANK:])) * SCALE
    allowed = (where_q[:, 0:1] >= where_k[0:1, :]) & (where_q[:, 1:2] == where_k[1:2, :])
    score = jnp.where(allowed, score, -1e30)
    power = jnp.exp(score - jnp.max(score, axis=1, keepdims=True))
    prob_h = power / jnp.sum(power, axis=1, keepdims=True)
    prob[0] = prob_h
    attended_h = dot_nn(prob_h.astype(bf16), kv_h[:, 128:]).astype(bf16)
    attended[...] = attended_h
    total[...] += dot_nt(attended_h, out_w[...])

    @pl.when(head == 3)
    def _():
        for s, out in enumerate((r0, r1, r2, r3)):
            row = pl.multiple_of(lax.rem(place[3] + s, 4) * 32, 32)
            out[...] = total[pl.ds(row, 32), :].astype(bf16)


def attend(place, normed, parts, attn_all, cosine, sine, where_q, where_k):
    by_head = attn_all.reshape(32, 4, 16, 1536)
    return pl.pallas_call(
        attend_kernel,
        grid=(4,),
        in_specs=[
            SCALARS,
            whole(128, 2048),
            pl.BlockSpec((2048, 128), lambda h: (0, h)),
            pl.BlockSpec((2048, 256), lambda h: (0, 2)),
            whole(128, 256),
            whole(128, 256),
        ]
        + [whole(512, 640)] * 4
        + [
            pl.BlockSpec((32, 1, 16, 256), lambda h: (0, h, 0, 5)),
            pl.BlockSpec((2048, 128), lambda h: (0, 6 + h)),
            whole(128, 2),
            whole(2, 2048),
        ],
        out_specs=[
            pl.BlockSpec((1, 128, 2048), lambda h: (h, 0, 0)),
            pl.BlockSpec((2048, 256), lambda h: (0, h)),
            pl.BlockSpec((128, 128), lambda h: (0, h)),
            whole(2048, 640),
            pl.BlockSpec((128, 256), lambda h: (0, h)),
        ]
        + [whole(32, 2048)] * 4,
        out_shape=[
            jax.ShapeDtypeStruct((4, 128, 2048), f32),
            jax.ShapeDtypeStruct((2048, 1024), bf16),
            jax.ShapeDtypeStruct((128, 512), bf16),
            jax.ShapeDtypeStruct((2048, 640), bf16),
            jax.ShapeDtypeStruct((128, 1024), bf16),
        ]
        + [jax.ShapeDtypeStruct((32, 2048), bf16)] * 4,
        scratch_shapes=[
            pltpu.VMEM((4, 128, 128), bf16),
            pltpu.VMEM((128, 2048), f32),
        ],
        compiler_params=pltpu.CompilerParams(vmem_limit_bytes=48 * MIB),
        cost_estimate=pl.CostEstimate(
            flops=5 * 10**9, bytes_accessed=26 * 10**6, transcendentals=2**20
        ),
        name="attend",
    )(
        place, normed, attn_all, attn_all, cosine, sine, *parts, by_head, attn_all,
        where_q, where_k,
    )


def middle_kernel(place, r0, r1, r2, r3, tok, gains, middle, far):
    row = pl.multiple_of(place[3] * 32, 32)
    values = tok[pl.ds(row, 32), :].astype(f32)
    for part in (r0, r1, r2, r3):
        values = values + part[...].astype(f32)
    middle[...] = values
    factor = lax.rsqrt(jnp.mean(values * values, axis=1, keepdims=True) + epsilon)
    far[...] = (values * factor * gains[1:2, :]).astype(bf16)


def middle_back_kernel(
    place, a0, a1, a2, a3, spread, middle, gains, weight, d_mid, d_low, small
):
    row = pl.multiple_of(place[3] * 32, 32)
    total = a0[...].astype(f32)
    for part in (a1, a2, a3):
        total = total + part[...].astype(f32)
    d_normed = total[:, :2048]
    d_gate = total[:, 2048:]
    mine = spread[pl.ds(row, 32), :]
    d_out = mine[:, :2048].astype(f32)
    chosen = mine[:, 2048:].astype(f32)
    values = middle[...]
    gain = gains[1:2, :]
    factor = lax.rsqrt(jnp.mean(values * values, axis=1, keepdims=True) + epsilon)
    low = (values * factor * gain).astype(bf16)
    table = weight[:, 512:640]
    lane = lax.broadcasted_iota(jnp.int32, (32, 128), 1)
    is_expert = (lane >= 66) & (lane < 74)
    logits = jnp.where(is_expert, dot_nn(low, table), -1e30)
    power = jnp.exp(logits - jnp.max(logits, axis=1, keepdims=True))
    router = power / jnp.sum(power, axis=1, keepdims=True)
    d_chosen = d_gate * chosen
    d_logits = router * (d_chosen - jnp.sum(router * d_chosen, axis=1, keepdims=True))
    d_logits = d_logits.astype(bf16)
    d_normed = d_normed + dot_nt(d_logits, table)
    scaled = d_normed * gain
    d_norm = factor * scaled - values * (factor * factor * factor) * jnp.mean(
        values * scaled, axis=1, keepdims=True
    )
    d_values = d_out + d_norm
    d_mid[...] = d_values
    d_low[...] = d_values.astype(bf16)
    terms = (d_normed * values * factor).astype(bf16)
    small[...] = (
        dot_tn(low, d_logits) + dot_tn(terms, (lane == 65).astype(bf16))
    ).astype(bf16)


def latent_back_kernel(
    place, t0, t1, t2, t3, compressed, gains, cosine, sine, d_comp, small
):
    row = pl.multiple_of(place[3] * 32, 32)
    terms = t0[...].astype(f32)
    for part in (t1, t2, t3):
        terms = terms + part[...].astype(f32)
    main = compressed[pl.ds(row, 32), :][:, :RANK]
    factor = lax.rsqrt(jnp.mean(main * main, axis=1, keepdims=True) + epsilon)
    grad_main = terms[:, :RANK]
    scaled = grad_main * gains[2:3, :RANK]
    d_main = factor * scaled - main * (factor * factor * factor) * jnp.mean(
        main * scaled, axis=1, keepdims=True
    )
    first, second = terms[:, RANK : RANK + 32], terms[:, RANK + 32 : RANK + 64]
    cos, sin = cosine[pl.ds(row, 32), :][:, :32], sine[pl.ds(row, 32), :][:, :32]
    rot = jnp.concatenate([first * cos + second * sin, second * cos - first * sin], axis=1)
    d_comp[:, :RANK] = d_main.astype(bf16)
    d_comp[:, RANK:] = jnp.concatenate([rot, jnp.zeros((32, 64), f32)], axis=1).astype(bf16)
    latent_terms = grad_main * main * factor
    gap = jnp.zeros((32, 48), f32)
    latent_terms = jnp.concatenate(
        [p for i in range(32) for p in (latent_terms[:, 16 * i : 16 * i + 16], gap)], axis=1
    )
    lane = lax.broadcasted_iota(jnp.int32, (32, 128), 1)
    small[...] = dot_tn(latent_terms.astype(bf16), (lane == 74).astype(bf16)).astype(bf16)


def token_back_kernel(place, d_comp, q0, q1, q2, q3, tok, gains, weight, d_mid, grad, small):
    row = pl.multiple_of(place[3] * 32, 32)
    d_normed = dot_nt(d_comp[...], weight[:, :640])
    for part in (q0, q1, q2, q3):
        d_normed = d_normed + part[...].astype(f32)
    values = tok[pl.ds(row, 32), :].astype(f32)
    factor = lax.rsqrt(jnp.mean(values * values, axis=1, keepdims=True) + epsilon)
    scaled = d_normed * gains[0:1, :]
    d_norm = factor * scaled - values * (factor * factor * factor) * jnp.mean(
        values * scaled, axis=1, keepdims=True
    )
    grad[...] = (d_mid[...] + d_norm).astype(bf16)
    lane = lax.broadcasted_iota(jnp.int32, (32, 128), 1)
    small[...] = dot_tn(
        (d_normed * values * factor).astype(bf16), (lane == 64).astype(bf16)
    ).astype(bf16)


def compress_grad_kernel(place, c0, c1, c2, c3, normed, s0, s1, s2, mine, other, d_all):
    for s, part in enumerate((c0, c1, c2, c3)):
        row = pl.multiple_of(lax.rem(place[3] - s + 4, 4) * 32, 32)
        d_all[pl.ds(row, 32), :] = part[...]
    column = pl.multiple_of(place[3] * 128, 128)
    own = d_all[:, pl.ds(column, 128)]
    rot = d_all[:, RANK:]
    main = dot_tn(normed[...], own).astype(bf16)
    rest = dot_tn(normed[...], rot)
    for part in (s0, s1, s2):
        rest = rest + part[...].astype(f32)
    rest = rest.astype(bf16)
    is_first = place[2] == 0
    for b in range(16):
        for columns, value in ((slice(0, 128), main), (slice(128, 256), rest)):
            low, high = value[b * 128 : b * 128 + 64], value[b * 128 + 64 : b * 128 + 128]
            mine[b * 64 : b * 64 + 64, columns] = jnp.where(is_first, low, high)
            other[b * 64 : b * 64 + 64, columns] = jnp.where(is_first, high, low)


def attend_back_kernel(
    place, d0, d1, d2, d3, out_w, q, kv, prob, lat, expand, nope_w, rot_w, cosine, sine,
    d_q, d_rot, d_exp, d_branch, k0, k1, k2, k3, r0, r1, r2, r3,
    lat_sum, rot_sum, rot_q, total,
):
    head = pl.program_id(0)

    @pl.when(head == 0)
    def _():
        for s, part in enumerate((d0, d1, d2, d3)):
            row = pl.multiple_of(lax.rem(place[3] - s + 4, 4) * 32, 32)
            d_branch[pl.ds(row, 32), :] = part[...]
        lat_sum[...] = jnp.zeros_like(lat_sum)
        rot_sum[...] = jnp.zeros_like(rot_sum)
        total[...] = jnp.zeros_like(total)

    d_att = dot_nn(d_branch[...], out_w[...]).astype(bf16)
    prob_h = prob[0]
    d_prob = dot_nt(d_att, kv[:, 128:])
    row_sum = jnp.sum(prob_h * d_prob, axis=1, keepdims=True)
    d_score = (prob_h * (d_prob - row_sum)).astype(bf16)
    d_nope = (dot_nn(d_score, kv[:, :128]) * SCALE).astype(bf16)
    d_q[...] = d_nope
    rot_q[head] = dot_nn(d_score, lat[:, RANK:]) * SCALE
    d_key = dot_tn(d_score, q[...]) * SCALE
    d_val = dot_tn(prob_h.astype(bf16), d_att)
    d_exp_h = jnp.concatenate([d_key[:, :128], d_val], axis=1).astype(bf16)
    d_exp[...] = d_exp_h
    rot_sum[...] += d_key[:, 128:]
    lat_sum[...] += dot_nt(d_exp_h, expand[...].reshape(RANK, 256))
    total[...] += dot_nt(d_nope, nope_w[...])

    @pl.when(head == 3)
    def _():
        rot = jnp.concatenate([rot_q[h][:, :64] for h in range(4)], axis=1)
        lane = lax.broadcasted_iota(jnp.int32, rot.shape, 1)
        partner = jnp.where(
            lane % 64 < 32, pltpu.roll(rot, 224, 1), pltpu.roll(rot, 32, 1)
        )
        rot = (rot * cosine[...] + partner * sine[...]).astype(bf16)
        d_rot[...] = rot
        summed = total[...] + dot_nt(rot, rot_w[...])
        total[...] = summed
        for s, out in enumerate((r0, r1, r2, r3)):
            row = pl.multiple_of(lax.rem(place[3] + s, 4) * 32, 32)
            out[...] = total[pl.ds(row, 32), :].astype(bf16)
        for sx in range(4):
            rows = slice(sx * 512, sx * 512 + 512)
            out = (k0, k1, k2, k3)[sx]
            out[:, :RANK] = lat_sum[rows, :].astype(bf16)
            out[:, RANK:] = rot_sum[rows, :].astype(bf16)


def attend_back(place, parts, q, kv, prob, lat, attn_all, cosine, sine, after):
    by_head = attn_all.reshape(32, 4, 16, 1536)
    return pl.pallas_call(
        without(attend_back_kernel, len(after), 15),
        grid=(4,),
        in_specs=[SCALARS]
        + [whole(32, 2048)] * 4
        + [
            pl.BlockSpec((2048, 128), lambda h: (0, 6 + h)),
            pl.BlockSpec((128, 256), lambda h: (0, h)),
            pl.BlockSpec((2048, 256), lambda h: (0, h)),
            pl.BlockSpec((1, 128, 2048), lambda h: (h, 0, 0)),
            whole(2048, 640),
            pl.BlockSpec((32, 1, 16, 256), lambda h: (0, h, 0, 5)),
            pl.BlockSpec((2048, 128), lambda h: (0, h)),
            pl.BlockSpec((2048, 256), lambda h: (0, 2)),
            whole(128, 256),
            whole(128, 256),
        ]
        + [corner(v) for v in after],
        out_specs=[
            pl.BlockSpec((128, 128), lambda h: (0, h)),
            whole(128, 256),
            pl.BlockSpec((2048, 256), lambda h: (0, h)),
            whole(128, 2048),
        ]
        + [whole(512, 640)] * 4
        + [whole(32, 2048)] * 4,
        out_shape=[
            jax.ShapeDtypeStruct((128, 512), bf16),
            jax.ShapeDtypeStruct((128, 256), bf16),
            jax.ShapeDtypeStruct((2048, 1024), bf16),
            jax.ShapeDtypeStruct((128, 2048), bf16),
        ]
        + [jax.ShapeDtypeStruct((512, 640), bf16)] * 4
        + [jax.ShapeDtypeStruct((32, 2048), bf16)] * 4,
        scratch_shapes=[
            pltpu.VMEM((2048, 512), f32),
            pltpu.VMEM((2048, 128), f32),
            pltpu.VMEM((4, 128, 128), f32),
            pltpu.VMEM((128, 2048), f32),
        ],
        compiler_params=pltpu.CompilerParams(vmem_limit_bytes=56 * MIB),
        cost_estimate=pl.CostEstimate(
            flops=8 * 10**9, bytes_accessed=30 * 10**6, transcendentals=0
        ),
        name="attend_back",
    )(
        place, *parts, attn_all, q, kv, prob, lat, by_head, attn_all, attn_all, cosine, sine,
        *after,
    )


def expert_kernel(place, far, spread, weight, d_far, d_hidden, hidden, out):
    expert = 2 * place[1] + place[2]
    for part in range(2):
        at = slice(part * 256, part * 256 + 256)
        raw = dot_nn(far[at, :], weight[:, :896])
        d_weighted = dot_nn(spread[at, :2048], weight[:, 896:])
        rows = raw.shape[0]
        logits = raw[:, 880:888]
        power = jnp.exp(logits - jnp.max(logits, axis=1, keepdims=True))
        router = power / jnp.sum(power, axis=1, keepdims=True)
        is_mine = lax.broadcasted_iota(jnp.int32, (rows, 8), 1) == expert
        chosen = spread[at, 2048:2176][:, 66:74].astype(f32)
        gate = jnp.sum(jnp.where(is_mine, router * chosen, 0.0), axis=1, keepdims=True)
        routed = lax.broadcasted_iota(jnp.int32, (rows, 440), 1) < 352
        gate = jnp.where(routed, gate, 1.0)
        low, upper = raw[:, :440], raw[:, 440:880]
        sigma = 1.0 / (1.0 + jnp.exp(-low))
        silu = low * sigma
        slope = sigma + silu * (1.0 - sigma)
        act = silu * upper
        weighted = (gate * act).astype(bf16)
        d_gate = jnp.sum(jnp.where(routed, d_weighted * act, 0.0), axis=1, keepdims=True)
        d_act = d_weighted * gate
        d_up = jnp.concatenate(
            [d_act * upper * slope, d_act * silu, jnp.zeros((rows, 16), f32)], axis=1
        ).astype(bf16)
        d_hidden[at, :] = d_up
        hidden[at, :] = jnp.concatenate([weighted, jnp.zeros((rows, 72), bf16)], axis=1)
        d_far[at, :2048] = dot_nt(d_up, weight[:, :896]).astype(bf16)
        lane = lax.broadcasted_iota(jnp.int32, (rows, 128), 1)
        d_far[at, 2048:] = jnp.where(lane == expert + 66, d_gate, 0.0).astype(bf16)
        out[at, :] = dot_nt(weighted, weight[:, 896:]).astype(bf16)


def expert(place, far, spread, weight):
    return run(
        expert_kernel,
        place,
        [far, spread, weight],
        [like(512, 2176), like(512, 896), like(512, 512), like(512, 2048)],
        flops=6 * 10**9,
    )


def expert_grad_kernel(x0, x1, y0, y1, d0, d1, h0, h1, out):
    out[:, :896] = (dot_tn(x0[...], d0[...]) + dot_tn(x1[...], d1[...])).astype(bf16)
    down = dot_tn(y0[...], h0[...]) + dot_tn(y1[...], h1[...])
    out[:, 896:] = down[:, :440].astype(bf16)


def expert_grad(fars, spreads, d_hiddens, hiddens, after):
    columns = pl.BlockSpec((512, 512), lambda i: (0, i))
    return pl.pallas_call(
        without(expert_grad_kernel, len(after), 8),
        grid=(4,),
        in_specs=[columns] * 4
        + [whole(512, 896)] * 2
        + [whole(512, 512)] * 2
        + [corner(v) for v in after],
        out_specs=pl.BlockSpec((512, 1336), lambda i: (i, 0)),
        out_shape=like(2048, 1336),
        compiler_params=pltpu.CompilerParams(vmem_limit_bytes=40 * MIB),
        cost_estimate=pl.CostEstimate(
            flops=6 * 10**9, bytes_accessed=18 * 10**6, transcendentals=0
        ),
        name="expert_grad",
    )(*fars, *spreads, *d_hiddens, *hiddens, *after)


def attn_grad_kernel(normed, d_q, d_rot, d_branch, attended, lat, d_exp, out, g_exp):
    step = pl.program_id(0)

    @pl.when(step == 0)
    def _():
        g_exp[...] = dot_tn(lat[:, :RANK], d_exp[...]).astype(bf16)

    out[:, :512] = dot_tn(normed[...], d_q[...]).astype(bf16)
    out[:, 512:768] = dot_tn(normed[...], d_rot[...]).astype(bf16)
    out[:, 768:1280] = dot_tn(d_branch[...], attended[...]).astype(bf16)
    for d in range(8):
        for h in range(4):
            row = pl.multiple_of((step * 8 + d) * 16, 16)
            to = d * 64 + h * 16
            out[to : to + 16, 1280:] = g_exp[pl.ds(row, 16), h * 256 : h * 256 + 256]


def attn_grad(normed, d_q, d_rot, d_branch, attended, lat, d_exp, after):
    columns = pl.BlockSpec((128, 512), lambda i: (0, i))
    return pl.pallas_call(
        without(attn_grad_kernel, len(after), 7),
        grid=(4,),
        in_specs=[
            columns,
            whole(128, 512),
            whole(128, 256),
            columns,
            whole(128, 512),
            whole(2048, 640),
            whole(2048, 1024),
        ]
        + [corner(v) for v in after],
        out_specs=pl.BlockSpec((512, 1536), lambda i: (i, 0)),
        out_shape=jax.ShapeDtypeStruct((2048, 1536), bf16),
        scratch_shapes=[pltpu.VMEM((512, 1024), bf16)],
        compiler_params=pltpu.CompilerParams(vmem_limit_bytes=48 * MIB),
        cost_estimate=pl.CostEstimate(
            flops=4 * 10**9, bytes_accessed=15 * 10**6, transcendentals=0
        ),
        name="attn_grad",
    )(normed, d_q, d_rot, d_branch, attended, lat, d_exp, *after)


def pair_kernel(place, mine, other, p0, p1, p2, p3):
    is_first = place[2] == 0
    for s, out in enumerate((p0, p1, p2, p3)):
        to = lax.rem(place[1] + s, 4)
        a, b = mine[to], other[to]
        out[:64, :] = jnp.where(is_first, a, b)
        out[64:, :] = jnp.where(is_first, b, a)


def turn_kernel(place, mine, other, natural, out):
    is_first = place[2] == 0
    natural[:64, :] = jnp.where(is_first, mine[...], other[...])
    natural[64:, :] = jnp.where(is_first, other[...], mine[...])
    for s in range(4):
        row = pl.multiple_of(lax.rem(place[3] - s + 4, 4) * 32, 32)
        out[s * 32 : s * 32 + 32, :] = natural[pl.ds(row, 32), :]


def stack_kernel(p0, p1, p2, p3, out):
    rows = p0.shape[0]
    for s, part in enumerate((p0, p1, p2, p3)):
        out[s * rows : s * rows + rows, :] = part[...]


def add_split_kernel(mine, other, *outs):
    rows = outs[0].shape[0]
    for s, out in enumerate(outs):
        at = slice(s * rows, s * rows + rows)
        out[...] = (mine[at, :].astype(f32) + other[at, :].astype(f32)).astype(bf16)


def sum_split_kernel(v0, v1, v2, v3, *outs):
    rows = outs[0].shape[0]
    for s, out in enumerate(outs):
        at = slice(s * rows, s * rows + rows)
        total = v0[at, :].astype(f32)
        for part in (v1, v2, v3):
            total = total + part[at, :].astype(f32)
        out[...] = total.astype(bf16)


def row_sum_kernel(place, v0, v1, v2, v3, *outs):
    for s, out in enumerate(outs):
        rows = pl.ds(pl.multiple_of(lax.rem(place[3] + s, 4) * 32, 32), 32)
        total = v0[rows, :].astype(f32)
        for part in (v1, v2, v3):
            total = total + part[rows, :].astype(f32)
        out[...] = total.astype(bf16)


def out_rows_kernel(v0, v1, v2, v3, middle, out):
    total = v0[...].astype(f32)
    for part in (v1, v2, v3):
        total = total + part[...].astype(f32)
    out[...] = (middle[...] + total).astype(bf16)


def cut_kernel(place, value, p0, p1, p2, p3):
    for s, out in enumerate((p0, p1, p2, p3)):
        rows = pl.ds(pl.multiple_of(lax.rem(place[1] + s, 4) * 128, 128), 128)
        out[...] = value[rows, :]


def join_kernel(place, p0, p1, p2, p3, out):
    for s, part in enumerate((p0, p1, p2, p3)):
        rows = pl.ds(pl.multiple_of(lax.rem(place[1] - s + 4, 4) * 128, 128), 128)
        out[rows, :] = part[...]


def pack_attn_kernel(query, output, expand, out):
    value = query[...]
    out[:, :512] = jnp.concatenate([value[:, 192 * h : 192 * h + 128] for h in range(4)], axis=1)
    out[:, 512:768] = jnp.concatenate(
        [value[:, 192 * h + 128 : 192 * h + 192] for h in range(4)], axis=1
    )
    out[:, 768:1280] = output[...]
    for h in range(4):
        out[h * 16 : h * 16 + 16, 1280:] = expand[:, h * 256 : h * 256 + 256]


def by_core_kernel(place, p0, p1, p2, p3, mine, other):
    is_first = place[2] == 0
    for s, part in enumerate((p0, p1, p2, p3)):
        at = lax.rem(place[1] - s + 4, 4)
        low, high = part[:64, :], part[64:, :]
        mine[at] = jnp.where(is_first, low, high)
        other[at] = jnp.where(is_first, high, low)


def unpack_kernel(place, mine, other, expert_in, expert_out, shared_in, shared_out):
    is_first = place[2] == 0
    ins, outs, downs = [], [], []
    for x in range(4):
        for core in range(2):
            a, b = (mine[x], other[x]) if core == 0 else (other[x], mine[x])
            value = jnp.where(is_first, a, b).astype(f32)
            expert = 2 * x + core
            expert_in[:, expert, 0, :] = value[:, :352]
            expert_in[:, expert, 1, :] = value[:, 440:792]
            expert_out[:, expert, :] = value[:, 896:1248]
            ins.append(value[:, 352:440])
            outs.append(value[:, 792:880])
            downs.append(value[:, 1248:])
    shared_in[:, 0, :] = jnp.concatenate(ins, axis=1)
    shared_in[:, 1, :] = jnp.concatenate(outs, axis=1)
    shared_out[...] = jnp.concatenate(downs, axis=1)


def finish_kernel(total, query, output, expand):
    value = total[...].astype(f32)
    query[...] = jnp.concatenate(
        [
            p
            for h in range(4)
            for p in (
                value[:, h * 128 : h * 128 + 128],
                value[:, 512 + h * 64 : 576 + h * 64],
            )
        ],
        axis=1,
    )
    output[...] = value[:, 768:1280]
    for h in range(4):
        expand[:, h * 256 : h * 256 + 256] = value[h * 16 : h * 16 + 16, 1280:]


def on_device(
    tokens,
    segment,
    routes,
    cotangent,
    gain_attn,
    w_query,
    w_compress,
    gain_latent,
    w_expand,
    w_output,
    gain_ffn,
    w_router,
    w_expert_in,
    w_expert_out,
    w_shared_in,
    w_shared_out,
):
    xi, zi, ci, yi = (lax.axis_index(a) for a in ("x", "z", "c", "y"))
    place = jnp.stack([xi, zi, ci, yi]).astype(jnp.int32)
    is_first = ci == 0
    heads = 4
    dim = 2048

    def leave(value):
        halves = value.reshape((2, 64) + value.shape[1:])
        mine, other = pick(halves, ci, 0), shift(pick(halves, 1 - ci, 0), "c", 1)
        return jnp.stack([jnp.where(is_first, mine, other), jnp.where(is_first, other, mine)])

    small = jnp.concatenate(
        [
            w_compress,
            gain_attn[:, None],
            gain_ffn[:, None],
            w_router,
            jnp.pad(gain_latent, (0, 48))[:, None],
            jnp.zeros((64, 53), bf16),
        ],
        axis=1,
    )
    (small_z,) = run(stack_kernel, None, gather_near(small, "z"), [like(256, 640)])
    small_x = gather_near(small_z, "x")
    (small_mine,) = run(stack_kernel, None, small_x, [like(1024, 640)])
    small_other = shift(small_mine, "c", 1)

    packed_w = jnp.concatenate(
        [
            w_expert_in[:, :, 0],
            w_shared_in[:, 0].reshape(64, 8, 88),
            w_expert_in[:, :, 1],
            w_shared_in[:, 1].reshape(64, 8, 88),
            jnp.broadcast_to(w_router[:, None, :], (64, 8, 8)),
            jnp.zeros((64, 8, 8), bf16),
            w_expert_out,
            w_shared_out.reshape(64, 8, 88),
        ],
        axis=-1,
    )
    packed_w = packed_w.transpose(1, 0, 2).reshape(4, 2, 64, 1336)
    mine_w, other_w = pick(packed_w, ci, 1), shift(pick(packed_w, 1 - ci, 1), "c", 1)
    mine_w, other_w = mine_w.reshape(4, 64, 1336), other_w.reshape(4, 64, 1336)
    tok_mine, tok_send, spread_mine, spread_send = run(
        enter_kernel,
        place,
        [tokens, cotangent, routes],
        [like(64, 2048), like(64, 2048), like(64, 2176), like(64, 2176)],
    )
    tok_other = shift(tok_send, "c", 1)
    spread_other = shift(spread_send, "c", 1)

    position = (xi * 4 + zi) * 128 + jnp.arange(128, dtype=jnp.int32)
    segment_row = pick(segment, ci, 0)
    blocks = jnp.stack(
        [lax.rem(xi - sx + 4, 4) * 4 + lax.rem(zi - sz + 4, 4) for sx in range(4) for sz in range(4)]
    )
    segment_near = segment_row.reshape(16, 128)[blocks].reshape(2048)
    key_place = (blocks[:, None] * 128 + jnp.arange(128, dtype=jnp.int32)[None, :]).reshape(2048)
    where_k = jnp.stack([key_place, segment_near])
    where_q = jnp.stack(
        [position, lax.dynamic_slice_in_dim(segment_row, (xi * 4 + zi) * 128, 128)], axis=1
    )
    lane = jnp.arange(256)[None, :]
    freq = jnp.exp((lane % 32).astype(f32) * (-jnp.log(10000.0) / 32))
    angle = position.astype(f32)[:, None] * freq
    cosine = jnp.cos(angle)
    sine = jnp.where(lane % 64 < 32, 1.0, -1.0) * jnp.sin(angle)

    pair_w = run(pair_kernel, place, [mine_w, other_w], [like(128, 1336)] * 4)
    pair_w = [pair_w[0]] + [shift(pair_w[s], "z", s) for s in range(1, 4)]
    (attn_w,) = run(
        pack_attn_kernel,
        None,
        [w_query, w_output, w_expand],
        [like(64, 1536)],
        after=small_x[1:] + pair_w[1:],
    )
    (expert_w,) = run(join_kernel, place, pair_w, [like(512, 1336)], after=[attn_w])
    attn_all = lax.all_gather(attn_w, ("x", "z", "c"), axis=0, tiled=True)
    ffn_all = lax.all_gather(expert_w, "x", axis=0, tiled=True)

    normed, packed, compressed, weight, gains, tok = run(
        front_kernel,
        place,
        [tok_mine, tok_other, small_mine, small_other, cosine, sine],
        [
            like(128, 2048),
            like(128, 640),
            like(128, 576, dtype=f32),
            like(2048, 640),
            like(8, 2048, dtype=f32),
            like(128, 2048),
        ],
    )
    (latent_near,) = run(stack_kernel, None, gather_near(packed, "z"), [like(512, 640)])
    latents = gather_near(latent_near, "x")
    spread_here, spread = run(
        turn_kernel,
        place,
        [spread_mine, spread_other],
        [like(128, 2176)] * 2,
        after=latents[1:2],
    )
    spread = gather_near(spread, "z")
    prob, kv, attended, latent_all, query, *branch = attend(
        place, normed, latents, attn_all, cosine, sine, where_q, where_k
    )
    branch = [branch[0]] + [shift(branch[s], "y", s) for s in range(1, 4)]
    (spread,) = run(stack_kernel, None, spread, [like(512, 2176)], after=[attended])
    spread_other = shift(spread, "c", 1)
    middle, far = run(
        middle_kernel,
        place,
        [*branch, tok, gains],
        [like(32, 2048, dtype=f32), like(32, 2048)],
        after=[spread],
    )

    (far,) = run(stack_kernel, None, gather_near(far, "y"), [like(128, 2048)])
    (far,) = run(stack_kernel, None, gather_near(far, "z"), [like(512, 2048)])
    far_other = shift(far, "c", 1)
    d_far2, d_hidden2, hidden2, out_far2 = expert(place, far_other, spread_other, ffn_all)
    d_far, d_hidden, hidden, out_far = expert(place, far, spread, ffn_all)
    d_far = run(
        add_split_kernel, None, [d_far, shift(d_far2, "c", 1)], [like(128, 2176)] * 4
    )
    d_far = [d_far[0]] + [shift(d_far[s], "z", -s) for s in range(1, 4)]
    d_far = run(sum_split_kernel, None, d_far, [like(32, 2176)] * 4)
    grad_ffn = expert_grad(
        (far, far_other), (spread, spread_other), (d_hidden, d_hidden2), (hidden, hidden2), d_far[:1]
    )
    grad_ffn = lax.psum_scatter(grad_ffn, "x", scatter_dimension=0, tiled=True)
    d_far = [d_far[0]] + [shift(d_far[s], "y", -s) for s in range(1, 4)]
    d_mid, d_low, small_a = run(
        middle_back_kernel,
        place,
        [*d_far, spread_here, middle, gains, weight],
        [like(32, 2048, dtype=f32), like(32, 2048), like(2048, 128)],
    )
    out_far = run(
        add_split_kernel,
        None,
        [out_far, shift(out_far2, "c", 1)],
        [like(128, 2048)] * 4,
        after=d_far[:1],
    )
    out_far = [out_far[0]] + [shift(out_far[s], "z", -s) for s in range(1, 4)]
    d_low = gather_near(d_low, "y")

    d_q, d_rot, d_expanded, d_branch, *rest = attend_back(
        place, d_low, query, kv, prob, latent_all, attn_all, cosine, sine, out_far[1:]
    )
    terms = [rest[0]] + [shift(rest[s], "x", -s) for s in range(1, 4)]
    d_queries = [rest[4]] + [shift(rest[4 + s], "y", s) for s in range(1, 4)]
    grad_ffn = run(cut_kernel, place, [grad_ffn], [like(128, 1336)] * 4)
    grad_ffn = [grad_ffn[0]] + [shift(grad_ffn[s], "z", s) for s in range(1, 4)]
    terms = run(
        sum_split_kernel, None, terms, [like(128, 640)] * 4, after=grad_ffn[1:]
    )
    out_far = run(sum_split_kernel, None, out_far, [like(32, 2048)] * 4, after=terms[:1])
    out_far = [out_far[0]] + [shift(out_far[s], "y", -s) for s in range(1, 4)]
    mine_g, other_g = run(by_core_kernel, place, grad_ffn, [like(4, 64, 1336)] * 2)
    terms = [terms[0]] + [shift(terms[s], "z", -s) for s in range(1, 4)]
    terms = run(
        row_sum_kernel, place, terms, [like(32, 640)] * 4, after=out_far[1:] + [mine_g]
    )
    terms = [terms[0]] + [shift(terms[s], "y", s) for s in range(1, 4)]
    (mixed,) = run(out_rows_kernel, None, [*out_far, middle], [like(32, 2048)], after=terms[:1])
    mixed = gather_near(mixed, "y")

    d_comp, small_b = run(
        latent_back_kernel,
        place,
        [*terms, compressed, gains, cosine, sine],
        [like(32, 640), like(2048, 128)],
        after=mixed[1:],
    )
    g_expert_in, g_expert_out, g_shared_in, g_shared_out = run(
        unpack_kernel,
        place,
        [mine_g, shift(other_g, "c", 1)],
        [
            like(64, 8, 2, 352, dtype=f32),
            like(64, 8, 352, dtype=f32),
            like(64, 2, 704, dtype=f32),
            like(64, 704, dtype=f32),
        ],
    )
    grad_rows, small_c = run(
        token_back_kernel,
        place,
        [d_comp, *d_queries, tok, gains, weight, d_mid],
        [like(32, 2048), like(2048, 128)],
    )
    grad_rows = leave(place_at(gather_near(grad_rows, "y"), "y").reshape(128, dim))
    mixed = leave(place_at(mixed, "y").reshape(128, dim))

    def fsdp_sum(mine, other, cuts):
        value = (mine.astype(f32) + shift(other, "c", 1).astype(f32)).astype(bf16)
        value = value.reshape(4, 4, 64, -1)
        done = []
        for start, stop, first, second in cuts:
            part = sum_at(value[..., start:stop], first, 0 if first == "x" else 1).astype(bf16)
            done.append(sum_at(part, second, 0))
        return done

    g_attn = attn_grad(normed, d_q, d_rot, d_branch, attended, latent_all, d_expanded, [])
    g_attn = lax.psum_scatter(g_attn, ("x", "z", "c"), scatter_dimension=0, tiled=True)
    g_mine, g_other = run(
        compress_grad_kernel,
        place,
        [*gather_near(d_comp, "y"), normed, small_a, small_b, small_c],
        [like(1024, 256)] * 2,
        scratch=[pltpu.VMEM((128, 640), bf16)],
    )
    (g_small,) = fsdp_sum(g_mine, g_other, ((0, 256, "x", "z"),))
    g_small = g_small.astype(bf16)
    g_parts = gather_near(g_small, "y")
    g_query, g_output, g_expand = run(
        finish_kernel,
        None,
        [g_attn],
        [like(64, 768, dtype=f32), like(64, 512, dtype=f32), like(16, 1024, dtype=f32)],
        after=g_parts[1:] + [g_shared_out],
    )
    g_small = place_at(g_parts, "y")
    g_small = g_small.astype(f32)
    g_compress = jnp.concatenate(
        [g_small[i, :, :128] for i in range(4)] + [g_small[0, :, 128:192]], axis=1
    )
    g_small = jnp.sum(g_small[:, :, 192:], axis=0)

    return (
        mixed,
        grad_rows,
        g_small[:, 0],
        g_query,
        g_compress,
        g_small[:16, 10],
        g_expand,
        g_output,
        g_small[:, 1],
        g_small[:, 2:10],
        g_expert_in,
        g_expert_out,
        g_shared_in,
        g_shared_out,
    )


def solution(mesh):
    fine = Mesh(mesh.devices.reshape(4, 4, 2, 4), ("x", "z", "c", "y"))
    rows = ("x", "z", "c")
    return jax.shard_map(
        on_device,
        mesh=fine,
        in_specs=(
            P(None, rows, None),
            P(),
            P(None, rows, None),
            P(None, rows, None),
            P(rows),
            P(rows, "y"),
            P(rows, None),
            P(rows),
            P(rows, "y"),
            P(rows, "y"),
            P(rows),
            P(rows, None),
            P(rows, None, None, "y"),
            P(rows, None, "y"),
            P(rows, None, "y"),
            P(rows, "y"),
        ),
        out_specs=(
            P(None, rows, None),
            P(None, rows, None),
            P(rows),
            P(rows, "y"),
            P(rows, None),
            P(rows),
            P(rows, "y"),
            P(rows, "y"),
            P(rows),
            P(rows, None),
            P(rows, None, None, "y"),
            P(rows, None, "y"),
            P(rows, None, "y"),
            P(rows, "y"),
        ),
        check_vma=False,
    )
```

```python
import jax
import jax.numpy as jnp
from jax import lax
from jax.experimental import pallas as pl
from jax.experimental.pallas import tpu as pltpu
from jax.sharding import Mesh
from jax.sharding import PartitionSpec as P

NOPE = 128
ROPE = 64
VHEAD = 128
RANK = 512
EXPERTS = 8

epsilon = 1e-06
bf16 = jnp.bfloat16
f32 = jnp.float32


def rotate_parts(values, position, inverse):
    half = values.shape[-1] // 2
    freq = jnp.exp(jnp.arange(half, dtype=f32) * (-jnp.log(10000.0) / half))
    angle = position.astype(f32)[:, None] * freq[None, :]
    cosine = jnp.cos(angle)
    sine = jnp.sin(angle)
    if inverse:
        sine = -sine
    if values.ndim == 3:
        cosine = cosine[:, None, :]
        sine = sine[:, None, :]
    first = values[..., :half]
    second = values[..., half:]
    return jnp.concatenate(
        [first * cosine - second * sine, second * cosine + first * sine], axis=-1
    )


def norm_forward(values, gain):
    factor = lax.rsqrt(jnp.mean(values * values, axis=-1, keepdims=True) + epsilon)
    return (values * factor * gain, factor)


def norm_backward(values, factor, gain, grad):
    scaled = grad * gain
    d_values = factor * scaled - values * (factor * factor * factor) * jnp.mean(
        values * scaled, axis=-1, keepdims=True
    )
    d_gain = jnp.sum(grad * values * factor, axis=0)
    return (d_values, d_gain)


def shift(value, axis, step):
    count = lax.axis_size(axis)
    return lax.ppermute(value, axis, [(i, (i + step) % count) for i in range(count)])


def pick(value, place, at):
    return lax.dynamic_index_in_dim(value, place, at, keepdims=False)


def gather_near(value, axis):
    return [value] + [shift(value, axis, s) for s in range(1, lax.axis_size(axis))]


def place_at(parts, axis):
    count = lax.axis_size(axis)
    me = lax.axis_index(axis)
    whole = jnp.zeros((count,) + parts[0].shape, parts[0].dtype)
    for s in range(count):
        at = lax.rem(me - s + count, count)
        whole = lax.dynamic_update_index_in_dim(whole, parts[s], at, 0)
    return whole


def sum_ahead(parts, axis):
    total = parts[0].astype(f32)
    for s in range(1, len(parts)):
        total = total + shift(parts[s], axis, s).astype(f32)
    return total


def sum_at(value, axis, at):
    count = lax.axis_size(axis)
    me = lax.axis_index(axis)
    return sum_ahead([pick(value, lax.rem(me + s, count), at) for s in range(count)], axis)


def dot_nn(a, b):
    return jnp.dot(a, b, preferred_element_type=f32)


def dot_nt(a, b):
    return lax.dot_general(a, b, (((1,), (1,)), ((), ())), preferred_element_type=f32)


def dot_tn(a, b):
    return lax.dot_general(a, b, (((0,), (0,)), ((), ())), preferred_element_type=f32)


def whole(*shape):
    return pl.BlockSpec(shape, lambda *_: (0,) * len(shape))


def corner(value):
    lead = value.ndim - 2
    return pl.BlockSpec((1,) * lead + (16, 128), lambda *_: (0,) * value.ndim)


def without(kernel, count, first):
    def body(*refs):
        return kernel(*refs[:first], *refs[first + count :])

    return body


SCALARS = pl.BlockSpec(memory_space=pltpu.SMEM)
SCALE = (NOPE + ROPE) ** (-0.5)
MIB = 1024 * 1024


def like(*shape, dtype=bf16):
    return jax.ShapeDtypeStruct(shape, dtype)


def run(kernel, place, inputs, outs, after=(), scratch=(), size=40, flops=10**6):
    vmem = pl.BlockSpec(memory_space=pltpu.VMEM)
    lead = [] if place is None else [SCALARS]
    given = [] if place is None else [place]
    moved = sum(v.size * v.dtype.itemsize for v in list(inputs) + list(outs))
    return pl.pallas_call(
        without(kernel, len(after), len(lead) + len(inputs)),
        grid=(1,) if after else (),
        in_specs=lead + [vmem] * len(inputs) + [corner(v) for v in after],
        out_specs=[vmem] * len(outs),
        out_shape=list(outs),
        scratch_shapes=list(scratch),
        compiler_params=pltpu.CompilerParams(vmem_limit_bytes=size * MIB),
        cost_estimate=pl.CostEstimate(flops=flops, bytes_accessed=moved, transcendentals=0),
        name=kernel.__name__.removesuffix("_kernel"),
    )(*given, *inputs, *after)


def enter_kernel(place, tokens, cotangent, routes, tok0, tok1, spread0, spread1):
    for side, tok, spread in ((place[2], tok0, spread0), (1 - place[2], tok1, spread1)):
        tok[...] = tokens[side]
        spread[:, :2048] = cotangent[side]
        named = routes[side]
        lane = lax.broadcasted_iota(jnp.int32, (64, 128), 1) - 66
        chosen = named[:, 0:1] == lane
        for k in range(1, named.shape[1]):
            chosen = chosen | (named[:, k : k + 1] == lane)
        spread[:, 2048:] = chosen.astype(f32).astype(bf16)


def front_kernel(
    place, tok0, tok1, mine, other, cosine, sine,
    normed, packed, compressed, weight, gains, tok,
):
    is_first = place[2] == 0
    tok[:64, :] = jnp.where(is_first, tok0[...], tok1[...])
    tok[64:, :] = jnp.where(is_first, tok1[...], tok0[...])
    for sx in range(4):
        for sz in range(4):
            block = lax.rem(place[0] - sx + 4, 4) * 4 + lax.rem(place[1] - sz + 4, 4)
            for part, core in ((mine, place[2]), (other, 1 - place[2])):
                row = pl.multiple_of(block * 128 + core * 64, 64)
                src = (sx * 4 + sz) * 64
                weight[pl.ds(row, 64), :] = part[src : src + 64, :]
    turned = weight[:, 512:640].astype(f32).T
    gains[0:2, :] = turned[64:66, :]
    latent_gain = jnp.concatenate(
        [turned[74:75, 64 * i : 64 * i + 16] for i in range(32)], axis=1
    )
    gains[2:3, :RANK] = latent_gain
    values = tok[...].astype(f32)
    factor = lax.rsqrt(jnp.mean(values * values, axis=1, keepdims=True) + epsilon)
    low = (values * factor * turned[64:65, :]).astype(bf16)
    normed[...] = low
    raw = dot_nn(low, weight[:, :576])
    compressed[...] = raw
    main = raw[:, :RANK]
    factor = lax.rsqrt(jnp.mean(main * main, axis=1, keepdims=True) + epsilon)
    latent = (main * factor * latent_gain).astype(bf16)
    first, second = raw[:, RANK : RANK + 32], raw[:, RANK + 32 :]
    cos, sin = cosine[:, :32], sine[:, :32]
    rot = jnp.concatenate([first * cos - second * sin, second * cos + first * sin], axis=1)
    packed[:, :RANK] = latent
    packed[:, RANK:] = jnp.concatenate([rot, jnp.zeros((128, 64), f32)], axis=1).astype(bf16)


def expansion(weight):
    blocks = weight[:, 1280:].reshape(32, 4, 16, 256)
    return jnp.concatenate([blocks[:, h].reshape(RANK, 256) for h in range(4)], axis=1)


def turned(rot):
    lane = lax.broadcasted_iota(jnp.int32, rot.shape, 1)
    return jnp.where(lane % 64 < 32, pltpu.roll(rot, 224, 1), pltpu.roll(rot, 32, 1))


def attend_kernel(
    place, normed, weight, cosine, sine, l0, l1, l2, l3, where_q, where_k,
    prob, kv, attended, q, r0, r1, r2, r3, key_rot, total,
):
    expand = expansion(weight)
    for s, part in enumerate((l0, l1, l2, l3)):
        rows = slice(s * 512, s * 512 + 512)
        kv[rows, :] = dot_nn(part[:, :RANK], expand).astype(bf16)
        key_rot[rows, :] = part[:, RANK:]
    nope = dot_nn(normed[...], weight[:, :512]).astype(bf16)
    rot = dot_nn(normed[...], weight[:, 512:768])
    rot = (rot * cosine[...] - turned(rot) * sine[...]).astype(bf16)
    allowed = (where_q[:, 0:1] >= where_k[0:1, :]) & (where_q[:, 1:2] == where_k[1:2, :])
    pad = jnp.zeros((128, 64), bf16)
    for h in range(4):
        at = h * 256
        q_h = jnp.concatenate(
            [nope[:, h * 128 : h * 128 + 128], rot[:, h * 64 : h * 64 + 64], pad], axis=1
        )
        q[:, at : at + 256] = q_h
        key = jnp.concatenate([kv[:, at : at + 128], key_rot[...]], axis=1)
        score = jnp.where(allowed, dot_nt(q_h, key) * SCALE, -1e30)
        power = jnp.exp(score - jnp.max(score, axis=1, keepdims=True))
        low = (power * (1.0 / jnp.sum(power, axis=1, keepdims=True))).astype(bf16)
        prob[h] = low
        attended[:, h * 128 : h * 128 + 128] = dot_nn(low, kv[:, at + 128 : at + 256]).astype(bf16)
    total[...] = dot_nt(attended[...], weight[:, 768:1280]).astype(bf16)
    for s, out in enumerate((r0, r1, r2, r3)):
        row = pl.multiple_of(lax.rem(place[3] + s, 4) * 32, 32)
        out[...] = total[pl.ds(row, 32), :]


def attend(place, normed, parts, attn_all, cosine, sine, where_q, where_k):
    return run(
        attend_kernel,
        place,
        [normed, attn_all, cosine, sine, *parts, where_q, where_k],
        [like(4, 128, 2048), like(2048, 1024), like(128, 512), like(128, 1024)]
        + [like(32, 2048)] * 4,
        scratch=[pltpu.VMEM((2048, 128), bf16), pltpu.VMEM((128, 2048), bf16)],
        flops=5 * 10**9,
    )


def middle_kernel(place, r0, r1, r2, r3, tok, gains, middle, far):
    row = pl.multiple_of(place[3] * 32, 32)
    values = tok[pl.ds(row, 32), :].astype(f32)
    for part in (r0, r1, r2, r3):
        values = values + part[...].astype(f32)
    middle[...] = values
    factor = lax.rsqrt(jnp.mean(values * values, axis=1, keepdims=True) + epsilon)
    far[...] = (values * factor * gains[1:2, :]).astype(bf16)


def middle_back_kernel(
    place, a0, a1, a2, a3, spread, middle, gains, weight, d_mid, d_low, small
):
    row = pl.multiple_of(place[3] * 32, 32)
    total = a0[...].astype(f32)
    for part in (a1, a2, a3):
        total = total + part[...].astype(f32)
    d_normed = total[:, :2048]
    d_gate = total[:, 2048:]
    mine = spread[pl.ds(row, 32), :]
    d_out = mine[:, :2048].astype(f32)
    chosen = mine[:, 2048:].astype(f32)
    values = middle[...]
    gain = gains[1:2, :]
    factor = lax.rsqrt(jnp.mean(values * values, axis=1, keepdims=True) + epsilon)
    low = (values * factor * gain).astype(bf16)
    table = weight[:, 512:640]
    lane = lax.broadcasted_iota(jnp.int32, (32, 128), 1)
    is_expert = (lane >= 66) & (lane < 74)
    logits = jnp.where(is_expert, dot_nn(low, table), -1e30)
    power = jnp.exp(logits - jnp.max(logits, axis=1, keepdims=True))
    router = power / jnp.sum(power, axis=1, keepdims=True)
    d_chosen = d_gate * chosen
    d_logits = router * (d_chosen - jnp.sum(router * d_chosen, axis=1, keepdims=True))
    d_logits = d_logits.astype(bf16)
    d_normed = d_normed + dot_nt(d_logits, table)
    scaled = d_normed * gain
    d_norm = factor * scaled - values * (factor * factor * factor) * jnp.mean(
        values * scaled, axis=1, keepdims=True
    )
    d_values = d_out + d_norm
    d_mid[...] = d_values
    d_low[...] = d_values.astype(bf16)
    terms = (d_normed * values * factor).astype(bf16)
    small[...] = (
        dot_tn(low, d_logits) + dot_tn(terms, (lane == 65).astype(bf16))
    ).astype(bf16)


def latent_back_kernel(
    place, t0, t1, t2, t3, compressed, gains, cosine, sine, d_comp, small
):
    row = pl.multiple_of(place[3] * 32, 32)
    terms = t0[...].astype(f32)
    for part in (t1, t2, t3):
        terms = terms + part[...].astype(f32)
    main = compressed[pl.ds(row, 32), :][:, :RANK]
    factor = lax.rsqrt(jnp.mean(main * main, axis=1, keepdims=True) + epsilon)
    grad_main = terms[:, :RANK]
    scaled = grad_main * gains[2:3, :RANK]
    d_main = factor * scaled - main * (factor * factor * factor) * jnp.mean(
        main * scaled, axis=1, keepdims=True
    )
    first, second = terms[:, RANK : RANK + 32], terms[:, RANK + 32 : RANK + 64]
    cos, sin = cosine[pl.ds(row, 32), :][:, :32], sine[pl.ds(row, 32), :][:, :32]
    rot = jnp.concatenate([first * cos + second * sin, second * cos - first * sin], axis=1)
    d_comp[:, :RANK] = d_main.astype(bf16)
    d_comp[:, RANK:] = jnp.concatenate([rot, jnp.zeros((32, 64), f32)], axis=1).astype(bf16)
    latent_terms = grad_main * main * factor
    gap = jnp.zeros((32, 48), f32)
    latent_terms = jnp.concatenate(
        [p for i in range(32) for p in (latent_terms[:, 16 * i : 16 * i + 16], gap)], axis=1
    )
    lane = lax.broadcasted_iota(jnp.int32, (32, 128), 1)
    small[...] = dot_tn(latent_terms.astype(bf16), (lane == 74).astype(bf16)).astype(bf16)


def token_back_kernel(place, d_comp, q0, q1, q2, q3, tok, gains, weight, d_mid, grad, small):
    row = pl.multiple_of(place[3] * 32, 32)
    d_normed = dot_nt(d_comp[...], weight[:, :640])
    for part in (q0, q1, q2, q3):
        d_normed = d_normed + part[...].astype(f32)
    values = tok[pl.ds(row, 32), :].astype(f32)
    factor = lax.rsqrt(jnp.mean(values * values, axis=1, keepdims=True) + epsilon)
    scaled = d_normed * gains[0:1, :]
    d_norm = factor * scaled - values * (factor * factor * factor) * jnp.mean(
        values * scaled, axis=1, keepdims=True
    )
    grad[...] = (d_mid[...] + d_norm).astype(bf16)
    lane = lax.broadcasted_iota(jnp.int32, (32, 128), 1)
    small[...] = dot_tn(
        (d_normed * values * factor).astype(bf16), (lane == 64).astype(bf16)
    ).astype(bf16)


def compress_grad_kernel(place, c0, c1, c2, c3, normed, s0, s1, s2, mine, other, d_all):
    for s, part in enumerate((c0, c1, c2, c3)):
        row = pl.multiple_of(lax.rem(place[3] - s + 4, 4) * 32, 32)
        d_all[pl.ds(row, 32), :] = part[...]
    column = pl.multiple_of(place[3] * 128, 128)
    own = d_all[:, pl.ds(column, 128)]
    rot = d_all[:, RANK:]
    main = dot_tn(normed[...], own).astype(bf16)
    rest = dot_tn(normed[...], rot)
    for part in (s0, s1, s2):
        rest = rest + part[...].astype(f32)
    rest = rest.astype(bf16)
    is_first = place[2] == 0
    for b in range(16):
        for columns, value in ((slice(0, 128), main), (slice(128, 256), rest)):
            low, high = value[b * 128 : b * 128 + 64], value[b * 128 + 64 : b * 128 + 128]
            mine[b * 64 : b * 64 + 64, columns] = jnp.where(is_first, low, high)
            other[b * 64 : b * 64 + 64, columns] = jnp.where(is_first, high, low)


def attend_back_kernel(
    place, d0, d1, d2, d3, weight, q, kv, prob, l0, l1, l2, l3, cosine, sine,
    d_q, d_rot, d_exp, d_branch, k0, k1, k2, k3, r0, r1, r2, r3, key_rot, rot_sum, total,
):
    for s, part in enumerate((d0, d1, d2, d3)):
        row = pl.multiple_of(lax.rem(place[3] - s + 4, 4) * 32, 32)
        d_branch[pl.ds(row, 32), :] = part[...]
    for s, part in enumerate((l0, l1, l2, l3)):
        key_rot[s * 512 : s * 512 + 512, :] = part[:, RANK:]
    d_att = dot_nn(d_branch[...], weight[:, 768:1280]).astype(bf16)
    rots = []
    for h in range(4):
        at = h * 256
        d_att_h = d_att[:, h * 128 : h * 128 + 128]
        low = prob[h]
        prob_h = low.astype(f32)
        d_prob = dot_nt(d_att_h, kv[:, at + 128 : at + 256])
        row_sum = jnp.sum(prob_h * d_prob, axis=1, keepdims=True)
        d_score = (prob_h * (d_prob - row_sum)).astype(bf16)
        key = jnp.concatenate([kv[:, at : at + 128], key_rot[...]], axis=1)
        d_query = dot_nn(d_score, key) * SCALE
        d_q[:, h * 128 : h * 128 + 128] = d_query[:, :128].astype(bf16)
        rots.append(d_query[:, 128:192])
        d_key = dot_tn(d_score, q[:, at : at + 256]) * SCALE
        d_exp[:, at : at + 128] = d_key[:, :128].astype(bf16)
        d_exp[:, at + 128 : at + 256] = dot_tn(low, d_att_h).astype(bf16)
        if h == 0:
            rot_sum[...] = d_key[:, 128:]
        else:
            rot_sum[...] += d_key[:, 128:]
    expand = expansion(weight)
    for s, out in enumerate((k0, k1, k2, k3)):
        rows = slice(s * 512, s * 512 + 512)
        out[:, :RANK] = dot_nt(d_exp[rows, :], expand).astype(bf16)
        out[:, RANK:] = rot_sum[rows, :].astype(bf16)
    rot = jnp.concatenate(rots, axis=1)
    rot = (rot * cosine[...] + turned(rot) * sine[...]).astype(bf16)
    d_rot[...] = rot
    total[...] = (dot_nt(d_q[...], weight[:, :512]) + dot_nt(rot, weight[:, 512:768])).astype(bf16)
    for s, out in enumerate((r0, r1, r2, r3)):
        row = pl.multiple_of(lax.rem(place[3] + s, 4) * 32, 32)
        out[...] = total[pl.ds(row, 32), :]


def attend_back(place, parts, q, kv, prob, latents, attn_all, cosine, sine, after):
    return run(
        attend_back_kernel,
        place,
        [*parts, attn_all, q, kv, prob, *latents, cosine, sine],
        [like(128, 512), like(128, 256), like(2048, 1024), like(128, 2048)]
        + [like(512, 640)] * 4
        + [like(32, 2048)] * 4,
        after=after,
        scratch=[
            pltpu.VMEM((2048, 128), bf16),
            pltpu.VMEM((2048, 128), f32),
            pltpu.VMEM((128, 2048), bf16),
        ],
        flops=8 * 10**9,
    )


PARTS = 1


def expert_kernel(place, far, spread, weight, d_far, d_hidden, hidden, out):
    expert = 2 * place[1] + place[2]
    for part in range(PARTS):
        at = slice(part * 512 // PARTS, (part + 1) * 512 // PARTS)
        raw = dot_nn(far[at, :], weight[:, :896])
        d_weighted = dot_nn(spread[at, :2048], weight[:, 896:])
        rows = raw.shape[0]
        logits = raw[:, 880:888]
        power = jnp.exp(logits - jnp.max(logits, axis=1, keepdims=True))
        router = power / jnp.sum(power, axis=1, keepdims=True)
        is_mine = lax.broadcasted_iota(jnp.int32, (rows, 8), 1) == expert
        chosen = spread[at, 2048:2176][:, 66:74].astype(f32)
        gate = jnp.sum(jnp.where(is_mine, router * chosen, 0.0), axis=1, keepdims=True)
        routed = lax.broadcasted_iota(jnp.int32, (rows, 440), 1) < 352
        gate = jnp.where(routed, gate, 1.0)
        low, upper = raw[:, :440], raw[:, 440:880]
        sigma = 1.0 / (1.0 + jnp.exp(-low))
        silu = low * sigma
        slope = sigma + silu * (1.0 - sigma)
        act = silu * upper
        weighted = (gate * act).astype(bf16)
        d_gate = jnp.sum(jnp.where(routed, d_weighted * act, 0.0), axis=1, keepdims=True)
        d_act = d_weighted * gate
        d_up = jnp.concatenate(
            [d_act * upper * slope, d_act * silu, jnp.zeros((rows, 16), f32)], axis=1
        ).astype(bf16)
        d_hidden[at, :] = d_up
        hidden[at, :] = jnp.concatenate([weighted, jnp.zeros((rows, 72), bf16)], axis=1)
        d_far[at, :2048] = dot_nt(d_up, weight[:, :896]).astype(bf16)
        lane = lax.broadcasted_iota(jnp.int32, (rows, 128), 1)
        d_far[at, 2048:] = jnp.where(lane == expert + 66, d_gate, 0.0).astype(bf16)
        out[at, :] = dot_nt(weighted, weight[:, 896:]).astype(bf16)


def expert(place, far, spread, weight):
    return run(
        expert_kernel,
        place,
        [far, spread, weight],
        [like(512, 2176), like(512, 896), like(512, 512), like(512, 2048)],
        flops=6 * 10**9,
    )


def expert_grad_kernel(x0, x1, y0, y1, d0, d1, h0, h1, out):
    out[:, :896] = (dot_tn(x0[...], d0[...]) + dot_tn(x1[...], d1[...])).astype(bf16)
    down = dot_tn(y0[...], h0[...]) + dot_tn(y1[...], h1[...])
    out[:, 896:] = down[:, :440].astype(bf16)


def expert_grad(fars, spreads, d_hiddens, hiddens, after):
    columns = pl.BlockSpec((512, 512), lambda i: (0, i))
    return pl.pallas_call(
        without(expert_grad_kernel, len(after), 8),
        grid=(4,),
        in_specs=[columns] * 4
        + [whole(512, 896)] * 2
        + [whole(512, 512)] * 2
        + [corner(v) for v in after],
        out_specs=pl.BlockSpec((512, 1336), lambda i: (i, 0)),
        out_shape=like(2048, 1336),
        compiler_params=pltpu.CompilerParams(vmem_limit_bytes=40 * MIB),
        cost_estimate=pl.CostEstimate(
            flops=6 * 10**9, bytes_accessed=18 * 10**6, transcendentals=0
        ),
        name="expert_grad",
    )(*fars, *spreads, *d_hiddens, *hiddens, *after)


def attn_grad_kernel(normed, d_q, d_rot, d_branch, attended, l0, l1, l2, l3, d_exp, out):
    g_exp = 0.0
    for s, part in enumerate((l0, l1, l2, l3)):
        g_exp = g_exp + dot_tn(part[:, :RANK], d_exp[s * 512 : s * 512 + 512, :])
    g_exp = g_exp.astype(bf16)
    out[:, :512] = dot_tn(normed[...], d_q[...]).astype(bf16)
    out[:, 512:768] = dot_tn(normed[...], d_rot[...]).astype(bf16)
    out[:, 768:1280] = dot_tn(d_branch[...], attended[...]).astype(bf16)
    for d in range(32):
        for h in range(4):
            to = d * 64 + h * 16
            out[to : to + 16, 1280:] = g_exp[d * 16 : d * 16 + 16, h * 256 : h * 256 + 256]


def attn_grad(normed, d_q, d_rot, d_branch, attended, latents, d_exp, after):
    return run(
        attn_grad_kernel,
        None,
        [normed, d_q, d_rot, d_branch, attended, *latents, d_exp],
        [like(2048, 1536)],
        after=after,
        flops=4 * 10**9,
    )[0]


def pack_expert_kernel(
    place, expert_in, expert_out, shared_in, shared_out, router, mine, send
):
    is_first = place[2] == 0
    gap = jnp.zeros((64, 8), f32)
    for z in range(4):
        both = []
        for core in range(2):
            expert = 2 * z + core
            cut = slice(88 * expert, 88 * expert + 88)
            parts = [
                expert_in[:, expert, 0, :],
                shared_in[:, 0, cut],
                expert_in[:, expert, 1, :],
                shared_in[:, 1, cut],
                router[...],
                gap,
                expert_out[:, expert, :],
                shared_out[:, cut],
            ]
            both.append(jnp.concatenate([part.astype(f32) for part in parts], axis=1))
        mine[z] = jnp.where(is_first, both[0], both[1]).astype(bf16)
        send[z] = jnp.where(is_first, both[1], both[0]).astype(bf16)


def pair_kernel(place, mine, other, p0, p1, p2, p3):
    is_first = place[2] == 0
    for s, out in enumerate((p0, p1, p2, p3)):
        to = lax.rem(place[1] + s, 4)
        a, b = mine[to], other[to]
        out[:64, :] = jnp.where(is_first, a, b)
        out[64:, :] = jnp.where(is_first, b, a)


def turn_kernel(place, mine, other, natural, out):
    is_first = place[2] == 0
    natural[:64, :] = jnp.where(is_first, mine[...], other[...])
    natural[64:, :] = jnp.where(is_first, other[...], mine[...])
    for s in range(4):
        row = pl.multiple_of(lax.rem(place[3] - s + 4, 4) * 32, 32)
        out[s * 32 : s * 32 + 32, :] = natural[pl.ds(row, 32), :]


def stack_kernel(p0, p1, p2, p3, out):
    rows = p0.shape[0]
    for s, part in enumerate((p0, p1, p2, p3)):
        out[s * rows : s * rows + rows, :] = part[...]


def add_split_kernel(mine, other, *outs):
    rows = outs[0].shape[0]
    for s, out in enumerate(outs):
        at = slice(s * rows, s * rows + rows)
        out[...] = (mine[at, :].astype(f32) + other[at, :].astype(f32)).astype(bf16)


def sum_split_kernel(v0, v1, v2, v3, *outs):
    rows = outs[0].shape[0]
    for s, out in enumerate(outs):
        at = slice(s * rows, s * rows + rows)
        total = v0[at, :].astype(f32)
        for part in (v1, v2, v3):
            total = total + part[at, :].astype(f32)
        out[...] = total.astype(bf16)


def row_sum_kernel(place, v0, v1, v2, v3, *outs):
    for s, out in enumerate(outs):
        rows = pl.ds(pl.multiple_of(lax.rem(place[3] + s, 4) * 32, 32), 32)
        total = v0[rows, :].astype(f32)
        for part in (v1, v2, v3):
            total = total + part[rows, :].astype(f32)
        out[...] = total.astype(bf16)


def out_rows_kernel(v0, v1, v2, v3, middle, out):
    total = v0[...].astype(f32)
    for part in (v1, v2, v3):
        total = total + part[...].astype(f32)
    out[...] = (middle[...] + total).astype(bf16)


def cut_kernel(place, value, p0, p1, p2, p3):
    for s, out in enumerate((p0, p1, p2, p3)):
        rows = pl.ds(pl.multiple_of(lax.rem(place[1] + s, 4) * 128, 128), 128)
        out[...] = value[rows, :]


def join_kernel(place, p0, p1, p2, p3, out):
    for s, part in enumerate((p0, p1, p2, p3)):
        rows = pl.ds(pl.multiple_of(lax.rem(place[1] - s + 4, 4) * 128, 128), 128)
        out[rows, :] = part[...]


def pack_attn_kernel(query, output, expand, out):
    value = query[...]
    out[:, :512] = jnp.concatenate([value[:, 192 * h : 192 * h + 128] for h in range(4)], axis=1)
    out[:, 512:768] = jnp.concatenate(
        [value[:, 192 * h + 128 : 192 * h + 192] for h in range(4)], axis=1
    )
    out[:, 768:1280] = output[...]
    for h in range(4):
        out[h * 16 : h * 16 + 16, 1280:] = expand[:, h * 256 : h * 256 + 256]


def by_core_kernel(place, p0, p1, p2, p3, mine, other):
    is_first = place[2] == 0
    for s, part in enumerate((p0, p1, p2, p3)):
        at = lax.rem(place[1] - s + 4, 4)
        low, high = part[:64, :], part[64:, :]
        mine[at] = jnp.where(is_first, low, high)
        other[at] = jnp.where(is_first, high, low)


def unpack_kernel(place, mine, other, expert_in, expert_out, shared_in, shared_out):
    is_first = place[2] == 0
    ins, outs, downs = [], [], []
    for x in range(4):
        for core in range(2):
            a, b = (mine[x], other[x]) if core == 0 else (other[x], mine[x])
            value = jnp.where(is_first, a, b).astype(f32)
            expert = 2 * x + core
            expert_in[:, expert, 0, :] = value[:, :352]
            expert_in[:, expert, 1, :] = value[:, 440:792]
            expert_out[:, expert, :] = value[:, 896:1248]
            ins.append(value[:, 352:440])
            outs.append(value[:, 792:880])
            downs.append(value[:, 1248:])
    shared_in[:, 0, :] = jnp.concatenate(ins, axis=1)
    shared_in[:, 1, :] = jnp.concatenate(outs, axis=1)
    shared_out[...] = jnp.concatenate(downs, axis=1)


def finish_kernel(total, query, output, expand):
    value = total[...].astype(f32)
    query[...] = jnp.concatenate(
        [
            p
            for h in range(4)
            for p in (
                value[:, h * 128 : h * 128 + 128],
                value[:, 512 + h * 64 : 576 + h * 64],
            )
        ],
        axis=1,
    )
    output[...] = value[:, 768:1280]
    for h in range(4):
        expand[:, h * 256 : h * 256 + 256] = value[h * 16 : h * 16 + 16, 1280:]


def on_device(
    tokens,
    segment,
    routes,
    cotangent,
    gain_attn,
    w_query,
    w_compress,
    gain_latent,
    w_expand,
    w_output,
    gain_ffn,
    w_router,
    w_expert_in,
    w_expert_out,
    w_shared_in,
    w_shared_out,
):
    xi, zi, ci, yi = (lax.axis_index(a) for a in ("x", "z", "c", "y"))
    place = jnp.stack([xi, zi, ci, yi]).astype(jnp.int32)
    is_first = ci == 0
    heads = 4
    dim = 2048

    def leave(value):
        halves = value.reshape((2, 64) + value.shape[1:])
        mine, other = pick(halves, ci, 0), shift(pick(halves, 1 - ci, 0), "c", 1)
        return jnp.stack([jnp.where(is_first, mine, other), jnp.where(is_first, other, mine)])

    small = jnp.concatenate(
        [
            w_compress,
            gain_attn[:, None],
            gain_ffn[:, None],
            w_router,
            jnp.pad(gain_latent, (0, 48))[:, None],
            jnp.zeros((64, 53), bf16),
        ],
        axis=1,
    )
    small_z_parts = gather_near(small, "z")
    (small_z,) = run(stack_kernel, None, small_z_parts, [like(256, 640)])
    small_x = gather_near(small_z, "x")
    (small_mine,) = run(stack_kernel, None, small_x, [like(1024, 640)])
    small_other = shift(small_mine, "c", 1)

    mine_w, send_w = run(
        pack_expert_kernel,
        place,
        [w_expert_in, w_expert_out, w_shared_in, w_shared_out, w_router],
        [like(4, 64, 1336)] * 2,
        after=small_z_parts[1:],
    )
    other_w = shift(send_w, "c", 1)

    tok_mine, tok_send, spread_mine, spread_send = run(
        enter_kernel,
        place,
        [tokens, cotangent, routes],
        [like(64, 2048), like(64, 2048), like(64, 2176), like(64, 2176)],
    )
    tok_other = shift(tok_send, "c", 1)
    spread_other = shift(spread_send, "c", 1)

    position = (xi * 4 + zi) * 128 + jnp.arange(128, dtype=jnp.int32)
    segment_row = pick(segment, ci, 0)
    blocks = jnp.stack(
        [lax.rem(xi - sx + 4, 4) * 4 + lax.rem(zi - sz + 4, 4) for sx in range(4) for sz in range(4)]
    )
    segment_near = segment_row.reshape(16, 128)[blocks].reshape(2048)
    key_place = (blocks[:, None] * 128 + jnp.arange(128, dtype=jnp.int32)[None, :]).reshape(2048)
    where_k = jnp.stack([key_place, segment_near])
    where_q = jnp.stack(
        [position, lax.dynamic_slice_in_dim(segment_row, (xi * 4 + zi) * 128, 128)], axis=1
    )
    lane = jnp.arange(256)[None, :]
    freq = jnp.exp((lane % 32).astype(f32) * (-jnp.log(10000.0) / 32))
    angle = position.astype(f32)[:, None] * freq
    cosine = jnp.cos(angle)
    sine = jnp.where(lane % 64 < 32, 1.0, -1.0) * jnp.sin(angle)

    pair_w = run(pair_kernel, place, [mine_w, other_w], [like(128, 1336)] * 4)
    pair_w = [pair_w[0]] + [shift(pair_w[s], "z", s) for s in range(1, 4)]
    (attn_w,) = run(
        pack_attn_kernel,
        None,
        [w_query, w_output, w_expand],
        [like(64, 1536)],
        after=small_x[1:] + pair_w[1:],
    )
    (expert_w,) = run(join_kernel, place, pair_w, [like(512, 1336)], after=[attn_w])
    attn_all = lax.all_gather(attn_w, ("x", "z", "c"), axis=0, tiled=True)
    ffn_all = lax.all_gather(expert_w, "x", axis=0, tiled=True)

    normed, packed, compressed, weight, gains, tok = run(
        front_kernel,
        place,
        [tok_mine, tok_other, small_mine, small_other, cosine, sine],
        [
            like(128, 2048),
            like(128, 640),
            like(128, 576, dtype=f32),
            like(2048, 640),
            like(8, 2048, dtype=f32),
            like(128, 2048),
        ],
    )
    (latent_near,) = run(stack_kernel, None, gather_near(packed, "z"), [like(512, 640)])
    latents = gather_near(latent_near, "x")
    spread_here, spread = run(
        turn_kernel,
        place,
        [spread_mine, spread_other],
        [like(128, 2176)] * 2,
        after=latents[1:2],
    )
    spread = gather_near(spread, "z")
    prob, kv, attended, query, *branch = attend(
        place, normed, latents, attn_all, cosine, sine, where_q, where_k
    )
    branch = [branch[0]] + [shift(branch[s], "y", s) for s in range(1, 4)]
    (spread,) = run(stack_kernel, None, spread, [like(512, 2176)], after=[attended])
    spread_other = shift(spread, "c", 1)
    middle, far = run(
        middle_kernel,
        place,
        [*branch, tok, gains],
        [like(32, 2048, dtype=f32), like(32, 2048)],
        after=[spread],
    )

    (far,) = run(stack_kernel, None, gather_near(far, "y"), [like(128, 2048)])
    (far,) = run(stack_kernel, None, gather_near(far, "z"), [like(512, 2048)])
    far_other = shift(far, "c", 1)
    d_far2, d_hidden2, hidden2, out_far2 = expert(place, far_other, spread_other, ffn_all)
    d_far, d_hidden, hidden, out_far = expert(place, far, spread, ffn_all)
    d_far = run(
        add_split_kernel, None, [d_far, shift(d_far2, "c", 1)], [like(128, 2176)] * 4
    )
    d_far = [d_far[0]] + [shift(d_far[s], "z", -s) for s in range(1, 4)]
    d_far = run(sum_split_kernel, None, d_far, [like(32, 2176)] * 4)
    grad_ffn = expert_grad(
        (far, far_other), (spread, spread_other), (d_hidden, d_hidden2), (hidden, hidden2), d_far[:1]
    )
    grad_ffn = lax.psum_scatter(grad_ffn, "x", scatter_dimension=0, tiled=True)
    d_far = [d_far[0]] + [shift(d_far[s], "y", -s) for s in range(1, 4)]
    d_mid, d_low, small_a = run(
        middle_back_kernel,
        place,
        [*d_far, spread_here, middle, gains, weight],
        [like(32, 2048, dtype=f32), like(32, 2048), like(2048, 128)],
    )
    out_far = run(
        add_split_kernel,
        None,
        [out_far, shift(out_far2, "c", 1)],
        [like(128, 2048)] * 4,
        after=d_far[:1],
    )
    out_far = [out_far[0]] + [shift(out_far[s], "z", -s) for s in range(1, 4)]
    d_low = gather_near(d_low, "y")

    d_q, d_rot, d_expanded, d_branch, *rest = attend_back(
        place, d_low, query, kv, prob, latents, attn_all, cosine, sine, out_far[1:]
    )
    terms = [rest[0]] + [shift(rest[s], "x", -s) for s in range(1, 4)]
    d_queries = [rest[4]] + [shift(rest[4 + s], "y", s) for s in range(1, 4)]
    grad_ffn = run(cut_kernel, place, [grad_ffn], [like(128, 1336)] * 4)
    grad_ffn = [grad_ffn[0]] + [shift(grad_ffn[s], "z", s) for s in range(1, 4)]
    terms = run(
        sum_split_kernel, None, terms, [like(128, 640)] * 4, after=grad_ffn[1:]
    )
    out_far = run(sum_split_kernel, None, out_far, [like(32, 2048)] * 4, after=terms[:1])
    out_far = [out_far[0]] + [shift(out_far[s], "y", -s) for s in range(1, 4)]
    mine_g, other_g = run(by_core_kernel, place, grad_ffn, [like(4, 64, 1336)] * 2)
    terms = [terms[0]] + [shift(terms[s], "z", -s) for s in range(1, 4)]
    terms = run(
        row_sum_kernel, place, terms, [like(32, 640)] * 4, after=out_far[1:] + [mine_g]
    )
    terms = [terms[0]] + [shift(terms[s], "y", s) for s in range(1, 4)]
    (mixed,) = run(out_rows_kernel, None, [*out_far, middle], [like(32, 2048)], after=terms[:1])
    mixed = gather_near(mixed, "y")

    d_comp, small_b = run(
        latent_back_kernel,
        place,
        [*terms, compressed, gains, cosine, sine],
        [like(32, 640), like(2048, 128)],
        after=mixed[1:],
    )
    g_expert_in, g_expert_out, g_shared_in, g_shared_out = run(
        unpack_kernel,
        place,
        [mine_g, shift(other_g, "c", 1)],
        [
            like(64, 8, 2, 352, dtype=f32),
            like(64, 8, 352, dtype=f32),
            like(64, 2, 704, dtype=f32),
            like(64, 704, dtype=f32),
        ],
    )
    grad_rows, small_c = run(
        token_back_kernel,
        place,
        [d_comp, *d_queries, tok, gains, weight, d_mid],
        [like(32, 2048), like(2048, 128)],
    )
    grad_rows = leave(place_at(gather_near(grad_rows, "y"), "y").reshape(128, dim))
    mixed = leave(place_at(mixed, "y").reshape(128, dim))

    def fsdp_sum(mine, other, cuts):
        value = (mine.astype(f32) + shift(other, "c", 1).astype(f32)).astype(bf16)
        value = value.reshape(4, 4, 64, -1)
        done = []
        for start, stop, first, second in cuts:
            part = sum_at(value[..., start:stop], first, 0 if first == "x" else 1).astype(bf16)
            done.append(sum_at(part, second, 0))
        return done

    g_attn = attn_grad(normed, d_q, d_rot, d_branch, attended, latents, d_expanded, [])
    g_attn = lax.psum_scatter(g_attn, ("x", "z", "c"), scatter_dimension=0, tiled=True)
    g_mine, g_other = run(
        compress_grad_kernel,
        place,
        [*gather_near(d_comp, "y"), normed, small_a, small_b, small_c],
        [like(1024, 256)] * 2,
        scratch=[pltpu.VMEM((128, 640), bf16)],
    )
    (g_small,) = fsdp_sum(g_mine, g_other, ((0, 256, "x", "z"),))
    g_small = g_small.astype(bf16)
    g_parts = gather_near(g_small, "y")
    g_query, g_output, g_expand = run(
        finish_kernel,
        None,
        [g_attn],
        [like(64, 768, dtype=f32), like(64, 512, dtype=f32), like(16, 1024, dtype=f32)],
        after=g_parts[1:] + [g_shared_out],
    )
    g_small = place_at(g_parts, "y")
    g_small = g_small.astype(f32)
    g_compress = jnp.concatenate(
        [g_small[i, :, :128] for i in range(4)] + [g_small[0, :, 128:192]], axis=1
    )
    g_small = jnp.sum(g_small[:, :, 192:], axis=0)

    return (
        mixed,
        grad_rows,
        g_small[:, 0],
        g_query,
        g_compress,
        g_small[:16, 10],
        g_expand,
        g_output,
        g_small[:, 1],
        g_small[:, 2:10],
        g_expert_in,
        g_expert_out,
        g_shared_in,
        g_shared_out,
    )


def solution(mesh):
    fine = Mesh(mesh.devices.reshape(4, 4, 2, 4), ("x", "z", "c", "y"))
    rows = ("x", "z", "c")
    return jax.shard_map(
        on_device,
        mesh=fine,
        in_specs=(
            P(None, rows, None),
            P(),
            P(None, rows, None),
            P(None, rows, None),
            P(rows),
            P(rows, "y"),
            P(rows, None),
            P(rows),
            P(rows, "y"),
            P(rows, "y"),
            P(rows),
            P(rows, None),
            P(rows, None, None, "y"),
            P(rows, None, "y"),
            P(rows, None, "y"),
            P(rows, "y"),
        ),
        out_specs=(
            P(None, rows, None),
            P(None, rows, None),
            P(rows),
            P(rows, "y"),
            P(rows, None),
            P(rows),
            P(rows, "y"),
            P(rows, "y"),
            P(rows),
            P(rows, None),
            P(rows, None, None, "y"),
            P(rows, None, "y"),
            P(rows, None, "y"),
            P(rows, "y"),
        ),
        check_vma=False,
    )
```

```python
import jax
import jax.numpy as jnp
from jax import lax
from jax.experimental import pallas as pl
from jax.experimental.pallas import tpu as pltpu
from jax.sharding import Mesh
from jax.sharding import PartitionSpec as P

NOPE = 128
ROPE = 64
VHEAD = 128
RANK = 512
EXPERTS = 8

epsilon = 1e-06
bf16 = jnp.bfloat16
f32 = jnp.float32


def rotate_parts(values, position, inverse):
    half = values.shape[-1] // 2
    freq = jnp.exp(jnp.arange(half, dtype=f32) * (-jnp.log(10000.0) / half))
    angle = position.astype(f32)[:, None] * freq[None, :]
    cosine = jnp.cos(angle)
    sine = jnp.sin(angle)
    if inverse:
        sine = -sine
    if values.ndim == 3:
        cosine = cosine[:, None, :]
        sine = sine[:, None, :]
    first = values[..., :half]
    second = values[..., half:]
    return jnp.concatenate(
        [first * cosine - second * sine, second * cosine + first * sine], axis=-1
    )


def norm_forward(values, gain):
    factor = lax.rsqrt(jnp.mean(values * values, axis=-1, keepdims=True) + epsilon)
    return (values * factor * gain, factor)


def norm_backward(values, factor, gain, grad):
    scaled = grad * gain
    d_values = factor * scaled - values * (factor * factor * factor) * jnp.mean(
        values * scaled, axis=-1, keepdims=True
    )
    d_gain = jnp.sum(grad * values * factor, axis=0)
    return (d_values, d_gain)


def shift(value, axis, step):
    count = lax.axis_size(axis)
    return lax.ppermute(value, axis, [(i, (i + step) % count) for i in range(count)])


def pick(value, place, at):
    return lax.dynamic_index_in_dim(value, place, at, keepdims=False)


def gather_near(value, axis):
    return [value] + [shift(value, axis, s) for s in range(1, lax.axis_size(axis))]


def place_at(parts, axis):
    count = lax.axis_size(axis)
    me = lax.axis_index(axis)
    whole = jnp.zeros((count,) + parts[0].shape, parts[0].dtype)
    for s in range(count):
        at = lax.rem(me - s + count, count)
        whole = lax.dynamic_update_index_in_dim(whole, parts[s], at, 0)
    return whole


def sum_ahead(parts, axis):
    total = parts[0].astype(f32)
    for s in range(1, len(parts)):
        total = total + shift(parts[s], axis, s).astype(f32)
    return total


def sum_at(value, axis, at):
    count = lax.axis_size(axis)
    me = lax.axis_index(axis)
    return sum_ahead([pick(value, lax.rem(me + s, count), at) for s in range(count)], axis)


def dot_nn(a, b):
    return jnp.dot(a, b, preferred_element_type=f32)


def dot_nt(a, b):
    return lax.dot_general(a, b, (((1,), (1,)), ((), ())), preferred_element_type=f32)


def dot_tn(a, b):
    return lax.dot_general(a, b, (((0,), (0,)), ((), ())), preferred_element_type=f32)


def whole(*shape):
    return pl.BlockSpec(shape, lambda *_: (0,) * len(shape))


def corner(value):
    lead = value.ndim - 2
    return pl.BlockSpec((1,) * lead + (16, 128), lambda *_: (0,) * value.ndim)


def without(kernel, count, first):
    def body(*refs):
        return kernel(*refs[:first], *refs[first + count :])

    return body


SCALARS = pl.BlockSpec(memory_space=pltpu.SMEM)
SCALE = (NOPE + ROPE) ** (-0.5)
MIB = 1024 * 1024


def like(*shape, dtype=bf16):
    return jax.ShapeDtypeStruct(shape, dtype)


def run(kernel, place, inputs, outs, after=(), scratch=(), size=40, flops=10**6):
    vmem = pl.BlockSpec(memory_space=pltpu.VMEM)
    lead = [] if place is None else [SCALARS]
    given = [] if place is None else [place]
    moved = sum(v.size * v.dtype.itemsize for v in list(inputs) + list(outs))
    return pl.pallas_call(
        without(kernel, len(after), len(lead) + len(inputs)),
        grid=(1,) if after else (),
        in_specs=lead + [vmem] * len(inputs) + [corner(v) for v in after],
        out_specs=[vmem] * len(outs),
        out_shape=list(outs),
        scratch_shapes=list(scratch),
        compiler_params=pltpu.CompilerParams(vmem_limit_bytes=size * MIB),
        cost_estimate=pl.CostEstimate(flops=flops, bytes_accessed=moved, transcendentals=0),
        name=kernel.__name__.removesuffix("_kernel"),
    )(*given, *inputs, *after)


def enter_kernel(place, tokens, cotangent, routes, tok0, tok1, spread0, spread1):
    for side, tok, spread in ((place[2], tok0, spread0), (1 - place[2], tok1, spread1)):
        tok[...] = tokens[side]
        spread[:, :2048] = cotangent[side]
        named = routes[side]
        lane = lax.broadcasted_iota(jnp.int32, (64, 128), 1) - 66
        chosen = named[:, 0:1] == lane
        for k in range(1, named.shape[1]):
            chosen = chosen | (named[:, k : k + 1] == lane)
        spread[:, 2048:] = chosen.astype(f32).astype(bf16)


def front_kernel(
    place, tok0, tok1, mine, other, cosine, sine,
    normed, packed, compressed, weight, gains, tok,
):
    is_first = place[2] == 0
    tok[:64, :] = jnp.where(is_first, tok0[...], tok1[...])
    tok[64:, :] = jnp.where(is_first, tok1[...], tok0[...])
    for sx in range(4):
        for sz in range(4):
            block = lax.rem(place[0] - sx + 4, 4) * 4 + lax.rem(place[1] - sz + 4, 4)
            for part, core in ((mine, place[2]), (other, 1 - place[2])):
                row = pl.multiple_of(block * 128 + core * 64, 64)
                src = (sx * 4 + sz) * 64
                weight[pl.ds(row, 64), :] = part[src : src + 64, :]
    turned = weight[:, 512:640].astype(f32).T
    gains[0:2, :] = turned[64:66, :]
    latent_gain = jnp.concatenate(
        [turned[74:75, 64 * i : 64 * i + 16] for i in range(32)], axis=1
    )
    gains[2:3, :RANK] = latent_gain
    values = tok[...].astype(f32)
    factor = lax.rsqrt(jnp.mean(values * values, axis=1, keepdims=True) + epsilon)
    low = (values * factor * turned[64:65, :]).astype(bf16)
    normed[...] = low
    raw = dot_nn(low, weight[:, :576])
    compressed[...] = raw
    main = raw[:, :RANK]
    factor = lax.rsqrt(jnp.mean(main * main, axis=1, keepdims=True) + epsilon)
    latent = (main * factor * latent_gain).astype(bf16)
    first, second = raw[:, RANK : RANK + 32], raw[:, RANK + 32 :]
    cos, sin = cosine[:, :32], sine[:, :32]
    rot = jnp.concatenate([first * cos - second * sin, second * cos + first * sin], axis=1)
    packed[:, :RANK] = latent
    packed[:, RANK:] = jnp.concatenate([rot, jnp.zeros((128, 64), f32)], axis=1).astype(bf16)


def expansion(weight):
    blocks = weight[:, 1280:].reshape(32, 4, 16, 256)
    return jnp.concatenate([blocks[:, h].reshape(RANK, 256) for h in range(4)], axis=1)


def turned(rot):
    lane = lax.broadcasted_iota(jnp.int32, rot.shape, 1)
    return jnp.where(lane % 64 < 32, pltpu.roll(rot, 224, 1), pltpu.roll(rot, 32, 1))


def attend_kernel(
    place, normed, weight, cosine, sine, l0, l1, l2, l3, where_q, where_k,
    prob, kv, attended, q, r0, r1, r2, r3, key_rot, total,
):
    expand = expansion(weight)
    for s, part in enumerate((l0, l1, l2, l3)):
        rows = slice(s * 512, s * 512 + 512)
        kv[rows, :] = dot_nn(part[:, :RANK], expand).astype(bf16)
        key_rot[rows, :] = part[:, RANK:]
    nope = dot_nn(normed[...], weight[:, :512]).astype(bf16)
    rot = dot_nn(normed[...], weight[:, 512:768])
    rot = (rot * cosine[...] - turned(rot) * sine[...]).astype(bf16)
    allowed = (where_q[:, 0:1] >= where_k[0:1, :]) & (where_q[:, 1:2] == where_k[1:2, :])
    pad = jnp.zeros((128, 64), bf16)
    for h in range(4):
        at = h * 256
        q_h = jnp.concatenate(
            [nope[:, h * 128 : h * 128 + 128], rot[:, h * 64 : h * 64 + 64], pad], axis=1
        )
        q[:, at : at + 256] = q_h
        key = jnp.concatenate([kv[:, at : at + 128], key_rot[...]], axis=1)
        score = jnp.where(allowed, dot_nt(q_h, key) * SCALE, -1e30)
        power = jnp.exp(score - jnp.max(score, axis=1, keepdims=True))
        low = (power * (1.0 / jnp.sum(power, axis=1, keepdims=True))).astype(bf16)
        prob[h] = low
        attended[:, h * 128 : h * 128 + 128] = dot_nn(low, kv[:, at + 128 : at + 256]).astype(bf16)
    total[...] = dot_nt(attended[...], weight[:, 768:1280]).astype(bf16)
    for s, out in enumerate((r0, r1, r2, r3)):
        row = pl.multiple_of(lax.rem(place[3] + s, 4) * 32, 32)
        out[...] = total[pl.ds(row, 32), :]


def attend(place, normed, parts, attn_all, cosine, sine, where_q, where_k):
    return run(
        attend_kernel,
        place,
        [normed, attn_all, cosine, sine, *parts, where_q, where_k],
        [like(4, 128, 2048), like(2048, 1024), like(128, 512), like(128, 1024)]
        + [like(32, 2048)] * 4,
        scratch=[pltpu.VMEM((2048, 128), bf16), pltpu.VMEM((128, 2048), bf16)],
        size=56,
        flops=5 * 10**9,
    )


def middle_kernel(place, r0, r1, r2, r3, tok, gains, middle, far):
    row = pl.multiple_of(place[3] * 32, 32)
    values = tok[pl.ds(row, 32), :].astype(f32)
    for part in (r0, r1, r2, r3):
        values = values + part[...].astype(f32)
    middle[...] = values
    factor = lax.rsqrt(jnp.mean(values * values, axis=1, keepdims=True) + epsilon)
    far[...] = (values * factor * gains[1:2, :]).astype(bf16)


def middle_back_kernel(
    place, a0, a1, a2, a3, spread, middle, gains, weight, d_mid, d_low, small
):
    row = pl.multiple_of(place[3] * 32, 32)
    total = a0[...].astype(f32)
    for part in (a1, a2, a3):
        total = total + part[...].astype(f32)
    d_normed = total[:, :2048]
    d_gate = total[:, 2048:]
    mine = spread[pl.ds(row, 32), :]
    d_out = mine[:, :2048].astype(f32)
    chosen = mine[:, 2048:].astype(f32)
    values = middle[...]
    gain = gains[1:2, :]
    factor = lax.rsqrt(jnp.mean(values * values, axis=1, keepdims=True) + epsilon)
    low = (values * factor * gain).astype(bf16)
    table = weight[:, 512:640]
    lane = lax.broadcasted_iota(jnp.int32, (32, 128), 1)
    is_expert = (lane >= 66) & (lane < 74)
    logits = jnp.where(is_expert, dot_nn(low, table), -1e30)
    power = jnp.exp(logits - jnp.max(logits, axis=1, keepdims=True))
    router = power / jnp.sum(power, axis=1, keepdims=True)
    d_chosen = d_gate * chosen
    d_logits = router * (d_chosen - jnp.sum(router * d_chosen, axis=1, keepdims=True))
    d_logits = d_logits.astype(bf16)
    d_normed = d_normed + dot_nt(d_logits, table)
    scaled = d_normed * gain
    d_norm = factor * scaled - values * (factor * factor * factor) * jnp.mean(
        values * scaled, axis=1, keepdims=True
    )
    d_values = d_out + d_norm
    d_mid[...] = d_values
    d_low[...] = d_values.astype(bf16)
    terms = (d_normed * values * factor).astype(bf16)
    small[...] = (
        dot_tn(low, d_logits) + dot_tn(terms, (lane == 65).astype(bf16))
    ).astype(bf16)


def latent_back_kernel(
    place, t0, t1, t2, t3, compressed, gains, cosine, sine, d_comp, small
):
    row = pl.multiple_of(place[3] * 32, 32)
    terms = t0[...].astype(f32)
    for part in (t1, t2, t3):
        terms = terms + part[...].astype(f32)
    main = compressed[pl.ds(row, 32), :][:, :RANK]
    factor = lax.rsqrt(jnp.mean(main * main, axis=1, keepdims=True) + epsilon)
    grad_main = terms[:, :RANK]
    scaled = grad_main * gains[2:3, :RANK]
    d_main = factor * scaled - main * (factor * factor * factor) * jnp.mean(
        main * scaled, axis=1, keepdims=True
    )
    first, second = terms[:, RANK : RANK + 32], terms[:, RANK + 32 : RANK + 64]
    cos, sin = cosine[pl.ds(row, 32), :][:, :32], sine[pl.ds(row, 32), :][:, :32]
    rot = jnp.concatenate([first * cos + second * sin, second * cos - first * sin], axis=1)
    d_comp[:, :RANK] = d_main.astype(bf16)
    d_comp[:, RANK:] = jnp.concatenate([rot, jnp.zeros((32, 64), f32)], axis=1).astype(bf16)
    latent_terms = grad_main * main * factor
    gap = jnp.zeros((32, 48), f32)
    latent_terms = jnp.concatenate(
        [p for i in range(32) for p in (latent_terms[:, 16 * i : 16 * i + 16], gap)], axis=1
    )
    lane = lax.broadcasted_iota(jnp.int32, (32, 128), 1)
    small[...] = dot_tn(latent_terms.astype(bf16), (lane == 74).astype(bf16)).astype(bf16)


def token_back_kernel(place, d_comp, q0, q1, q2, q3, tok, gains, weight, d_mid, grad, small):
    row = pl.multiple_of(place[3] * 32, 32)
    d_normed = dot_nt(d_comp[...], weight[:, :640])
    for part in (q0, q1, q2, q3):
        d_normed = d_normed + part[...].astype(f32)
    values = tok[pl.ds(row, 32), :].astype(f32)
    factor = lax.rsqrt(jnp.mean(values * values, axis=1, keepdims=True) + epsilon)
    scaled = d_normed * gains[0:1, :]
    d_norm = factor * scaled - values * (factor * factor * factor) * jnp.mean(
        values * scaled, axis=1, keepdims=True
    )
    grad[...] = (d_mid[...] + d_norm).astype(bf16)
    lane = lax.broadcasted_iota(jnp.int32, (32, 128), 1)
    small[...] = dot_tn(
        (d_normed * values * factor).astype(bf16), (lane == 64).astype(bf16)
    ).astype(bf16)


def compress_grad_kernel(place, c0, c1, c2, c3, normed, s0, s1, s2, mine, other, d_all):
    for s, part in enumerate((c0, c1, c2, c3)):
        row = pl.multiple_of(lax.rem(place[3] - s + 4, 4) * 32, 32)
        d_all[pl.ds(row, 32), :] = part[...]
    column = pl.multiple_of(place[3] * 128, 128)
    own = d_all[:, pl.ds(column, 128)]
    rot = d_all[:, RANK:]
    main = dot_tn(normed[...], own).astype(bf16)
    rest = dot_tn(normed[...], rot)
    for part in (s0, s1, s2):
        rest = rest + part[...].astype(f32)
    rest = rest.astype(bf16)
    is_first = place[2] == 0
    for b in range(16):
        for columns, value in ((slice(0, 128), main), (slice(128, 256), rest)):
            low, high = value[b * 128 : b * 128 + 64], value[b * 128 + 64 : b * 128 + 128]
            mine[b * 64 : b * 64 + 64, columns] = jnp.where(is_first, low, high)
            other[b * 64 : b * 64 + 64, columns] = jnp.where(is_first, high, low)


def attend_back_kernel(
    place, d0, d1, d2, d3, weight, q, kv, prob, l0, l1, l2, l3, cosine, sine,
    d_q, d_rot, d_exp, d_branch, k0, k1, k2, k3, r0, r1, r2, r3, key_rot, rot_sum, total,
):
    for s, part in enumerate((d0, d1, d2, d3)):
        row = pl.multiple_of(lax.rem(place[3] - s + 4, 4) * 32, 32)
        d_branch[pl.ds(row, 32), :] = part[...]
    for s, part in enumerate((l0, l1, l2, l3)):
        key_rot[s * 512 : s * 512 + 512, :] = part[:, RANK:]
    d_att = dot_nn(d_branch[...], weight[:, 768:1280]).astype(bf16)
    rots = []
    for h in range(4):
        at = h * 256
        d_att_h = d_att[:, h * 128 : h * 128 + 128]
        low = prob[h]
        prob_h = low.astype(f32)
        d_prob = dot_nt(d_att_h, kv[:, at + 128 : at + 256])
        row_sum = jnp.sum(prob_h * d_prob, axis=1, keepdims=True)
        d_score = (prob_h * (d_prob - row_sum)).astype(bf16)
        key = jnp.concatenate([kv[:, at : at + 128], key_rot[...]], axis=1)
        d_query = dot_nn(d_score, key) * SCALE
        d_q[:, h * 128 : h * 128 + 128] = d_query[:, :128].astype(bf16)
        rots.append(d_query[:, 128:192])
        d_key = dot_tn(d_score, q[:, at : at + 256]) * SCALE
        d_exp[:, at : at + 128] = d_key[:, :128].astype(bf16)
        d_exp[:, at + 128 : at + 256] = dot_tn(low, d_att_h).astype(bf16)
        if h == 0:
            rot_sum[...] = d_key[:, 128:]
        else:
            rot_sum[...] += d_key[:, 128:]
    expand = expansion(weight)
    for s, out in enumerate((k0, k1, k2, k3)):
        rows = slice(s * 512, s * 512 + 512)
        out[:, :RANK] = dot_nt(d_exp[rows, :], expand).astype(bf16)
        out[:, RANK:] = rot_sum[rows, :].astype(bf16)
    rot = jnp.concatenate(rots, axis=1)
    rot = (rot * cosine[...] + turned(rot) * sine[...]).astype(bf16)
    d_rot[...] = rot
    total[...] = (dot_nt(d_q[...], weight[:, :512]) + dot_nt(rot, weight[:, 512:768])).astype(bf16)
    for s, out in enumerate((r0, r1, r2, r3)):
        row = pl.multiple_of(lax.rem(place[3] + s, 4) * 32, 32)
        out[...] = total[pl.ds(row, 32), :]


def attend_back(place, parts, q, kv, prob, latents, attn_all, cosine, sine, after):
    return run(
        attend_back_kernel,
        place,
        [*parts, attn_all, q, kv, prob, *latents, cosine, sine],
        [like(128, 512), like(128, 256), like(2048, 1024), like(128, 2048)]
        + [like(512, 640)] * 4
        + [like(32, 2048)] * 4,
        after=after,
        scratch=[
            pltpu.VMEM((2048, 128), bf16),
            pltpu.VMEM((2048, 128), f32),
            pltpu.VMEM((128, 2048), bf16),
        ],
        flops=8 * 10**9,
    )


PARTS = 1


def expert_kernel(place, far, spread, weight, d_far, d_hidden, hidden, out):
    expert = 2 * place[1] + place[2]
    for part in range(PARTS):
        at = slice(part * 512 // PARTS, (part + 1) * 512 // PARTS)
        raw = dot_nn(far[at, :], weight[:, :896])
        d_weighted = dot_nn(spread[at, :2048], weight[:, 896:])
        rows = raw.shape[0]
        logits = raw[:, 880:888]
        power = jnp.exp(logits - jnp.max(logits, axis=1, keepdims=True))
        router = power / jnp.sum(power, axis=1, keepdims=True)
        is_mine = lax.broadcasted_iota(jnp.int32, (rows, 8), 1) == expert
        chosen = spread[at, 2048:2176][:, 66:74].astype(f32)
        gate = jnp.sum(jnp.where(is_mine, router * chosen, 0.0), axis=1, keepdims=True)
        routed = lax.broadcasted_iota(jnp.int32, (rows, 440), 1) < 352
        gate = jnp.where(routed, gate, 1.0)
        low, upper = raw[:, :440], raw[:, 440:880]
        sigma = 1.0 / (1.0 + jnp.exp(-low))
        silu = low * sigma
        slope = sigma + silu * (1.0 - sigma)
        act = silu * upper
        weighted = (gate * act).astype(bf16)
        d_gate = jnp.sum(jnp.where(routed, d_weighted * act, 0.0), axis=1, keepdims=True)
        d_act = d_weighted * gate
        d_up = jnp.concatenate(
            [d_act * upper * slope, d_act * silu, jnp.zeros((rows, 16), f32)], axis=1
        ).astype(bf16)
        d_hidden[at, :] = d_up
        hidden[at, :] = jnp.concatenate([weighted, jnp.zeros((rows, 72), bf16)], axis=1)
        d_far[at, :2048] = dot_nt(d_up, weight[:, :896]).astype(bf16)
        lane = lax.broadcasted_iota(jnp.int32, (rows, 128), 1)
        d_far[at, 2048:] = jnp.where(lane == expert + 66, d_gate, 0.0).astype(bf16)
        out[at, :] = dot_nt(weighted, weight[:, 896:]).astype(bf16)


def expert(place, far, spread, weight):
    return run(
        expert_kernel,
        place,
        [far, spread, weight],
        [like(512, 2176), like(512, 896), like(512, 512), like(512, 2048)],
        flops=6 * 10**9,
    )


def expert_grad_kernel(x0, x1, y0, y1, d0, d1, h0, h1, out):
    out[:, :896] = (dot_tn(x0[...], d0[...]) + dot_tn(x1[...], d1[...])).astype(bf16)
    down = dot_tn(y0[...], h0[...]) + dot_tn(y1[...], h1[...])
    out[:, 896:] = down[:, :440].astype(bf16)


def expert_grad(fars, spreads, d_hiddens, hiddens, after):
    columns = pl.BlockSpec((512, 512), lambda i: (0, i))
    return pl.pallas_call(
        without(expert_grad_kernel, len(after), 8),
        grid=(4,),
        in_specs=[columns] * 4
        + [whole(512, 896)] * 2
        + [whole(512, 512)] * 2
        + [corner(v) for v in after],
        out_specs=pl.BlockSpec((512, 1336), lambda i: (i, 0)),
        out_shape=like(2048, 1336),
        compiler_params=pltpu.CompilerParams(vmem_limit_bytes=40 * MIB),
        cost_estimate=pl.CostEstimate(
            flops=6 * 10**9, bytes_accessed=18 * 10**6, transcendentals=0
        ),
        name="expert_grad",
    )(*fars, *spreads, *d_hiddens, *hiddens, *after)


def attn_grad_kernel(normed, d_q, d_rot, d_branch, attended, l0, l1, l2, l3, d_exp, out):
    g_exp = 0.0
    for s, part in enumerate((l0, l1, l2, l3)):
        g_exp = g_exp + dot_tn(part[:, :RANK], d_exp[s * 512 : s * 512 + 512, :])
    g_exp = g_exp.astype(bf16)
    out[:, :512] = dot_tn(normed[...], d_q[...]).astype(bf16)
    out[:, 512:768] = dot_tn(normed[...], d_rot[...]).astype(bf16)
    out[:, 768:1280] = dot_tn(d_branch[...], attended[...]).astype(bf16)
    for d in range(32):
        for h in range(4):
            to = d * 64 + h * 16
            out[to : to + 16, 1280:] = g_exp[d * 16 : d * 16 + 16, h * 256 : h * 256 + 256]


def attn_grad(normed, d_q, d_rot, d_branch, attended, latents, d_exp, after):
    return run(
        attn_grad_kernel,
        None,
        [normed, d_q, d_rot, d_branch, attended, *latents, d_exp],
        [like(2048, 1536)],
        after=after,
        size=56,
        flops=4 * 10**9,
    )[0]


def pack_expert_kernel(
    place, expert_in, expert_out, shared_in, shared_out, router, mine, send
):
    is_first = place[2] == 0
    gap = jnp.zeros((64, 8), f32)
    for z in range(4):
        both = []
        for core in range(2):
            expert = 2 * z + core
            cut = slice(88 * expert, 88 * expert + 88)
            parts = [
                expert_in[:, expert, 0, :],
                shared_in[:, 0, cut],
                expert_in[:, expert, 1, :],
                shared_in[:, 1, cut],
                router[...],
                gap,
                expert_out[:, expert, :],
                shared_out[:, cut],
            ]
            both.append(jnp.concatenate([part.astype(f32) for part in parts], axis=1))
        mine[z] = jnp.where(is_first, both[0], both[1]).astype(bf16)
        send[z] = jnp.where(is_first, both[1], both[0]).astype(bf16)


def pair_kernel(place, mine, other, p0, p1, p2, p3):
    is_first = place[2] == 0
    for s, out in enumerate((p0, p1, p2, p3)):
        to = lax.rem(place[1] + s, 4)
        a, b = mine[to], other[to]
        out[:64, :] = jnp.where(is_first, a, b)
        out[64:, :] = jnp.where(is_first, b, a)


def turn_kernel(place, mine, other, natural, out):
    is_first = place[2] == 0
    natural[:64, :] = jnp.where(is_first, mine[...], other[...])
    natural[64:, :] = jnp.where(is_first, other[...], mine[...])
    for s in range(4):
        row = pl.multiple_of(lax.rem(place[3] - s + 4, 4) * 32, 32)
        out[s * 32 : s * 32 + 32, :] = natural[pl.ds(row, 32), :]


def stack_kernel(p0, p1, p2, p3, out):
    rows = p0.shape[0]
    for s, part in enumerate((p0, p1, p2, p3)):
        out[s * rows : s * rows + rows, :] = part[...]


def add_split_kernel(mine, other, *outs):
    rows = outs[0].shape[0]
    for s, out in enumerate(outs):
        at = slice(s * rows, s * rows + rows)
        out[...] = (mine[at, :].astype(f32) + other[at, :].astype(f32)).astype(bf16)


def sum_split_kernel(v0, v1, v2, v3, *outs):
    rows = outs[0].shape[0]
    for s, out in enumerate(outs):
        at = slice(s * rows, s * rows + rows)
        total = v0[at, :].astype(f32)
        for part in (v1, v2, v3):
            total = total + part[at, :].astype(f32)
        out[...] = total.astype(bf16)


def row_sum_kernel(place, v0, v1, v2, v3, *outs):
    for s, out in enumerate(outs):
        rows = pl.ds(pl.multiple_of(lax.rem(place[3] + s, 4) * 32, 32), 32)
        total = v0[rows, :].astype(f32)
        for part in (v1, v2, v3):
            total = total + part[rows, :].astype(f32)
        out[...] = total.astype(bf16)


def out_rows_kernel(v0, v1, v2, v3, middle, out):
    total = v0[...].astype(f32)
    for part in (v1, v2, v3):
        total = total + part[...].astype(f32)
    out[...] = (middle[...] + total).astype(bf16)


def cut_kernel(place, value, p0, p1, p2, p3):
    for s, out in enumerate((p0, p1, p2, p3)):
        rows = pl.ds(pl.multiple_of(lax.rem(place[1] + s, 4) * 128, 128), 128)
        out[...] = value[rows, :]


def join_kernel(place, p0, p1, p2, p3, out):
    for s, part in enumerate((p0, p1, p2, p3)):
        rows = pl.ds(pl.multiple_of(lax.rem(place[1] - s + 4, 4) * 128, 128), 128)
        out[rows, :] = part[...]


def pack_attn_kernel(query, output, expand, out):
    value = query[...]
    out[:, :512] = jnp.concatenate([value[:, 192 * h : 192 * h + 128] for h in range(4)], axis=1)
    out[:, 512:768] = jnp.concatenate(
        [value[:, 192 * h + 128 : 192 * h + 192] for h in range(4)], axis=1
    )
    out[:, 768:1280] = output[...]
    for h in range(4):
        out[h * 16 : h * 16 + 16, 1280:] = expand[:, h * 256 : h * 256 + 256]


def by_core_kernel(place, p0, p1, p2, p3, mine, other):
    is_first = place[2] == 0
    for s, part in enumerate((p0, p1, p2, p3)):
        at = lax.rem(place[1] - s + 4, 4)
        low, high = part[:64, :], part[64:, :]
        mine[at] = jnp.where(is_first, low, high)
        other[at] = jnp.where(is_first, high, low)


def unpack_kernel(place, mine, other, expert_in, expert_out, shared_in, shared_out):
    is_first = place[2] == 0
    ins, outs, downs = [], [], []
    for x in range(4):
        for core in range(2):
            a, b = (mine[x], other[x]) if core == 0 else (other[x], mine[x])
            value = jnp.where(is_first, a, b).astype(f32)
            expert = 2 * x + core
            expert_in[:, expert, 0, :] = value[:, :352]
            expert_in[:, expert, 1, :] = value[:, 440:792]
            expert_out[:, expert, :] = value[:, 896:1248]
            ins.append(value[:, 352:440])
            outs.append(value[:, 792:880])
            downs.append(value[:, 1248:])
    shared_in[:, 0, :] = jnp.concatenate(ins, axis=1)
    shared_in[:, 1, :] = jnp.concatenate(outs, axis=1)
    shared_out[...] = jnp.concatenate(downs, axis=1)


def finish_kernel(total, query, output, expand):
    value = total[...].astype(f32)
    query[...] = jnp.concatenate(
        [
            p
            for h in range(4)
            for p in (
                value[:, h * 128 : h * 128 + 128],
                value[:, 512 + h * 64 : 576 + h * 64],
            )
        ],
        axis=1,
    )
    output[...] = value[:, 768:1280]
    for h in range(4):
        expand[:, h * 256 : h * 256 + 256] = value[h * 16 : h * 16 + 16, 1280:]


def on_device(
    tokens,
    segment,
    routes,
    cotangent,
    gain_attn,
    w_query,
    w_compress,
    gain_latent,
    w_expand,
    w_output,
    gain_ffn,
    w_router,
    w_expert_in,
    w_expert_out,
    w_shared_in,
    w_shared_out,
):
    xi, zi, ci, yi = (lax.axis_index(a) for a in ("x", "z", "c", "y"))
    place = jnp.stack([xi, zi, ci, yi]).astype(jnp.int32)
    is_first = ci == 0
    heads = 4
    dim = 2048

    def leave(value):
        halves = value.reshape((2, 64) + value.shape[1:])
        mine, other = pick(halves, ci, 0), shift(pick(halves, 1 - ci, 0), "c", 1)
        return jnp.stack([jnp.where(is_first, mine, other), jnp.where(is_first, other, mine)])

    small = jnp.concatenate(
        [
            w_compress,
            gain_attn[:, None],
            gain_ffn[:, None],
            w_router,
            jnp.pad(gain_latent, (0, 48))[:, None],
            jnp.zeros((64, 53), bf16),
        ],
        axis=1,
    )
    small_z_parts = gather_near(small, "z")
    (small_z,) = run(stack_kernel, None, small_z_parts, [like(256, 640)])
    small_x = gather_near(small_z, "x")
    (small_mine,) = run(stack_kernel, None, small_x, [like(1024, 640)])
    small_other = shift(small_mine, "c", 1)

    mine_w, send_w = run(
        pack_expert_kernel,
        place,
        [w_expert_in, w_expert_out, w_shared_in, w_shared_out, w_router],
        [like(4, 64, 1336)] * 2,
        after=small_z_parts[1:],
    )
    other_w = shift(send_w, "c", 1)

    tok_mine, tok_send, spread_mine, spread_send = run(
        enter_kernel,
        place,
        [tokens, cotangent, routes],
        [like(64, 2048), like(64, 2048), like(64, 2176), like(64, 2176)],
    )
    tok_other = shift(tok_send, "c", 1)
    spread_other = shift(spread_send, "c", 1)

    position = (xi * 4 + zi) * 128 + jnp.arange(128, dtype=jnp.int32)
    segment_row = pick(segment, ci, 0)
    blocks = jnp.stack(
        [lax.rem(xi - sx + 4, 4) * 4 + lax.rem(zi - sz + 4, 4) for sx in range(4) for sz in range(4)]
    )
    segment_near = segment_row.reshape(16, 128)[blocks].reshape(2048)
    key_place = (blocks[:, None] * 128 + jnp.arange(128, dtype=jnp.int32)[None, :]).reshape(2048)
    where_k = jnp.stack([key_place, segment_near])
    where_q = jnp.stack(
        [position, lax.dynamic_slice_in_dim(segment_row, (xi * 4 + zi) * 128, 128)], axis=1
    )
    lane = jnp.arange(256)[None, :]
    freq = jnp.exp((lane % 32).astype(f32) * (-jnp.log(10000.0) / 32))
    angle = position.astype(f32)[:, None] * freq
    cosine = jnp.cos(angle)
    sine = jnp.where(lane % 64 < 32, 1.0, -1.0) * jnp.sin(angle)

    pair_w = run(pair_kernel, place, [mine_w, other_w], [like(128, 1336)] * 4)
    pair_w = [pair_w[0]] + [shift(pair_w[s], "z", s) for s in range(1, 4)]
    (attn_w,) = run(
        pack_attn_kernel,
        None,
        [w_query, w_output, w_expand],
        [like(64, 1536)],
        after=small_x[1:] + pair_w[1:],
    )
    (expert_w,) = run(join_kernel, place, pair_w, [like(512, 1336)], after=[attn_w])
    attn_all = lax.all_gather(attn_w, ("x", "z", "c"), axis=0, tiled=True)
    ffn_all = lax.all_gather(expert_w, "x", axis=0, tiled=True)

    normed, packed, compressed, weight, gains, tok = run(
        front_kernel,
        place,
        [tok_mine, tok_other, small_mine, small_other, cosine, sine],
        [
            like(128, 2048),
            like(128, 640),
            like(128, 576, dtype=f32),
            like(2048, 640),
            like(8, 2048, dtype=f32),
            like(128, 2048),
        ],
    )
    (latent_near,) = run(stack_kernel, None, gather_near(packed, "z"), [like(512, 640)])
    latents = gather_near(latent_near, "x")
    spread_here, spread = run(
        turn_kernel,
        place,
        [spread_mine, spread_other],
        [like(128, 2176)] * 2,
        after=latents[1:2],
    )
    spread = gather_near(spread, "z")
    prob, kv, attended, query, *branch = attend(
        place, normed, latents, attn_all, cosine, sine, where_q, where_k
    )
    branch = [branch[0]] + [shift(branch[s], "y", s) for s in range(1, 4)]
    (spread,) = run(stack_kernel, None, spread, [like(512, 2176)], after=[attended])
    spread_other = shift(spread, "c", 1)
    middle, far = run(
        middle_kernel,
        place,
        [*branch, tok, gains],
        [like(32, 2048, dtype=f32), like(32, 2048)],
        after=[spread],
    )

    (far,) = run(stack_kernel, None, gather_near(far, "y"), [like(128, 2048)])
    (far,) = run(stack_kernel, None, gather_near(far, "z"), [like(512, 2048)])
    far_other = shift(far, "c", 1)
    d_far2, d_hidden2, hidden2, out_far2 = expert(place, far_other, spread_other, ffn_all)
    d_far, d_hidden, hidden, out_far = expert(place, far, spread, ffn_all)
    d_far = run(
        add_split_kernel, None, [d_far, shift(d_far2, "c", 1)], [like(128, 2176)] * 4
    )
    d_far = [d_far[0]] + [shift(d_far[s], "z", -s) for s in range(1, 4)]
    d_far = run(sum_split_kernel, None, d_far, [like(32, 2176)] * 4)
    grad_ffn = expert_grad(
        (far, far_other), (spread, spread_other), (d_hidden, d_hidden2), (hidden, hidden2), d_far[:1]
    )
    grad_ffn = lax.psum_scatter(grad_ffn, "x", scatter_dimension=0, tiled=True)
    d_far = [d_far[0]] + [shift(d_far[s], "y", -s) for s in range(1, 4)]
    d_mid, d_low, small_a = run(
        middle_back_kernel,
        place,
        [*d_far, spread_here, middle, gains, weight],
        [like(32, 2048, dtype=f32), like(32, 2048), like(2048, 128)],
    )
    out_far = run(
        add_split_kernel,
        None,
        [out_far, shift(out_far2, "c", 1)],
        [like(128, 2048)] * 4,
        after=d_far[:1],
    )
    out_far = [out_far[0]] + [shift(out_far[s], "z", -s) for s in range(1, 4)]
    d_low = gather_near(d_low, "y")

    d_q, d_rot, d_expanded, d_branch, *rest = attend_back(
        place, d_low, query, kv, prob, latents, attn_all, cosine, sine, out_far[1:]
    )
    terms = [rest[0]] + [shift(rest[s], "x", -s) for s in range(1, 4)]
    d_queries = [rest[4]] + [shift(rest[4 + s], "y", s) for s in range(1, 4)]
    grad_ffn = run(cut_kernel, place, [grad_ffn], [like(128, 1336)] * 4)
    grad_ffn = [grad_ffn[0]] + [shift(grad_ffn[s], "z", s) for s in range(1, 4)]
    terms = run(
        sum_split_kernel, None, terms, [like(128, 640)] * 4, after=grad_ffn[1:]
    )
    out_far = run(sum_split_kernel, None, out_far, [like(32, 2048)] * 4, after=terms[:1])
    out_far = [out_far[0]] + [shift(out_far[s], "y", -s) for s in range(1, 4)]
    mine_g, other_g = run(by_core_kernel, place, grad_ffn, [like(4, 64, 1336)] * 2)
    terms = [terms[0]] + [shift(terms[s], "z", -s) for s in range(1, 4)]
    terms = run(
        row_sum_kernel, place, terms, [like(32, 640)] * 4, after=out_far[1:] + [mine_g]
    )
    terms = [terms[0]] + [shift(terms[s], "y", s) for s in range(1, 4)]
    (mixed,) = run(out_rows_kernel, None, [*out_far, middle], [like(32, 2048)], after=terms[:1])
    mixed = gather_near(mixed, "y")

    d_comp, small_b = run(
        latent_back_kernel,
        place,
        [*terms, compressed, gains, cosine, sine],
        [like(32, 640), like(2048, 128)],
        after=mixed[1:],
    )
    g_expert_in, g_expert_out, g_shared_in, g_shared_out = run(
        unpack_kernel,
        place,
        [mine_g, shift(other_g, "c", 1)],
        [
            like(64, 8, 2, 352, dtype=f32),
            like(64, 8, 352, dtype=f32),
            like(64, 2, 704, dtype=f32),
            like(64, 704, dtype=f32),
        ],
    )
    grad_rows, small_c = run(
        token_back_kernel,
        place,
        [d_comp, *d_queries, tok, gains, weight, d_mid],
        [like(32, 2048), like(2048, 128)],
    )
    grad_rows = leave(place_at(gather_near(grad_rows, "y"), "y").reshape(128, dim))
    mixed = leave(place_at(mixed, "y").reshape(128, dim))

    def fsdp_sum(mine, other, cuts):
        value = (mine.astype(f32) + shift(other, "c", 1).astype(f32)).astype(bf16)
        value = value.reshape(4, 4, 64, -1)
        done = []
        for start, stop, first, second in cuts:
            part = sum_at(value[..., start:stop], first, 0 if first == "x" else 1).astype(bf16)
            done.append(sum_at(part, second, 0))
        return done

    g_attn = attn_grad(normed, d_q, d_rot, d_branch, attended, latents, d_expanded, [])
    g_attn = lax.psum_scatter(g_attn, ("x", "z", "c"), scatter_dimension=0, tiled=True)
    g_mine, g_other = run(
        compress_grad_kernel,
        place,
        [*gather_near(d_comp, "y"), normed, small_a, small_b, small_c],
        [like(1024, 256)] * 2,
        scratch=[pltpu.VMEM((128, 640), bf16)],
    )
    (g_small,) = fsdp_sum(g_mine, g_other, ((0, 256, "x", "z"),))
    g_small = g_small.astype(bf16)
    g_parts = gather_near(g_small, "y")
    g_query, g_output, g_expand = run(
        finish_kernel,
        None,
        [g_attn],
        [like(64, 768, dtype=f32), like(64, 512, dtype=f32), like(16, 1024, dtype=f32)],
        after=g_parts[1:] + [g_shared_out],
    )
    g_small = place_at(g_parts, "y")
    g_small = g_small.astype(f32)
    g_compress = jnp.concatenate(
        [g_small[i, :, :128] for i in range(4)] + [g_small[0, :, 128:192]], axis=1
    )
    g_small = jnp.sum(g_small[:, :, 192:], axis=0)

    return (
        mixed,
        grad_rows,
        g_small[:, 0],
        g_query,
        g_compress,
        g_small[:16, 10],
        g_expand,
        g_output,
        g_small[:, 1],
        g_small[:, 2:10],
        g_expert_in,
        g_expert_out,
        g_shared_in,
        g_shared_out,
    )


def solution(mesh):
    fine = Mesh(mesh.devices.reshape(4, 4, 2, 4), ("x", "z", "c", "y"))
    rows = ("x", "z", "c")
    return jax.shard_map(
        on_device,
        mesh=fine,
        in_specs=(
            P(None, rows, None),
            P(),
            P(None, rows, None),
            P(None, rows, None),
            P(rows),
            P(rows, "y"),
            P(rows, None),
            P(rows),
            P(rows, "y"),
            P(rows, "y"),
            P(rows),
            P(rows, None),
            P(rows, None, None, "y"),
            P(rows, None, "y"),
            P(rows, None, "y"),
            P(rows, "y"),
        ),
        out_specs=(
            P(None, rows, None),
            P(None, rows, None),
            P(rows),
            P(rows, "y"),
            P(rows, None),
            P(rows),
            P(rows, "y"),
            P(rows, "y"),
            P(rows),
            P(rows, None),
            P(rows, None, None, "y"),
            P(rows, None, "y"),
            P(rows, None, "y"),
            P(rows, "y"),
        ),
        check_vma=False,
    )
```

```python
import jax
import jax.numpy as jnp
from jax import lax
from jax.experimental import pallas as pl
from jax.experimental.pallas import tpu as pltpu
from jax.sharding import Mesh
from jax.sharding import PartitionSpec as P

NOPE = 128
ROPE = 64
VHEAD = 128
RANK = 512
EXPERTS = 8

epsilon = 1e-06
bf16 = jnp.bfloat16
f32 = jnp.float32


def rotate_parts(values, position, inverse):
    half = values.shape[-1] // 2
    freq = jnp.exp(jnp.arange(half, dtype=f32) * (-jnp.log(10000.0) / half))
    angle = position.astype(f32)[:, None] * freq[None, :]
    cosine = jnp.cos(angle)
    sine = jnp.sin(angle)
    if inverse:
        sine = -sine
    if values.ndim == 3:
        cosine = cosine[:, None, :]
        sine = sine[:, None, :]
    first = values[..., :half]
    second = values[..., half:]
    return jnp.concatenate(
        [first * cosine - second * sine, second * cosine + first * sine], axis=-1
    )


def norm_forward(values, gain):
    factor = lax.rsqrt(jnp.mean(values * values, axis=-1, keepdims=True) + epsilon)
    return (values * factor * gain, factor)


def norm_backward(values, factor, gain, grad):
    scaled = grad * gain
    d_values = factor * scaled - values * (factor * factor * factor) * jnp.mean(
        values * scaled, axis=-1, keepdims=True
    )
    d_gain = jnp.sum(grad * values * factor, axis=0)
    return (d_values, d_gain)


def shift(value, axis, step):
    count = lax.axis_size(axis)
    return lax.ppermute(value, axis, [(i, (i + step) % count) for i in range(count)])


def pick(value, place, at):
    return lax.dynamic_index_in_dim(value, place, at, keepdims=False)


def gather_near(value, axis):
    return [value] + [shift(value, axis, s) for s in range(1, lax.axis_size(axis))]


def place_at(parts, axis):
    count = lax.axis_size(axis)
    me = lax.axis_index(axis)
    whole = jnp.zeros((count,) + parts[0].shape, parts[0].dtype)
    for s in range(count):
        at = lax.rem(me - s + count, count)
        whole = lax.dynamic_update_index_in_dim(whole, parts[s], at, 0)
    return whole


def sum_ahead(parts, axis):
    total = parts[0].astype(f32)
    for s in range(1, len(parts)):
        total = total + shift(parts[s], axis, s).astype(f32)
    return total


def sum_at(value, axis, at):
    count = lax.axis_size(axis)
    me = lax.axis_index(axis)
    return sum_ahead([pick(value, lax.rem(me + s, count), at) for s in range(count)], axis)


def dot_nn(a, b):
    return jnp.dot(a, b, preferred_element_type=f32)


def dot_nt(a, b):
    return lax.dot_general(a, b, (((1,), (1,)), ((), ())), preferred_element_type=f32)


def dot_tn(a, b):
    return lax.dot_general(a, b, (((0,), (0,)), ((), ())), preferred_element_type=f32)


def whole(*shape):
    return pl.BlockSpec(shape, lambda *_: (0,) * len(shape))


def corner(value):
    lead = value.ndim - 2
    return pl.BlockSpec((1,) * lead + (16, 128), lambda *_: (0,) * value.ndim)


def without(kernel, count, first):
    def body(*refs):
        return kernel(*refs[:first], *refs[first + count :])

    return body


SCALARS = pl.BlockSpec(memory_space=pltpu.SMEM)
SCALE = (NOPE + ROPE) ** (-0.5)
MIB = 1024 * 1024


def like(*shape, dtype=bf16):
    return jax.ShapeDtypeStruct(shape, dtype)


def run(kernel, place, inputs, outs, after=(), scratch=(), size=40, flops=10**6):
    vmem = pl.BlockSpec(memory_space=pltpu.VMEM)
    lead = [] if place is None else [SCALARS]
    given = [] if place is None else [place]
    moved = sum(v.size * v.dtype.itemsize for v in list(inputs) + list(outs))
    return pl.pallas_call(
        without(kernel, len(after), len(lead) + len(inputs)),
        grid=(1,) if after else (),
        in_specs=lead + [vmem] * len(inputs) + [corner(v) for v in after],
        out_specs=[vmem] * len(outs),
        out_shape=list(outs),
        scratch_shapes=list(scratch),
        compiler_params=pltpu.CompilerParams(vmem_limit_bytes=size * MIB),
        cost_estimate=pl.CostEstimate(flops=flops, bytes_accessed=moved, transcendentals=0),
        name=kernel.__name__.removesuffix("_kernel"),
    )(*given, *inputs, *after)


def enter_kernel(place, tokens, cotangent, routes, tok0, tok1, spread0, spread1):
    for side, tok, spread in ((place[2], tok0, spread0), (1 - place[2], tok1, spread1)):
        tok[...] = tokens[side]
        spread[:, :2048] = cotangent[side]
        named = routes[side]
        lane = lax.broadcasted_iota(jnp.int32, (64, 128), 1) - 66
        chosen = named[:, 0:1] == lane
        for k in range(1, named.shape[1]):
            chosen = chosen | (named[:, k : k + 1] == lane)
        spread[:, 2048:] = chosen.astype(f32).astype(bf16)


def front_kernel(
    place, tok0, tok1, mine, other, cosine, sine,
    normed, packed, compressed, weight, gains, tok,
):
    is_first = place[2] == 0
    tok[:64, :] = jnp.where(is_first, tok0[...], tok1[...])
    tok[64:, :] = jnp.where(is_first, tok1[...], tok0[...])
    for sx in range(4):
        for sz in range(4):
            block = lax.rem(place[0] - sx + 4, 4) * 4 + lax.rem(place[1] - sz + 4, 4)
            for part, core in ((mine, place[2]), (other, 1 - place[2])):
                row = pl.multiple_of(block * 128 + core * 64, 64)
                src = (sx * 4 + sz) * 64
                weight[pl.ds(row, 64), :] = part[src : src + 64, :]
    turned = weight[:, 512:640].astype(f32).T
    gains[0:2, :] = turned[64:66, :]
    latent_gain = jnp.concatenate(
        [turned[74:75, 64 * i : 64 * i + 16] for i in range(32)], axis=1
    )
    gains[2:3, :RANK] = latent_gain
    values = tok[...].astype(f32)
    factor = lax.rsqrt(jnp.mean(values * values, axis=1, keepdims=True) + epsilon)
    low = (values * factor * turned[64:65, :]).astype(bf16)
    normed[...] = low
    raw = dot_nn(low, weight[:, :576])
    compressed[...] = raw
    main = raw[:, :RANK]
    factor = lax.rsqrt(jnp.mean(main * main, axis=1, keepdims=True) + epsilon)
    latent = (main * factor * latent_gain).astype(bf16)
    first, second = raw[:, RANK : RANK + 32], raw[:, RANK + 32 :]
    cos, sin = cosine[:, :32], sine[:, :32]
    rot = jnp.concatenate([first * cos - second * sin, second * cos + first * sin], axis=1)
    packed[:, :RANK] = latent
    packed[:, RANK:] = jnp.concatenate([rot, jnp.zeros((128, 64), f32)], axis=1).astype(bf16)


def expansion(weight):
    blocks = weight[:, 1280:].reshape(32, 4, 16, 256)
    return jnp.concatenate([blocks[:, h].reshape(RANK, 256) for h in range(4)], axis=1)


def turned(rot):
    lane = lax.broadcasted_iota(jnp.int32, rot.shape, 1)
    return jnp.where(lane % 64 < 32, pltpu.roll(rot, 224, 1), pltpu.roll(rot, 32, 1))


def attend_kernel(
    place, normed, weight, cosine, sine, l0, l1, l2, l3, where_q, where_k,
    prob, kv, attended, q, r0, r1, r2, r3, key_rot, total,
):
    expand = expansion(weight)
    for s, part in enumerate((l0, l1, l2, l3)):
        rows = slice(s * 512, s * 512 + 512)
        kv[rows, :] = dot_nn(part[:, :RANK], expand).astype(bf16)
        key_rot[rows, :] = part[:, RANK:]
    nope = dot_nn(normed[...], weight[:, :512]).astype(bf16)
    rot = dot_nn(normed[...], weight[:, 512:768])
    rot = (rot * cosine[...] - turned(rot) * sine[...]).astype(bf16)
    allowed = (where_q[:, 0:1] >= where_k[0:1, :]) & (where_q[:, 1:2] == where_k[1:2, :])
    pad = jnp.zeros((128, 64), bf16)
    for h in range(4):
        at = h * 256
        q_h = jnp.concatenate(
            [nope[:, h * 128 : h * 128 + 128], rot[:, h * 64 : h * 64 + 64], pad], axis=1
        )
        q[:, at : at + 256] = q_h
        key = jnp.concatenate([kv[:, at : at + 128], key_rot[...]], axis=1)
        score = jnp.where(allowed, dot_nt(q_h, key) * SCALE, -1e30)
        power = jnp.exp(score - jnp.max(score, axis=1, keepdims=True))
        low = (power * (1.0 / jnp.sum(power, axis=1, keepdims=True))).astype(bf16)
        prob[h] = low
        attended[:, h * 128 : h * 128 + 128] = dot_nn(low, kv[:, at + 128 : at + 256]).astype(bf16)
    total[...] = dot_nt(attended[...], weight[:, 768:1280]).astype(bf16)
    for s, out in enumerate((r0, r1, r2, r3)):
        row = pl.multiple_of(lax.rem(place[3] + s, 4) * 32, 32)
        out[...] = total[pl.ds(row, 32), :]


def attend(place, normed, parts, attn_all, cosine, sine, where_q, where_k):
    return run(
        attend_kernel,
        place,
        [normed, attn_all, cosine, sine, *parts, where_q, where_k],
        [like(4, 128, 2048), like(2048, 1024), like(128, 512), like(128, 1024)]
        + [like(32, 2048)] * 4,
        scratch=[pltpu.VMEM((2048, 128), bf16), pltpu.VMEM((128, 2048), bf16)],
        size=56,
        flops=5 * 10**9,
    )


def middle_kernel(place, r0, r1, r2, r3, tok, gains, middle, far):
    row = pl.multiple_of(place[3] * 32, 32)
    values = tok[pl.ds(row, 32), :].astype(f32)
    for part in (r0, r1, r2, r3):
        values = values + part[...].astype(f32)
    middle[...] = values
    factor = lax.rsqrt(jnp.mean(values * values, axis=1, keepdims=True) + epsilon)
    far[...] = (values * factor * gains[1:2, :]).astype(bf16)


def middle_back_kernel(
    place, a0, a1, a2, a3, spread, middle, gains, weight, d_mid, d_low, small
):
    row = pl.multiple_of(place[3] * 32, 32)
    total = a0[...].astype(f32)
    for part in (a1, a2, a3):
        total = total + part[...].astype(f32)
    d_normed = total[:, :2048]
    d_gate = total[:, 2048:]
    mine = spread[pl.ds(row, 32), :]
    d_out = mine[:, :2048].astype(f32)
    chosen = mine[:, 2048:].astype(f32)
    values = middle[...]
    gain = gains[1:2, :]
    factor = lax.rsqrt(jnp.mean(values * values, axis=1, keepdims=True) + epsilon)
    low = (values * factor * gain).astype(bf16)
    table = weight[:, 512:640]
    lane = lax.broadcasted_iota(jnp.int32, (32, 128), 1)
    is_expert = (lane >= 66) & (lane < 74)
    logits = jnp.where(is_expert, dot_nn(low, table), -1e30)
    power = jnp.exp(logits - jnp.max(logits, axis=1, keepdims=True))
    router = power / jnp.sum(power, axis=1, keepdims=True)
    d_chosen = d_gate * chosen
    d_logits = router * (d_chosen - jnp.sum(router * d_chosen, axis=1, keepdims=True))
    d_logits = d_logits.astype(bf16)
    d_normed = d_normed + dot_nt(d_logits, table)
    scaled = d_normed * gain
    d_norm = factor * scaled - values * (factor * factor * factor) * jnp.mean(
        values * scaled, axis=1, keepdims=True
    )
    d_values = d_out + d_norm
    d_mid[...] = d_values
    d_low[...] = d_values.astype(bf16)
    terms = (d_normed * values * factor).astype(bf16)
    small[...] = (
        dot_tn(low, d_logits) + dot_tn(terms, (lane == 65).astype(bf16))
    ).astype(bf16)


def latent_back_kernel(
    place, t0, t1, t2, t3, compressed, gains, cosine, sine, d_comp, small
):
    row = pl.multiple_of(place[3] * 32, 32)
    terms = t0[...].astype(f32)
    for part in (t1, t2, t3):
        terms = terms + part[...].astype(f32)
    main = compressed[pl.ds(row, 32), :][:, :RANK]
    factor = lax.rsqrt(jnp.mean(main * main, axis=1, keepdims=True) + epsilon)
    grad_main = terms[:, :RANK]
    scaled = grad_main * gains[2:3, :RANK]
    d_main = factor * scaled - main * (factor * factor * factor) * jnp.mean(
        main * scaled, axis=1, keepdims=True
    )
    first, second = terms[:, RANK : RANK + 32], terms[:, RANK + 32 : RANK + 64]
    cos, sin = cosine[pl.ds(row, 32), :][:, :32], sine[pl.ds(row, 32), :][:, :32]
    rot = jnp.concatenate([first * cos + second * sin, second * cos - first * sin], axis=1)
    d_comp[:, :RANK] = d_main.astype(bf16)
    d_comp[:, RANK:] = jnp.concatenate([rot, jnp.zeros((32, 64), f32)], axis=1).astype(bf16)
    latent_terms = grad_main * main * factor
    gap = jnp.zeros((32, 48), f32)
    latent_terms = jnp.concatenate(
        [p for i in range(32) for p in (latent_terms[:, 16 * i : 16 * i + 16], gap)], axis=1
    )
    lane = lax.broadcasted_iota(jnp.int32, (32, 128), 1)
    small[...] = dot_tn(latent_terms.astype(bf16), (lane == 74).astype(bf16)).astype(bf16)


def token_back_kernel(place, d_comp, q0, q1, q2, q3, tok, gains, weight, d_mid, grad, small):
    row = pl.multiple_of(place[3] * 32, 32)
    d_normed = dot_nt(d_comp[...], weight[:, :640])
    for part in (q0, q1, q2, q3):
        d_normed = d_normed + part[...].astype(f32)
    values = tok[pl.ds(row, 32), :].astype(f32)
    factor = lax.rsqrt(jnp.mean(values * values, axis=1, keepdims=True) + epsilon)
    scaled = d_normed * gains[0:1, :]
    d_norm = factor * scaled - values * (factor * factor * factor) * jnp.mean(
        values * scaled, axis=1, keepdims=True
    )
    grad[...] = (d_mid[...] + d_norm).astype(bf16)
    lane = lax.broadcasted_iota(jnp.int32, (32, 128), 1)
    small[...] = dot_tn(
        (d_normed * values * factor).astype(bf16), (lane == 64).astype(bf16)
    ).astype(bf16)


def compress_grad_kernel(place, c0, c1, c2, c3, normed, s0, s1, s2, mine, other, d_all):
    for s, part in enumerate((c0, c1, c2, c3)):
        row = pl.multiple_of(lax.rem(place[3] - s + 4, 4) * 32, 32)
        d_all[pl.ds(row, 32), :] = part[...]
    column = pl.multiple_of(place[3] * 128, 128)
    own = d_all[:, pl.ds(column, 128)]
    rot = d_all[:, RANK:]
    main = dot_tn(normed[...], own).astype(bf16)
    rest = dot_tn(normed[...], rot)
    for part in (s0, s1, s2):
        rest = rest + part[...].astype(f32)
    rest = rest.astype(bf16)
    is_first = place[2] == 0
    for b in range(16):
        for columns, value in ((slice(0, 128), main), (slice(128, 256), rest)):
            low, high = value[b * 128 : b * 128 + 64], value[b * 128 + 64 : b * 128 + 128]
            mine[b * 64 : b * 64 + 64, columns] = jnp.where(is_first, low, high)
            other[b * 64 : b * 64 + 64, columns] = jnp.where(is_first, high, low)


def attend_back_kernel(
    place, d0, d1, d2, d3, weight, q, kv, prob, l0, l1, l2, l3, cosine, sine,
    d_q, d_rot, d_exp, d_branch, k0, k1, k2, k3, r0, r1, r2, r3, key_rot, rot_sum, total,
):
    for s, part in enumerate((d0, d1, d2, d3)):
        row = pl.multiple_of(lax.rem(place[3] - s + 4, 4) * 32, 32)
        d_branch[pl.ds(row, 32), :] = part[...]
    for s, part in enumerate((l0, l1, l2, l3)):
        key_rot[s * 512 : s * 512 + 512, :] = part[:, RANK:]
    d_att = dot_nn(d_branch[...], weight[:, 768:1280]).astype(bf16)
    rots = []
    for h in range(4):
        at = h * 256
        d_att_h = d_att[:, h * 128 : h * 128 + 128]
        low = prob[h]
        prob_h = low.astype(f32)
        d_prob = dot_nt(d_att_h, kv[:, at + 128 : at + 256])
        row_sum = jnp.sum(prob_h * d_prob, axis=1, keepdims=True)
        d_score = (prob_h * (d_prob - row_sum)).astype(bf16)
        key = jnp.concatenate([kv[:, at : at + 128], key_rot[...]], axis=1)
        d_query = dot_nn(d_score, key) * SCALE
        d_q[:, h * 128 : h * 128 + 128] = d_query[:, :128].astype(bf16)
        rots.append(d_query[:, 128:192])
        d_key = dot_tn(d_score, q[:, at : at + 256]) * SCALE
        d_exp[:, at : at + 128] = d_key[:, :128].astype(bf16)
        d_exp[:, at + 128 : at + 256] = dot_tn(low, d_att_h).astype(bf16)
        if h == 0:
            rot_sum[...] = d_key[:, 128:]
        else:
            rot_sum[...] += d_key[:, 128:]
    expand = expansion(weight)
    for s, out in enumerate((k0, k1, k2, k3)):
        rows = slice(s * 512, s * 512 + 512)
        out[:, :RANK] = dot_nt(d_exp[rows, :], expand).astype(bf16)
        out[:, RANK:] = rot_sum[rows, :].astype(bf16)
    rot = jnp.concatenate(rots, axis=1)
    rot = (rot * cosine[...] + turned(rot) * sine[...]).astype(bf16)
    d_rot[...] = rot
    total[...] = (dot_nt(d_q[...], weight[:, :512]) + dot_nt(rot, weight[:, 512:768])).astype(bf16)
    for s, out in enumerate((r0, r1, r2, r3)):
        row = pl.multiple_of(lax.rem(place[3] + s, 4) * 32, 32)
        out[...] = total[pl.ds(row, 32), :]


def attend_back(place, parts, q, kv, prob, latents, attn_all, cosine, sine, after):
    return run(
        attend_back_kernel,
        place,
        [*parts, attn_all, q, kv, prob, *latents, cosine, sine],
        [like(128, 512), like(128, 256), like(2048, 1024), like(128, 2048)]
        + [like(512, 640)] * 4
        + [like(32, 2048)] * 4,
        after=after,
        scratch=[
            pltpu.VMEM((2048, 128), bf16),
            pltpu.VMEM((2048, 128), f32),
            pltpu.VMEM((128, 2048), bf16),
        ],
        flops=8 * 10**9,
    )


PARTS = 1


def expert_kernel(place, far, spread, weight, d_far, d_hidden, hidden, out):
    expert = 2 * place[1] + place[2]
    for part in range(PARTS):
        at = slice(part * 512 // PARTS, (part + 1) * 512 // PARTS)
        raw = dot_nn(far[at, :], weight[:, :896])
        d_weighted = dot_nn(spread[at, :2048], weight[:, 896:])
        rows = raw.shape[0]
        logits = raw[:, 880:888]
        power = jnp.exp(logits - jnp.max(logits, axis=1, keepdims=True))
        router = power / jnp.sum(power, axis=1, keepdims=True)
        is_mine = lax.broadcasted_iota(jnp.int32, (rows, 8), 1) == expert
        chosen = spread[at, 2048:2176][:, 66:74].astype(f32)
        gate = jnp.sum(jnp.where(is_mine, router * chosen, 0.0), axis=1, keepdims=True)
        routed = lax.broadcasted_iota(jnp.int32, (rows, 440), 1) < 352
        gate = jnp.where(routed, gate, 1.0)
        low, upper = raw[:, :440], raw[:, 440:880]
        sigma = 1.0 / (1.0 + jnp.exp(-low))
        silu = low * sigma
        slope = sigma + silu * (1.0 - sigma)
        act = silu * upper
        weighted = (gate * act).astype(bf16)
        d_gate = jnp.sum(jnp.where(routed, d_weighted * act, 0.0), axis=1, keepdims=True)
        d_act = d_weighted * gate
        d_up = jnp.concatenate(
            [d_act * upper * slope, d_act * silu, jnp.zeros((rows, 16), f32)], axis=1
        ).astype(bf16)
        d_hidden[at, :] = d_up
        hidden[at, :] = jnp.concatenate([weighted, jnp.zeros((rows, 72), bf16)], axis=1)
        d_far[at, :2048] = dot_nt(d_up, weight[:, :896]).astype(bf16)
        lane = lax.broadcasted_iota(jnp.int32, (rows, 128), 1)
        d_far[at, 2048:] = jnp.where(lane == expert + 66, d_gate, 0.0).astype(bf16)
        out[at, :] = dot_nt(weighted, weight[:, 896:]).astype(bf16)


def expert(place, far, spread, weight):
    return run(
        expert_kernel,
        place,
        [far, spread, weight],
        [like(512, 2176), like(512, 896), like(512, 512), like(512, 2048)],
        flops=6 * 10**9,
    )


def expert_grad_kernel(x0, x1, y0, y1, d0, d1, h0, h1, out):
    out[:, :896] = (dot_tn(x0[...], d0[...]) + dot_tn(x1[...], d1[...])).astype(bf16)
    down = dot_tn(y0[...], h0[...]) + dot_tn(y1[...], h1[...])
    out[:, 896:] = down[:, :440].astype(bf16)


def expert_grad(fars, spreads, d_hiddens, hiddens, after):
    columns = pl.BlockSpec((512, 512), lambda i: (0, i))
    return pl.pallas_call(
        without(expert_grad_kernel, len(after), 8),
        grid=(4,),
        in_specs=[columns] * 4
        + [whole(512, 896)] * 2
        + [whole(512, 512)] * 2
        + [corner(v) for v in after],
        out_specs=pl.BlockSpec((512, 1336), lambda i: (i, 0)),
        out_shape=like(2048, 1336),
        compiler_params=pltpu.CompilerParams(vmem_limit_bytes=40 * MIB),
        cost_estimate=pl.CostEstimate(
            flops=6 * 10**9, bytes_accessed=18 * 10**6, transcendentals=0
        ),
        name="expert_grad",
    )(*fars, *spreads, *d_hiddens, *hiddens, *after)


def attn_grad_kernel(normed, d_q, d_rot, d_branch, attended, l0, l1, l2, l3, d_exp, out):
    g_exp = 0.0
    for s, part in enumerate((l0, l1, l2, l3)):
        g_exp = g_exp + dot_tn(part[:, :RANK], d_exp[s * 512 : s * 512 + 512, :])
    g_exp = g_exp.astype(bf16)
    out[:, :512] = dot_tn(normed[...], d_q[...]).astype(bf16)
    out[:, 512:768] = dot_tn(normed[...], d_rot[...]).astype(bf16)
    out[:, 768:1280] = dot_tn(d_branch[...], attended[...]).astype(bf16)
    for d in range(32):
        for h in range(4):
            to = d * 64 + h * 16
            out[to : to + 16, 1280:] = g_exp[d * 16 : d * 16 + 16, h * 256 : h * 256 + 256]


def attn_grad(normed, d_q, d_rot, d_branch, attended, latents, d_exp, after):
    return run(
        attn_grad_kernel,
        None,
        [normed, d_q, d_rot, d_branch, attended, *latents, d_exp],
        [like(2048, 1536)],
        after=after,
        size=56,
        flops=4 * 10**9,
    )[0]


def pack_expert_kernel(
    place, expert_in, expert_out, shared_in, shared_out, router, mine, send
):
    is_first = place[2] == 0
    gap = jnp.zeros((64, 8), f32)
    for z in range(4):
        both = []
        for core in range(2):
            expert = 2 * z + core
            cut = slice(88 * expert, 88 * expert + 88)
            parts = [
                expert_in[:, expert, 0, :],
                shared_in[:, 0, cut],
                expert_in[:, expert, 1, :],
                shared_in[:, 1, cut],
                router[...],
                gap,
                expert_out[:, expert, :],
                shared_out[:, cut],
            ]
            both.append(jnp.concatenate([part.astype(f32) for part in parts], axis=1))
        mine[z] = jnp.where(is_first, both[0], both[1]).astype(bf16)
        send[z] = jnp.where(is_first, both[1], both[0]).astype(bf16)


def pair_kernel(place, mine, other, p0, p1, p2, p3):
    is_first = place[2] == 0
    for s, out in enumerate((p0, p1, p2, p3)):
        to = lax.rem(place[1] + s, 4)
        a, b = mine[to], other[to]
        out[:64, :] = jnp.where(is_first, a, b)
        out[64:, :] = jnp.where(is_first, b, a)


def turn_kernel(place, mine, other, natural, out):
    is_first = place[2] == 0
    natural[:64, :] = jnp.where(is_first, mine[...], other[...])
    natural[64:, :] = jnp.where(is_first, other[...], mine[...])
    for s in range(4):
        row = pl.multiple_of(lax.rem(place[3] - s + 4, 4) * 32, 32)
        out[s * 32 : s * 32 + 32, :] = natural[pl.ds(row, 32), :]


def stack_kernel(p0, p1, p2, p3, out):
    rows = p0.shape[0]
    for s, part in enumerate((p0, p1, p2, p3)):
        out[s * rows : s * rows + rows, :] = part[...]


def add_split_kernel(mine, other, *outs):
    rows = outs[0].shape[0]
    for s, out in enumerate(outs):
        at = slice(s * rows, s * rows + rows)
        out[...] = (mine[at, :].astype(f32) + other[at, :].astype(f32)).astype(bf16)


def sum_split_kernel(v0, v1, v2, v3, *outs):
    rows = outs[0].shape[0]
    for s, out in enumerate(outs):
        at = slice(s * rows, s * rows + rows)
        total = v0[at, :].astype(f32)
        for part in (v1, v2, v3):
            total = total + part[at, :].astype(f32)
        out[...] = total.astype(bf16)


def row_sum_kernel(place, v0, v1, v2, v3, *outs):
    for s, out in enumerate(outs):
        rows = pl.ds(pl.multiple_of(lax.rem(place[3] + s, 4) * 32, 32), 32)
        total = v0[rows, :].astype(f32)
        for part in (v1, v2, v3):
            total = total + part[rows, :].astype(f32)
        out[...] = total.astype(bf16)


def out_rows_kernel(v0, v1, v2, v3, middle, out):
    total = v0[...].astype(f32)
    for part in (v1, v2, v3):
        total = total + part[...].astype(f32)
    out[...] = (middle[...] + total).astype(bf16)


def cut_kernel(place, value, p0, p1, p2, p3):
    for s, out in enumerate((p0, p1, p2, p3)):
        rows = pl.ds(pl.multiple_of(lax.rem(place[1] + s, 4) * 128, 128), 128)
        out[...] = value[rows, :]


def join_kernel(place, p0, p1, p2, p3, out):
    for s, part in enumerate((p0, p1, p2, p3)):
        rows = pl.ds(pl.multiple_of(lax.rem(place[1] - s + 4, 4) * 128, 128), 128)
        out[rows, :] = part[...]


def pack_attn_kernel(query, output, expand, out):
    value = query[...]
    out[:, :512] = jnp.concatenate([value[:, 192 * h : 192 * h + 128] for h in range(4)], axis=1)
    out[:, 512:768] = jnp.concatenate(
        [value[:, 192 * h + 128 : 192 * h + 192] for h in range(4)], axis=1
    )
    out[:, 768:1280] = output[...]
    for h in range(4):
        out[h * 16 : h * 16 + 16, 1280:] = expand[:, h * 256 : h * 256 + 256]


def by_core_kernel(place, p0, p1, p2, p3, mine, other):
    is_first = place[2] == 0
    for s, part in enumerate((p0, p1, p2, p3)):
        at = lax.rem(place[1] - s + 4, 4)
        low, high = part[:64, :], part[64:, :]
        mine[at] = jnp.where(is_first, low, high)
        other[at] = jnp.where(is_first, high, low)


def unpack_kernel(place, mine, other, expert_in, expert_out, shared_in, shared_out):
    is_first = place[2] == 0
    ins, outs, downs = [], [], []
    for x in range(4):
        for core in range(2):
            a, b = (mine[x], other[x]) if core == 0 else (other[x], mine[x])
            value = jnp.where(is_first, a, b).astype(f32)
            expert = 2 * x + core
            expert_in[:, expert, 0, :] = value[:, :352]
            expert_in[:, expert, 1, :] = value[:, 440:792]
            expert_out[:, expert, :] = value[:, 896:1248]
            ins.append(value[:, 352:440])
            outs.append(value[:, 792:880])
            downs.append(value[:, 1248:])
    shared_in[:, 0, :] = jnp.concatenate(ins, axis=1)
    shared_in[:, 1, :] = jnp.concatenate(outs, axis=1)
    shared_out[...] = jnp.concatenate(downs, axis=1)


def finish_kernel(total, query, output, expand):
    value = total[...].astype(f32)
    query[...] = jnp.concatenate(
        [
            p
            for h in range(4)
            for p in (
                value[:, h * 128 : h * 128 + 128],
                value[:, 512 + h * 64 : 576 + h * 64],
            )
        ],
        axis=1,
    )
    output[...] = value[:, 768:1280]
    for h in range(4):
        expand[:, h * 256 : h * 256 + 256] = value[h * 16 : h * 16 + 16, 1280:]


def on_device(
    tokens,
    segment,
    routes,
    cotangent,
    gain_attn,
    w_query,
    w_compress,
    gain_latent,
    w_expand,
    w_output,
    gain_ffn,
    w_router,
    w_expert_in,
    w_expert_out,
    w_shared_in,
    w_shared_out,
):
    xi, zi, ci, yi = (lax.axis_index(a) for a in ("x", "z", "c", "y"))
    place = jnp.stack([xi, zi, ci, yi]).astype(jnp.int32)
    is_first = ci == 0
    heads = 4
    dim = 2048

    def leave(value):
        halves = value.reshape((2, 64) + value.shape[1:])
        mine, other = pick(halves, ci, 0), shift(pick(halves, 1 - ci, 0), "c", 1)
        return jnp.stack([jnp.where(is_first, mine, other), jnp.where(is_first, other, mine)])

    small = jnp.concatenate(
        [
            w_compress,
            gain_attn[:, None],
            gain_ffn[:, None],
            w_router,
            jnp.pad(gain_latent, (0, 48))[:, None],
            jnp.zeros((64, 53), bf16),
        ],
        axis=1,
    )
    small_z_parts = gather_near(small, "z")
    (small_z,) = run(stack_kernel, None, small_z_parts, [like(256, 640)])
    small_x = gather_near(small_z, "x")
    (small_mine,) = run(stack_kernel, None, small_x, [like(1024, 640)])
    small_other = shift(small_mine, "c", 1)

    mine_w, send_w = run(
        pack_expert_kernel,
        place,
        [w_expert_in, w_expert_out, w_shared_in, w_shared_out, w_router],
        [like(4, 64, 1336)] * 2,
        after=small_z_parts[1:],
    )
    other_w = shift(send_w, "c", 1)

    tok_mine, tok_send, spread_mine, spread_send = run(
        enter_kernel,
        place,
        [tokens, cotangent, routes],
        [like(64, 2048), like(64, 2048), like(64, 2176), like(64, 2176)],
    )
    tok_other = shift(tok_send, "c", 1)
    spread_other = shift(spread_send, "c", 1)

    position = (xi * 4 + zi) * 128 + jnp.arange(128, dtype=jnp.int32)
    segment_row = pick(segment, ci, 0)
    blocks = jnp.stack(
        [lax.rem(xi - sx + 4, 4) * 4 + lax.rem(zi - sz + 4, 4) for sx in range(4) for sz in range(4)]
    )
    segment_near = segment_row.reshape(16, 128)[blocks].reshape(2048)
    key_place = (blocks[:, None] * 128 + jnp.arange(128, dtype=jnp.int32)[None, :]).reshape(2048)
    where_k = jnp.stack([key_place, segment_near])
    where_q = jnp.stack(
        [position, lax.dynamic_slice_in_dim(segment_row, (xi * 4 + zi) * 128, 128)], axis=1
    )
    lane = jnp.arange(256)[None, :]
    freq = jnp.exp((lane % 32).astype(f32) * (-jnp.log(10000.0) / 32))
    angle = position.astype(f32)[:, None] * freq
    cosine = jnp.cos(angle)
    sine = jnp.where(lane % 64 < 32, 1.0, -1.0) * jnp.sin(angle)

    pair_w = run(pair_kernel, place, [mine_w, other_w], [like(128, 1336)] * 4)
    pair_w = [pair_w[0]] + [shift(pair_w[s], "z", s) for s in range(1, 4)]
    (attn_w,) = run(
        pack_attn_kernel,
        None,
        [w_query, w_output, w_expand],
        [like(64, 1536)],
        after=small_x[1:] + pair_w[1:],
    )
    (expert_w,) = run(join_kernel, place, pair_w, [like(512, 1336)], after=[attn_w])
    attn_all = lax.all_gather(attn_w, ("x", "z", "c"), axis=0, tiled=True)
    ffn_all = lax.all_gather(expert_w, "x", axis=0, tiled=True)

    normed, packed, compressed, weight, gains, tok = run(
        front_kernel,
        place,
        [tok_mine, tok_other, small_mine, small_other, cosine, sine],
        [
            like(128, 2048),
            like(128, 640),
            like(128, 576, dtype=f32),
            like(2048, 640),
            like(8, 2048, dtype=f32),
            like(128, 2048),
        ],
    )
    (latent_near,) = run(stack_kernel, None, gather_near(packed, "z"), [like(512, 640)])
    latents = gather_near(latent_near, "x")
    spread_here, spread = run(
        turn_kernel,
        place,
        [spread_mine, spread_other],
        [like(128, 2176)] * 2,
        after=latents[1:2],
    )
    spread = gather_near(spread, "z")
    prob, kv, attended, query, *branch = attend(
        place, normed, latents, attn_all, cosine, sine, where_q, where_k
    )
    branch = [branch[0]] + [shift(branch[s], "y", s) for s in range(1, 4)]
    (spread,) = run(stack_kernel, None, spread, [like(512, 2176)], after=[attended])
    spread_other = shift(spread, "c", 1)
    middle, far = run(
        middle_kernel,
        place,
        [*branch, tok, gains],
        [like(32, 2048, dtype=f32), like(32, 2048)],
        after=[spread],
    )

    (far,) = run(stack_kernel, None, gather_near(far, "y"), [like(128, 2048)])
    (far,) = run(stack_kernel, None, gather_near(far, "z"), [like(512, 2048)])
    far_other = shift(far, "c", 1)
    d_far2, d_hidden2, hidden2, out_far2 = expert(place, far_other, spread_other, ffn_all)
    d_far, d_hidden, hidden, out_far = expert(place, far, spread, ffn_all)
    d_far = run(
        add_split_kernel, None, [d_far, shift(d_far2, "c", 1)], [like(128, 2176)] * 4
    )
    d_far = [d_far[0]] + [shift(d_far[s], "z", -s) for s in range(1, 4)]
    d_far = run(sum_split_kernel, None, d_far, [like(32, 2176)] * 4)
    grad_ffn = expert_grad(
        (far, far_other), (spread, spread_other), (d_hidden, d_hidden2), (hidden, hidden2), d_far[:1]
    )
    grad_ffn = lax.psum_scatter(grad_ffn, "x", scatter_dimension=0, tiled=True)
    d_far = [d_far[0]] + [shift(d_far[s], "y", -s) for s in range(1, 4)]
    d_mid, d_low, small_a = run(
        middle_back_kernel,
        place,
        [*d_far, spread_here, middle, gains, weight],
        [like(32, 2048, dtype=f32), like(32, 2048), like(2048, 128)],
    )
    out_far = run(
        add_split_kernel,
        None,
        [out_far, shift(out_far2, "c", 1)],
        [like(128, 2048)] * 4,
        after=d_far[:1],
    )
    out_far = [out_far[0]] + [shift(out_far[s], "z", -s) for s in range(1, 4)]
    d_low = gather_near(d_low, "y")

    d_q, d_rot, d_expanded, d_branch, *rest = attend_back(
        place, d_low, query, kv, prob, latents, attn_all, cosine, sine, out_far[1:]
    )
    terms = [rest[0]] + [shift(rest[s], "x", -s) for s in range(1, 4)]
    d_queries = [rest[4]] + [shift(rest[4 + s], "y", s) for s in range(1, 4)]
    grad_ffn = run(cut_kernel, place, [grad_ffn], [like(128, 1336)] * 4)
    grad_ffn = [grad_ffn[0]] + [shift(grad_ffn[s], "z", s) for s in range(1, 4)]
    terms = run(
        sum_split_kernel, None, terms, [like(128, 640)] * 4, after=grad_ffn[1:]
    )
    out_far = run(sum_split_kernel, None, out_far, [like(32, 2048)] * 4, after=terms[:1])
    out_far = [out_far[0]] + [shift(out_far[s], "y", -s) for s in range(1, 4)]
    mine_g, other_g = run(by_core_kernel, place, grad_ffn, [like(4, 64, 1336)] * 2)
    terms = [terms[0]] + [shift(terms[s], "z", -s) for s in range(1, 4)]
    terms = run(
        row_sum_kernel, place, terms, [like(32, 640)] * 4, after=out_far[1:] + [mine_g]
    )
    terms = [terms[0]] + [shift(terms[s], "y", s) for s in range(1, 4)]
    (mixed,) = run(out_rows_kernel, None, [*out_far, middle], [like(32, 2048)], after=terms[:1])
    mixed = gather_near(mixed, "y")

    d_comp, small_b = run(
        latent_back_kernel,
        place,
        [*terms, compressed, gains, cosine, sine],
        [like(32, 640), like(2048, 128)],
    )
    g_expert_in, g_expert_out, g_shared_in, g_shared_out = run(
        unpack_kernel,
        place,
        [mine_g, shift(other_g, "c", 1)],
        [
            like(64, 8, 2, 352, dtype=f32),
            like(64, 8, 352, dtype=f32),
            like(64, 2, 704, dtype=f32),
            like(64, 704, dtype=f32),
        ],
        after=mixed[1:],
    )
    grad_rows, small_c = run(
        token_back_kernel,
        place,
        [d_comp, *d_queries, tok, gains, weight, d_mid],
        [like(32, 2048), like(2048, 128)],
    )
    grad_rows = leave(place_at(gather_near(grad_rows, "y"), "y").reshape(128, dim))
    mixed = leave(place_at(mixed, "y").reshape(128, dim))

    def fsdp_sum(mine, other, cuts):
        value = (mine.astype(f32) + shift(other, "c", 1).astype(f32)).astype(bf16)
        value = value.reshape(4, 4, 64, -1)
        done = []
        for start, stop, first, second in cuts:
            part = sum_at(value[..., start:stop], first, 0 if first == "x" else 1).astype(bf16)
            done.append(sum_at(part, second, 0))
        return done

    g_attn = attn_grad(normed, d_q, d_rot, d_branch, attended, latents, d_expanded, [])
    g_attn = lax.psum_scatter(g_attn, ("x", "z", "c"), scatter_dimension=0, tiled=True)
    g_mine, g_other = run(
        compress_grad_kernel,
        place,
        [*gather_near(d_comp, "y"), normed, small_a, small_b, small_c],
        [like(1024, 256)] * 2,
        scratch=[pltpu.VMEM((128, 640), bf16)],
    )
    (g_small,) = fsdp_sum(g_mine, g_other, ((0, 256, "x", "z"),))
    g_small = g_small.astype(bf16)
    g_parts = gather_near(g_small, "y")
    g_query, g_output, g_expand = run(
        finish_kernel,
        None,
        [g_attn],
        [like(64, 768, dtype=f32), like(64, 512, dtype=f32), like(16, 1024, dtype=f32)],
        after=g_parts[1:] + [g_shared_out],
    )
    g_small = place_at(g_parts, "y")
    g_small = g_small.astype(f32)
    g_compress = jnp.concatenate(
        [g_small[i, :, :128] for i in range(4)] + [g_small[0, :, 128:192]], axis=1
    )
    g_small = jnp.sum(g_small[:, :, 192:], axis=0)

    return (
        mixed,
        grad_rows,
        g_small[:, 0],
        g_query,
        g_compress,
        g_small[:16, 10],
        g_expand,
        g_output,
        g_small[:, 1],
        g_small[:, 2:10],
        g_expert_in,
        g_expert_out,
        g_shared_in,
        g_shared_out,
    )


def solution(mesh):
    fine = Mesh(mesh.devices.reshape(4, 4, 2, 4), ("x", "z", "c", "y"))
    rows = ("x", "z", "c")
    return jax.shard_map(
        on_device,
        mesh=fine,
        in_specs=(
            P(None, rows, None),
            P(),
            P(None, rows, None),
            P(None, rows, None),
            P(rows),
            P(rows, "y"),
            P(rows, None),
            P(rows),
            P(rows, "y"),
            P(rows, "y"),
            P(rows),
            P(rows, None),
            P(rows, None, None, "y"),
            P(rows, None, "y"),
            P(rows, None, "y"),
            P(rows, "y"),
        ),
        out_specs=(
            P(None, rows, None),
            P(None, rows, None),
            P(rows),
            P(rows, "y"),
            P(rows, None),
            P(rows),
            P(rows, "y"),
            P(rows, "y"),
            P(rows),
            P(rows, None),
            P(rows, None, None, "y"),
            P(rows, None, "y"),
            P(rows, None, "y"),
            P(rows, "y"),
        ),
        check_vma=False,
    )
```
